128 devices in a mesh: chan: 16 (over y, z_hi, core), seq: 8 (over z_lo, x).
Axes of the slice: x: 4, y: 4, z: 4 (z_hi: 2, z_lo: 2; z = z_hi * 2 + z_lo), core: 2. Of those that a mesh axis runs over, the one named last changes fastest.
Arguments:
- queries: bfloat16 [4096, 8192], P('seq', 'chan'), may hold values from -6 to 6
- key_proj: bfloat16 [4096, 8192], P('seq', 'chan'), may hold values from -6 to 6
- value_proj: bfloat16 [4096, 8192], P('seq', 'chan'), may hold values from -6 to 6
- skip_gain: float32 [8192], P('chan'), may hold values from 0.5 to 1.5
- residue: float32 [16, 8192], P(None, 'chan'), may hold values from -1.5 to 1.5
- log_decay: float32 [16, 8192], P(None, 'chan')
- out_weight: bfloat16 [8192, 8192], P('chan'), may hold values from -0.0625 to 0.0625
- cotangent: bfloat16 [4096, 8192], P(('seq', 'chan')), may hold values from -6 to 6
Outputs:
- mixed: bfloat16 [4096, 8192], P(('seq', 'chan'))
- grad_query: bfloat16 [4096, 8192], P('seq', 'chan')
- grad_key: bfloat16 [4096, 8192], P('seq', 'chan')
- grad_value: bfloat16 [4096, 8192], P('seq', 'chan')
- grad_weight: bfloat16 [8192, 8192], P('chan', 'seq')
- grad_residue: float32 [16, 8192], P(None, 'chan')
- grad_decay: float32 [16, 8192], P(None, 'chan')
- grad_skip: float32 [8192], P('chan')
The draws below stay inside these ranges and needn't reach their ends.
All inputs are finite; a program needn't handle non-finite values.
Results may differ from the reference program's by a relative error of at most 0.019.
Values may be sent and summed in bfloat16 or wider, within the bound.
No kernel may reach another device: no remote copies, remote signals or barrier semaphores. Data moves between devices by JAX's collectives and lax.ppermute only.
A program may use at most 256 MiB of HBM per device.

```python
import math
import jax
import jax.numpy as jnp
from jax import lax

D = 8192
M = 16
TOKENS = 4096
N_CHAN = 16


def draw_log_decay(key, part):
    key = jax.random.fold_in(key, 11)
    lowest = math.log(1.0 / TOKENS)
    return jax.random.uniform(key, (M, D), jnp.float32, minval=lowest, maxval=math.log(1.0 / 24.0))


def level_of(key, shape, pieces, least, largest):
    def one(dim, blocks):
        draws = jax.random.uniform(jax.random.fold_in(jax.random.fold_in(key, 6), dim), (blocks,), jnp.float32, least / len(pieces), largest / len(pieces))
        return jnp.repeat(jnp.exp(draws), shape[dim] // blocks).reshape((-1,) + (1,) * (len(shape) - dim - 1))

    gain = one(*pieces[0])
    for cut in pieces[1:]:
        gain = gain * one(*cut)
    return gain


def normal_values(stream_key, shape, deviation, reach, shards=(), held_as=jnp.bfloat16):
    result = jax.random.normal(stream_key, shape, jnp.float32) * deviation
    if len(shards) > 0:
        result = level_of(stream_key, shape, shards, -0.22, 0.18) * result
    return jnp.clip(result, min=-reach, max=reach).astype(held_as)


def setup_inputs(seed: int = 0) -> dict:
    arg_keys = jax.random.split(jax.random.key(seed), 9)
    return {
        "queries": normal_values(arg_keys[0], (TOKENS, D), 1.0, 6.0, ((0, 8), (1, 16))),
        "key_proj": normal_values(arg_keys[1], (TOKENS, D), 1.0, 6.0, ((0, 8), (1, 16))),
        "value_proj": normal_values(arg_keys[2], (TOKENS, D), 1.0, 6.0, ((0, 8), (1, 16))),
        "skip_gain": jnp.clip(1.0 + 0.1 * jax.random.normal(arg_keys[3], (D,), jnp.float32), 0.5, 1.5),
        "residue": normal_values(arg_keys[4], (M, D), M ** -0.5, 1.5, ((1, 16),), jnp.float32),
        "log_decay": draw_log_decay(jax.random.fold_in(arg_keys[8], 71), 0),
        "out_weight": normal_values(arg_keys[6], (D, D), D ** -0.5, 0.0625, ((0, 16),)),
        "cotangent": normal_values(arg_keys[7], (TOKENS, D), 1.0, 6.0, ((0, 128),)),
    }


def reference(queries, key_proj, value_proj, skip_gain, residue, log_decay, out_weight, cotangent):
    decay_rate = jnp.exp(log_decay)
    decays = jnp.exp(-decay_rate)
    norm_gain = jnp.sqrt(2.0 * decay_rate)
    mode_gain = residue * norm_gain
    query_f = queries.astype(jnp.float32)
    key_f = key_proj.astype(jnp.float32)
    value_f = value_proj.astype(jnp.float32)
    driving = key_f * value_f
    grad_gated = jnp.dot(cotangent, out_weight.T, preferred_element_type=jnp.float32)
    gate_back = grad_gated * query_f

    def forward_step(carried, inputs):
        current, lagged, acc_pair, acc_lag = carried
        drive_row, back_row = inputs
        lagged = decays * (lagged + current)
        current = decays * current + drive_row[None, :]
        acc_pair = acc_pair + back_row[None, :] * current
        acc_lag = acc_lag + back_row[None, :] * lagged
        return ((current, lagged, acc_pair, acc_lag), lax.optimization_barrier(jnp.sum(mode_gain * current, axis=0)))
    zero_state = jnp.zeros((M, D), jnp.float32)
    (final_state, final_lag, pair_sum, lag_sum), convolved = lax.scan(forward_step, (zero_state, zero_state, zero_state, zero_state), (driving, gate_back))
    pre_gate = convolved + skip_gain[None, :] * driving
    gated = (query_f * pre_gate).astype(jnp.bfloat16)
    groups = gated.reshape(TOKENS, N_CHAN, D // N_CHAN).transpose(1, 0, 2)
    weight_groups = out_weight.reshape(N_CHAN, D // N_CHAN, D)

    def add_group(totals, pair):
        partial_out = jnp.dot(pair[0], pair[1], preferred_element_type=jnp.float32).astype(jnp.bfloat16)
        partial_out = lax.optimization_barrier(partial_out)
        return (totals + partial_out.astype(jnp.float32), None)
    summed, unused = lax.scan(add_group, jnp.zeros((TOKENS, D), jnp.float32), (groups, weight_groups))
    mixed = summed.astype(jnp.bfloat16)
    scale = 1.0 / math.sqrt(TOKENS)
    grad_weight = (jnp.dot(gated.T, cotangent, preferred_element_type=jnp.float32) * scale).astype(jnp.bfloat16)
    grad_query = (grad_gated * pre_gate).astype(jnp.bfloat16)

    def backward_step(current, back_row):
        current = decays * current + back_row[None, :]
        return (current, lax.optimization_barrier(jnp.sum(mode_gain * current, axis=0)))
    last_back, back_conv = lax.scan(backward_step, zero_state, gate_back, reverse=True)
    grad_driving = back_conv + skip_gain[None, :] * gate_back
    grad_key = (grad_driving * value_f).astype(jnp.bfloat16)
    grad_value = (grad_driving * key_f).astype(jnp.bfloat16)
    grad_residue = norm_gain * pair_sum * scale
    grad_decay = mode_gain * (0.5 * pair_sum - decay_rate * lag_sum) * scale
    grad_skip = lax.optimization_barrier(jnp.sum(gate_back * driving, axis=0)) * scale
    return (mixed, grad_query, grad_key, grad_value, grad_weight, grad_residue, grad_decay, grad_skip)
```

```python
import functools
import itertools
import math

import jax
import jax.numpy as jnp
from jax import lax
from jax.experimental import pallas as pl
from jax.experimental.pallas import tpu as pltpu
from jax.sharding import PartitionSpec as P

RING = 4
SUBS = 8
LANES = 128
F32 = jnp.float32
BF16 = jnp.bfloat16


def strided(first, step):
    return pl.ds(first, SUBS, stride=step)


def spread(ref, mode, lanes):
    return jnp.broadcast_to(ref[pl.ds(mode, 1), lanes], (SUBS, LANES))


def tree_sum(parts):
    while len(parts) > 1:
        parts = [a + b for a, b in zip(parts[::2], parts[1::2])] + parts[len(parts) & ~1 :]
    return parts[0]


def lane_tiles(channels):
    return [(tile, pl.ds(tile * LANES, LANES)) for tile in range(channels // LANES)]


def places():
    chan, seq = lax.axis_index("chan"), lax.axis_index("seq")
    return chan // 4, lax.rem(chan // 2, 2), lax.rem(chan, 2), seq // RING, lax.rem(seq, RING)


def hop(value, x=0, y=0, z=0, core=0, pair=0):
    moves = []
    for i, j, k, c in itertools.product(range(RING), range(RING), range(RING), range(2)):
        there = ((i + x) % RING, (j + y) % RING, ((k + z) % RING) ^ pair, c ^ core)
        moves.append(tuple(((b * 2 + d // 2) * 2 + e) * 2 * RING + d % 2 * RING + a for a, b, d, e in ((i, j, k, c), there)))
    return lax.ppermute(value, ("chan", "seq"), moves)


def gather_cotangent(cotangent):
    y, high, core, low, _ = places()
    tokens, width = cotangent.shape
    half = width // 2
    mine = lax.dynamic_slice(cotangent, (0, low * half), (tokens, half))
    theirs = lax.dynamic_slice(cotangent, (0, (1 - low) * half), (tokens, half))
    above, below, across = hop(theirs, z=1), hop(theirs, z=-1), hop(mine, z=2)
    stack = jnp.where(high == 0, jnp.stack([mine, across]), jnp.stack([across, mine]))
    same, differ = jnp.where(low == 1, above, below), jnp.where(low == 1, below, above)
    other = jnp.where(high == 0, jnp.stack([same, differ]), jnp.stack([differ, same]))
    block = jnp.stack([stack, other])

    def put(whole, part, first, row, at_core):
        return lax.dynamic_update_slice(whole, part[:, None, :, None], (first, row, 0, at_core, 0, 0))

    whole = jnp.zeros((2, RING, 2, 2, tokens, half), cotangent.dtype)
    before, after = lax.rem(y + RING - 1, RING), lax.rem(y + 1, RING)
    far = lax.rem(y + 2, RING)
    from_before, from_after = hop(block, y=1), hop(block, y=-1)
    far_own, far_other = hop(from_before[:1], y=1), hop(from_after[1:], y=-1)
    for part, first, row in (
        (block, 0, y), (from_before, 0, before), (from_after, 0, after), (far_own, 0, far), (far_other, 1, far)
    ):
        whole = put(whole, part, first, row, core)
        whole = put(whole, hop(part, core=1), first, row, 1 - core)
    return whole


def add(*parts):
    return functools.reduce(jnp.add, [part.astype(F32) for part in parts])


def ring_sum(blocks, axis):
    half = blocks[2].shape[0] // 2
    first = hop(blocks[2][:half], **{axis: 1})
    second = hop(blocks[2][half:], **{axis: -1})
    up = jnp.concatenate([add(blocks[1][:half], first).astype(BF16), blocks[1][half:]])
    down = jnp.concatenate([blocks[3][:half], add(blocks[3][half:], second).astype(BF16)])
    return add(blocks[0], hop(up, **{axis: 1}), hop(down, **{axis: -1}))


def mix(turned, out_weight):
    half = turned.shape[0] // 2
    sent = hop(jnp.dot(turned[half:], out_weight, preferred_element_type=F32).astype(BF16), core=1)
    kept = add(jnp.dot(turned[:half], out_weight, preferred_element_type=F32), sent).astype(BF16)
    total = ring_sum(kept.reshape(RING, half // RING, -1), "y")
    rest = total.shape[0] // 2
    return add(total[:rest], hop(total[rest:].astype(BF16), z=2)).astype(BF16)


def weigh(gated, cot_rows, scale):
    x = places()[4]
    width = cot_rows.shape[1] // RING
    blocks = [None] * RING
    for r in (2, 1, 3, 0):
        columns = lax.dynamic_slice(cot_rows, (0, lax.rem(x + r, RING) * width), (cot_rows.shape[0], width))
        product = lax.dot_general(gated, columns, (((0,), (0,)), ((), ())), preferred_element_type=F32)
        blocks[r] = (product * scale).astype(BF16)
    return ring_sum(blocks, "x").astype(BF16)


def forward_ends(key_ref, value_ref, log_ref, ends_ref, sub_ref, drive_ref, decay_ref, zero_ref):
    length, channels = key_ref.shape
    modes = log_ref.shape[0]
    span = length // SUBS
    decay_ref[...] = jnp.exp(-jnp.exp(log_ref[...]))
    zero_ref[...] = jnp.zeros_like(zero_ref)
    for tile, lanes in lane_tiles(channels):
        drive_ref[tile] = key_ref[:, lanes].astype(F32) * value_ref[:, lanes].astype(F32)
        decay = [spread(decay_ref, m, lanes) for m in range(modes)]

        def step(i, carry):
            now, lag = carry
            u = drive_ref[tile, strided(i, span)]
            lag = [decay[m] * (lag[m] + now[m]) for m in range(modes)]
            now = [decay[m] * now[m] + u for m in range(modes)]
            return now, lag

        zero = [zero_ref[...]] * modes
        now, lag = lax.fori_loop(0, span, step, (zero, zero), unroll=4)
        for m in range(modes):
            sub_ref[tile, strided(m, modes)] = now[m]
            sub_ref[tile, strided(SUBS * modes + m, modes)] = lag[m]
        power = jnp.exp(-span * jnp.exp(log_ref[:, lanes]))
        state = jnp.zeros_like(power)
        lagged = jnp.zeros_like(power)
        for j in range(SUBS):
            lagged = power * (lagged + span * state) + sub_ref[tile, pl.ds((SUBS + j) * modes, modes)]
            state = power * state + sub_ref[tile, pl.ds(j * modes, modes)]
        ends_ref[pl.ds(0, modes), lanes] = state
        ends_ref[pl.ds(modes, modes), lanes] = lagged


def forward_full(*refs):
    (query_ref, drive_ref, sub_ref, log_ref, residue_ref, skip_ref, *end_refs) = refs[:-6]
    (gated_ref, turned_ref, pre_ref, lead_ref, decay_ref, gain_ref) = refs[-6:]
    length, channels = query_ref.shape
    modes = log_ref.shape[0]
    span = length // SUBS
    rate = jnp.exp(log_ref[...])
    decay_ref[...] = jnp.exp(-rate)
    gain_ref[...] = residue_ref[...] * jnp.sqrt(2.0 * rate)
    for tile, lanes in lane_tiles(channels):
        rate = jnp.exp(log_ref[:, lanes])
        stretch = jnp.exp(-length * rate)
        power = jnp.exp(-span * rate)
        state = jnp.zeros_like(rate)
        lagged = jnp.zeros_like(rate)
        for end in end_refs[::-1]:
            lagged = stretch * (lagged + length * state) + end[pl.ds(modes, modes), lanes]
            state = stretch * state + end[pl.ds(0, modes), lanes]
        for j in range(SUBS):
            now_rows, lag_rows = (pl.ds((j + k) * modes, modes) for k in (0, SUBS))
            lead_ref[tile, now_rows] = state
            lead_ref[tile, lag_rows] = lagged
            lagged = power * (lagged + span * state) + sub_ref[tile, lag_rows]
            state = power * state + sub_ref[tile, now_rows]
        decay = [spread(decay_ref, m, lanes) for m in range(modes)]
        gain = [spread(gain_ref, m, lanes) for m in range(modes)]
        skip = spread(skip_ref, 0, lanes)

        def step(i, now):
            place = strided(i, span)
            u = drive_ref[tile, place]
            now = [decay[m] * now[m] + u for m in range(modes)]
            pre_ref[tile, place] = tree_sum([gain[m] * now[m] for m in range(modes)]) + skip * u
            return now

        first = [lead_ref[tile, strided(m, modes)] for m in range(modes)]
        lax.fori_loop(0, span, step, first, unroll=4)
        gated_ref[:, lanes] = (query_ref[:, lanes].astype(F32) * pre_ref[tile]).astype(BF16)
    part = length // (RING * 4)
    y, high, core, _, _ = places()
    for i in range(RING * 4):
        there = lax.rem(i % 2 + core, 2) * RING + lax.rem(i // 4 + RING - y, RING)
        there = there * 2 + lax.rem(i // 2 % 2 + high, 2)
        turned_ref[pl.ds(pl.multiple_of(there * part, part), part)] = gated_ref[pl.ds(i * part, part)]


def backward_ends(
    grad_ref, query_ref, pre_ref, drive_ref, lead_ref, log_ref,
    grad_query_ref, back_ref, sums_ref, sub_ref, decay_ref, part_ref, zero_ref,
):
    length, channels = query_ref.shape
    modes = log_ref.shape[0]
    span = length // SUBS
    half = modes // 2
    decay_ref[...] = jnp.exp(-jnp.exp(log_ref[...]))
    zero_ref[...] = jnp.zeros_like(zero_ref)
    for tile, lanes in lane_tiles(channels):
        grad = grad_ref[:, lanes].astype(F32)
        grad_query_ref[:, lanes] = (grad * pre_ref[tile]).astype(BF16)
        back_ref[tile] = grad * query_ref[:, lanes].astype(F32)
        decay = [spread(decay_ref, m, lanes) for m in range(modes)]

        def back_step(i, now):
            g = back_ref[tile, strided(span - 1 - i, span)]
            return [decay[m] * now[m] + g for m in range(modes)]

        zero = [zero_ref[...]] * modes
        now = lax.fori_loop(0, span, back_step, zero, unroll=4)
        for m in range(modes):
            sub_ref[tile, strided(m, modes)] = now[m]
        for low in range(0, modes, half):
            group = range(low, low + half)
            decay = [spread(decay_ref, m, lanes) for m in group]

            def pair_step(i, carry):
                state, lag, pair, lag_pair, skip = carry
                place = strided(i, span)
                u = drive_ref[tile, place]
                g = back_ref[tile, place]
                lag = [decay[m] * (lag[m] + state[m]) for m in range(half)]
                state = [decay[m] * state[m] + u for m in range(half)]
                pair = [pair[m] + g * state[m] for m in range(half)]
                lag_pair = [lag_pair[m] + g * lag[m] for m in range(half)]
                return state, lag, pair, lag_pair, skip + g * u

            state = [lead_ref[tile, strided(m, modes)] for m in group]
            lag = [lead_ref[tile, strided(SUBS * modes + m, modes)] for m in group]
            zero = [zero_ref[...]] * half
            state, lag, pair, lag_pair, skip = lax.fori_loop(
                0, span, pair_step, (state, lag, zero, zero, zero[0]), unroll=4
            )
            for m in range(half):
                part_ref[tile, strided(low + m, modes)] = pair[m]
                part_ref[tile, strided(SUBS * modes + low + m, modes)] = lag_pair[m]
        total = jnp.sum(skip, axis=0, keepdims=True)
        sums_ref[pl.ds(3 * modes, SUBS), lanes] = jnp.broadcast_to(total, (SUBS, LANES))
        power = jnp.exp(-span * jnp.exp(log_ref[:, lanes]))
        start = jnp.zeros_like(power)
        pair = jnp.zeros_like(power)
        lag_pair = jnp.zeros_like(power)
        for j in range(SUBS - 1, -1, -1):
            start = power * start + sub_ref[tile, pl.ds(j * modes, modes)]
            pair = pair + part_ref[tile, pl.ds(j * modes, modes)]
            lag_pair = lag_pair + part_ref[tile, pl.ds((SUBS + j) * modes, modes)]
        sums_ref[pl.ds(0, modes), lanes] = start
        sums_ref[pl.ds(modes, modes), lanes] = pair
        sums_ref[pl.ds(2 * modes, modes), lanes] = lag_pair


def backward_full(*refs, blocks, scale):
    (key_ref, value_ref, back_ref, sub_ref, log_ref, residue_ref, skip_ref, *sum_refs) = refs[:-9]
    (grad_key_ref, grad_value_ref, grad_residue_ref, grad_decay_ref, grad_skip_ref) = refs[-9:-4]
    (decay_ref, gain_ref, lead_ref, drive_grad_ref) = refs[-4:]
    length, channels = key_ref.shape
    modes = log_ref.shape[0]
    span = length // SUBS
    mine = lax.axis_index("seq")
    rate = jnp.exp(log_ref[...])
    norm = jnp.sqrt(2.0 * rate)
    gain = residue_ref[...] * norm
    decay_ref[...] = jnp.exp(-rate)
    gain_ref[...] = gain
    pair = tree_sum([ref[pl.ds(modes, modes)] for ref in sum_refs])
    lag_pair = tree_sum([ref[pl.ds(2 * modes, modes)] for ref in sum_refs])
    grad_residue_ref[...] = norm * pair * scale
    grad_decay_ref[...] = gain * (0.5 * pair - rate * lag_pair) * scale
    grad_skip_ref[...] = tree_sum([ref[pl.ds(3 * modes, SUBS)] for ref in sum_refs]) * scale
    for tile, lanes in lane_tiles(channels):
        rate = jnp.exp(log_ref[:, lanes])
        stretch = jnp.exp(-length * rate)
        power = jnp.exp(-span * rate)
        start = jnp.zeros_like(rate)
        for offset in range(blocks - 1, 0, -1):
            after = jnp.where(mine + offset < blocks, sum_refs[offset][pl.ds(0, modes), lanes], 0.0)
            start = stretch * start + after
        for j in range(SUBS - 1, -1, -1):
            lead_ref[tile, pl.ds(j * modes, modes)] = start
            start = power * start + sub_ref[tile, pl.ds(j * modes, modes)]
        decay = [spread(decay_ref, m, lanes) for m in range(modes)]
        gain = [spread(gain_ref, m, lanes) for m in range(modes)]
        skip = spread(skip_ref, 0, lanes)

        def step(i, now):
            place = strided(span - 1 - i, span)
            g = back_ref[tile, place]
            now = [decay[m] * now[m] + g for m in range(modes)]
            drive_grad_ref[tile, place] = tree_sum([gain[m] * now[m] for m in range(modes)]) + skip * g
            return now

        first = [lead_ref[tile, strided(m, modes)] for m in range(modes)]
        lax.fori_loop(0, span, step, first, unroll=4)
        drive_grad = drive_grad_ref[tile]
        grad_key_ref[:, lanes] = (drive_grad * value_ref[:, lanes].astype(F32)).astype(BF16)
        grad_value_ref[:, lanes] = (drive_grad * key_ref[:, lanes].astype(F32)).astype(BF16)


def call(body, args, outs, scratch, flops, name):
    whole = pl.BlockSpec(memory_space=pltpu.VMEM)
    moved = sum(a.size * a.dtype.itemsize for a in (*args, *outs))
    return pl.pallas_call(
        body,
        out_shape=[jax.ShapeDtypeStruct(o.shape, o.dtype) for o in outs],
        in_specs=[whole] * len(args),
        out_specs=[whole] * len(outs),
        scratch_shapes=[pltpu.VMEM(shape, F32) for shape in scratch],
        compiler_params=pltpu.CompilerParams(vmem_limit_bytes=32 * 2**20),
        cost_estimate=pl.CostEstimate(flops=flops, bytes_accessed=moved, transcendentals=0),
        name=name,
    )(*args)


def like(shape, dtype):
    return jax.ShapeDtypeStruct(shape, dtype)


def shifted(value, axis, offset, wrap):
    count = lax.axis_size(axis)
    pairs = [(i, (i + offset) % count) for i in range(count) if wrap or 0 <= i + offset < count]
    return lax.ppermute(value, axis, pairs)


def local(queries, key_proj, value_proj, skip_gain, residue, log_decay, out_weight, cotangent):
    length, channels = queries.shape
    modes = residue.shape[0]
    blocks = lax.axis_size("seq")
    scale = 1.0 / math.sqrt(length * blocks)
    skip_row = skip_gain.reshape(1, channels)
    tiles = channels // LANES
    wide = like((tiles, length, LANES), F32)
    narrow = like((length, channels), BF16)
    table = (modes, channels)
    work = length * channels * modes

    cot_rows = gather_cotangent(cotangent).reshape(2 * length, -1)

    ends, subs, driving = call(
        forward_ends,
        (key_proj, value_proj, log_decay),
        (like((2 * modes, channels), F32), like((tiles, 2 * SUBS * modes, LANES), F32), wide),
        [table, (SUBS, LANES)],
        4 * work,
        "forward_ends",
    )
    earlier = [shifted(ends, "seq", offset, False) for offset in range(1, blocks)]
    gated, turned, pre_gate, lead = call(
        forward_full,
        (queries, driving, subs, log_decay, residue, skip_row, *earlier),
        (narrow, narrow, wide, like((tiles, 2 * SUBS * modes, LANES), F32)),
        [table, table],
        4 * work,
        "forward_full",
    )
    half = out_weight.shape[1] // 2
    low_weight = lax.dynamic_slice(out_weight, (0, places()[3] * half), (channels, half))
    grad_parts = lax.dot_general(
        cot_rows, low_weight, (((1,), (1,)), ((), ())), preferred_element_type=F32
    )
    grad_gated = add(grad_parts[:length], hop(grad_parts[length:].astype(BF16), pair=1))
    grad_weight = weigh(jnp.concatenate([gated, hop(gated, pair=1)]), cot_rows, scale)
    mixed = mix(turned, out_weight)

    grad_query, back, sums, back_subs = call(
        backward_ends,
        (grad_gated, queries, pre_gate, driving, lead, log_decay),
        (narrow, wide, like((3 * modes + SUBS, channels), F32), like((tiles, SUBS * modes, LANES), F32)),
        [table, (tiles, 2 * SUBS * modes, LANES), (SUBS, LANES)],
        10 * work,
        "backward_ends",
    )
    all_sums = [sums] + [shifted(sums, "seq", -offset, True) for offset in range(1, blocks)]
    grad_key, grad_value, grad_residue, grad_decay, grad_skip = call(
        functools.partial(backward_full, blocks=blocks, scale=scale),
        (key_proj, value_proj, back, back_subs, log_decay, residue, skip_row, *all_sums),
        (narrow, narrow, like(table, F32), like(table, F32), like((SUBS, channels), F32)),
        [table, table, (tiles, SUBS * modes, LANES), (tiles, length, LANES)],
        4 * work,
        "backward_full",
    )
    return (
        mixed,
        grad_query,
        grad_key,
        grad_value,
        grad_weight,
        grad_residue,
        grad_decay,
        grad_skip[0],
    )


def solution(mesh):
    in_specs = (
        P("seq", "chan"),
        P("seq", "chan"),
        P("seq", "chan"),
        P("chan"),
        P(None, "chan"),
        P(None, "chan"),
        P("chan", None),
        P(("seq", "chan"), None),
    )
    out_specs = (
        P(("seq", "chan"), None),
        P("seq", "chan"),
        P("seq", "chan"),
        P("seq", "chan"),
        P("chan", "seq"),
        P(None, "chan"),
        P(None, "chan"),
        P("chan"),
    )
    return jax.shard_map(local, mesh=mesh, in_specs=in_specs, out_specs=out_specs, check_vma=False)
```

```python
import functools
import itertools
import math

import jax
import jax.numpy as jnp
from jax import lax
from jax.experimental import pallas as pl
from jax.experimental.pallas import tpu as pltpu
from jax.sharding import PartitionSpec as P

RING = 4
SUBS = 8
LANES = 128
F32 = jnp.float32
BF16 = jnp.bfloat16


def strided(first, step):
    return pl.ds(first, SUBS, stride=step)


def spread(ref, mode, lanes):
    return jnp.broadcast_to(ref[pl.ds(mode, 1), lanes], (SUBS, LANES))


def tree_sum(parts):
    while len(parts) > 1:
        parts = [a + b for a, b in zip(parts[::2], parts[1::2])] + parts[len(parts) & ~1 :]
    return parts[0]


def lane_tiles(channels):
    return [(tile, pl.ds(tile * LANES, LANES)) for tile in range(channels // LANES)]


def places():
    chan, seq = lax.axis_index("chan"), lax.axis_index("seq")
    return chan // 4, lax.rem(chan // 2, 2), lax.rem(chan, 2), seq // RING, lax.rem(seq, RING)


def hop(value, x=0, y=0, z=0, core=0, pair=0):
    moves = []
    for i, j, k, c in itertools.product(range(RING), range(RING), range(RING), range(2)):
        there = ((i + x) % RING, (j + y) % RING, ((k + z) % RING) ^ pair, c ^ core)
        moves.append(tuple(((b * 2 + d // 2) * 2 + e) * 2 * RING + d % 2 * RING + a for a, b, d, e in ((i, j, k, c), there)))
    return lax.ppermute(value, ("chan", "seq"), moves)


def gather_z(cotangent):
    _, high, _, low, _ = places()
    tokens, width = cotangent.shape
    half = width // 2
    mine = lax.dynamic_slice(cotangent, (0, low * half), (tokens, half))
    theirs = lax.dynamic_slice(cotangent, (0, (1 - low) * half), (tokens, half))
    above, below, across = hop(theirs, z=1), hop(theirs, z=-1), hop(mine, z=2)
    stack = jnp.where(high == 0, jnp.stack([mine, across]), jnp.stack([across, mine]))
    same, differ = jnp.where(low == 1, above, below), jnp.where(low == 1, below, above)
    other = jnp.where(high == 0, jnp.stack([same, differ]), jnp.stack([differ, same]))
    return jnp.stack([stack, other])


def gather_y(block, near_blocks, kept):
    y, _, core, _, _ = places()
    _, _, tokens, half = block.shape

    def put(whole, part, first, row, at_core):
        return lax.dynamic_update_slice(whole, part[:, None, :, None], (first, row, 0, at_core, 0, 0))

    whole = jnp.zeros((2, RING, 2, 2, tokens, half), block.dtype)
    before, after = lax.rem(y + RING - 1, RING), lax.rem(y + 1, RING)
    far = lax.rem(y + 2, RING)
    from_before, from_after = near_blocks
    far_own, far_other = hop(from_before[:1], y=1), hop(from_after[1:], y=-1)
    far_own, far_other, kept = together(far_own, far_other, kept)
    for part, first, row in (
        (block, 0, y), (from_before, 0, before), (from_after, 0, after), (far_own, 0, far), (far_other, 1, far)
    ):
        whole = put(whole, part, first, row, core)
        whole = put(whole, hop(part, core=1), first, row, 1 - core)
    return whole, kept


def add(*parts):
    return functools.reduce(jnp.add, [part.astype(F32) for part in parts])


def project_tile(rows_ref, weight_ref, *out_refs):
    product = jnp.dot(rows_ref[...], weight_ref[...], preferred_element_type=F32).astype(BF16)
    first = 0
    for ref in out_refs:
        ref[...] = product[first : first + ref.shape[0]]
        first += ref.shape[0]


def project(turned, out_weight):
    rows, depth = turned.shape
    width = out_weight.shape[1]
    tile = 1024
    sizes = [rows // 8, 3 * rows // 8] * 2
    return pl.pallas_call(
        project_tile,
        grid=(width // tile,),
        out_shape=[jax.ShapeDtypeStruct((size, width), BF16) for size in sizes],
        in_specs=[pl.BlockSpec((rows, depth), lambda i: (0, 0)), pl.BlockSpec((depth, tile), lambda i: (0, i))],
        out_specs=[pl.BlockSpec((size, tile), lambda i: (0, i)) for size in sizes],
        compiler_params=pltpu.CompilerParams(vmem_limit_bytes=32 * 2**20),
        cost_estimate=pl.CostEstimate(
            flops=2 * rows * depth * width, bytes_accessed=2 * width * (rows + depth), transcendentals=0
        ),
        name="project",
    )(turned, out_weight)


def weigh(gated, cot_rows, scale, r):
    width = cot_rows.shape[1] // RING
    first = lax.rem(places()[4] + r, RING) * width
    columns = lax.dynamic_slice(cot_rows, (0, first), (cot_rows.shape[0], width))
    product = lax.dot_general(gated, columns, (((0,), (0,)), ((), ())), preferred_element_type=F32)
    return (product * scale).astype(BF16)


def nearby(refs, distance, way, first, modes, lanes):
    _, _, _, low, x = places()
    before = x if way == 1 else RING - 1 - x
    other_counts = low == (way + 1) // 2
    other = refs[0].shape[0] // 2 if way == 1 else modes
    step = distance % RING
    ref = refs[way * step % RING]
    mine = ref[pl.ds(first, modes), lanes]
    theirs = jnp.where(other_counts, ref[pl.ds(other + first, modes), lanes], 0.0)
    if distance < RING:
        return jnp.where(step <= before, mine, theirs)
    return jnp.where(step <= before, theirs, 0.0)


def forward_ends(key_ref, value_ref, log_ref, ends_ref, sub_ref, drive_ref, decay_ref, zero_ref):
    length, channels = key_ref.shape
    modes = log_ref.shape[0]
    span = length // SUBS
    decay_ref[...] = jnp.exp(-jnp.exp(log_ref[...]))
    zero_ref[...] = jnp.zeros_like(zero_ref)
    for tile, lanes in lane_tiles(channels):
        drive_ref[tile] = key_ref[:, lanes].astype(F32) * value_ref[:, lanes].astype(F32)
        decay = [spread(decay_ref, m, lanes) for m in range(modes)]

        def step(i, carry):
            now, lag = carry
            u = drive_ref[tile, strided(i, span)]
            lag = [decay[m] * (lag[m] + now[m]) for m in range(modes)]
            now = [decay[m] * now[m] + u for m in range(modes)]
            return now, lag

        zero = [zero_ref[...]] * modes
        now, lag = lax.fori_loop(0, span, step, (zero, zero), unroll=4)
        for m in range(modes):
            sub_ref[tile, strided(m, modes)] = now[m]
            sub_ref[tile, strided(SUBS * modes + m, modes)] = lag[m]
        power = jnp.exp(-span * jnp.exp(log_ref[:, lanes]))
        state = jnp.zeros_like(power)
        lagged = jnp.zeros_like(power)
        for j in range(SUBS):
            lagged = power * (lagged + span * state) + sub_ref[tile, pl.ds((SUBS + j) * modes, modes)]
            state = power * state + sub_ref[tile, pl.ds(j * modes, modes)]
        ends_ref[pl.ds(0, modes), lanes] = state
        ends_ref[pl.ds(modes, modes), lanes] = lagged


def forward_full(*refs):
    (query_ref, drive_ref, sub_ref, log_ref, residue_ref, skip_ref, *end_refs) = refs[:-6]
    (gated_ref, turned_ref, pre_ref, lead_ref, decay_ref, gain_ref) = refs[-6:]
    length, channels = query_ref.shape
    modes = log_ref.shape[0]
    span = length // SUBS
    rate = jnp.exp(log_ref[...])
    decay_ref[...] = jnp.exp(-rate)
    gain_ref[...] = residue_ref[...] * jnp.sqrt(2.0 * rate)
    for tile, lanes in lane_tiles(channels):
        rate = jnp.exp(log_ref[:, lanes])
        stretch = jnp.exp(-length * rate)
        power = jnp.exp(-span * rate)
        state = jnp.zeros_like(rate)
        lagged = jnp.zeros_like(rate)
        for distance in range(2 * RING - 1, 0, -1):
            lagged = stretch * (lagged + length * state) + nearby(end_refs, distance, 1, modes, modes, lanes)
            state = stretch * state + nearby(end_refs, distance, 1, 0, modes, lanes)
        for j in range(SUBS):
            now_rows, lag_rows = (pl.ds((j + k) * modes, modes) for k in (0, SUBS))
            lead_ref[tile, now_rows] = state
            lead_ref[tile, lag_rows] = lagged
            lagged = power * (lagged + span * state) + sub_ref[tile, lag_rows]
            state = power * state + sub_ref[tile, now_rows]
        decay = [spread(decay_ref, m, lanes) for m in range(modes)]
        gain = [spread(gain_ref, m, lanes) for m in range(modes)]
        skip = spread(skip_ref, 0, lanes)

        def step(i, now):
            place = strided(i, span)
            u = drive_ref[tile, place]
            now = [decay[m] * now[m] + u for m in range(modes)]
            pre_ref[tile, place] = tree_sum([gain[m] * now[m] for m in range(modes)]) + skip * u
            return now

        first = [lead_ref[tile, strided(m, modes)] for m in range(modes)]
        lax.fori_loop(0, span, step, first, unroll=4)
        gated_ref[:, lanes] = (query_ref[:, lanes].astype(F32) * pre_ref[tile]).astype(BF16)
    part = length // (RING * 4)
    y, high, core, _, _ = places()
    for i in range(RING * 4):
        on = lax.rem(i // 4 + RING - y, RING)
        there = lax.rem(i % 2 + core, 2) * RING + jnp.where(on == 0, 3, jnp.where(on == 2, 0, (on + 1) // 2))
        there = there * 2 + lax.rem(i // 2 % 2 + high, 2)
        turned_ref[pl.ds(pl.multiple_of(there * part, part), part)] = gated_ref[pl.ds(i * part, part)]


def backward_ends(
    grad_ref, query_ref, pre_ref, drive_ref, lead_ref, log_ref,
    grad_query_ref, back_ref, sums_ref, sub_ref, decay_ref, part_ref, zero_ref,
):
    length, channels = query_ref.shape
    modes = log_ref.shape[0]
    span = length // SUBS
    half = modes // 2
    decay_ref[...] = jnp.exp(-jnp.exp(log_ref[...]))
    zero_ref[...] = jnp.zeros_like(zero_ref)
    for tile, lanes in lane_tiles(channels):
        grad = grad_ref[:, lanes].astype(F32)
        grad_query_ref[:, lanes] = (grad * pre_ref[tile]).astype(BF16)
        back_ref[tile] = grad * query_ref[:, lanes].astype(F32)
        decay = [spread(decay_ref, m, lanes) for m in range(modes)]

        def back_step(i, now):
            g = back_ref[tile, strided(span - 1 - i, span)]
            return [decay[m] * now[m] + g for m in range(modes)]

        zero = [zero_ref[...]] * modes
        now = lax.fori_loop(0, span, back_step, zero, unroll=4)
        for m in range(modes):
            sub_ref[tile, strided(m, modes)] = now[m]
        for low in range(0, modes, half):
            group = range(low, low + half)
            decay = [spread(decay_ref, m, lanes) for m in group]

            def pair_step(i, carry):
                state, lag, pair, lag_pair, skip = carry
                place = strided(i, span)
                u = drive_ref[tile, place]
                g = back_ref[tile, place]
                lag = [decay[m] * (lag[m] + state[m]) for m in range(half)]
                state = [decay[m] * state[m] + u for m in range(half)]
                pair = [pair[m] + g * state[m] for m in range(half)]
                lag_pair = [lag_pair[m] + g * lag[m] for m in range(half)]
                return state, lag, pair, lag_pair, skip + g * u

            state = [lead_ref[tile, strided(m, modes)] for m in group]
            lag = [lead_ref[tile, strided(SUBS * modes + m, modes)] for m in group]
            zero = [zero_ref[...]] * half
            state, lag, pair, lag_pair, skip = lax.fori_loop(
                0, span, pair_step, (state, lag, zero, zero, zero[0]), unroll=4
            )
            for m in range(half):
                part_ref[tile, strided(low + m, modes)] = pair[m]
                part_ref[tile, strided(SUBS * modes + low + m, modes)] = lag_pair[m]
        total = jnp.sum(skip, axis=0, keepdims=True)
        sums_ref[pl.ds(3 * modes, SUBS), lanes] = jnp.broadcast_to(total, (SUBS, LANES))
        power = jnp.exp(-span * jnp.exp(log_ref[:, lanes]))
        start = jnp.zeros_like(power)
        pair = jnp.zeros_like(power)
        lag_pair = jnp.zeros_like(power)
        for j in range(SUBS - 1, -1, -1):
            start = power * start + sub_ref[tile, pl.ds(j * modes, modes)]
            pair = pair + part_ref[tile, pl.ds(j * modes, modes)]
            lag_pair = lag_pair + part_ref[tile, pl.ds((SUBS + j) * modes, modes)]
        sums_ref[pl.ds(0, modes), lanes] = start
        sums_ref[pl.ds(modes, modes), lanes] = pair
        sums_ref[pl.ds(2 * modes, modes), lanes] = lag_pair


def backward_full(*refs, scale):
    (key_ref, value_ref, back_ref, sub_ref, log_ref, residue_ref, skip_ref, *sum_refs) = refs[:-9]
    (grad_key_ref, grad_value_ref, grad_residue_ref, grad_decay_ref, grad_skip_ref) = refs[-9:-4]
    (decay_ref, gain_ref, lead_ref, drive_grad_ref) = refs[-4:]
    length, channels = key_ref.shape
    modes = log_ref.shape[0]
    span = length // SUBS
    rate = jnp.exp(log_ref[...])
    norm = jnp.sqrt(2.0 * rate)
    gain = residue_ref[...] * norm
    decay_ref[...] = jnp.exp(-rate)
    gain_ref[...] = gain
    pair = tree_sum([ref[pl.ds(2 * modes, modes)] for ref in sum_refs])
    lag_pair = tree_sum([ref[pl.ds(3 * modes, modes)] for ref in sum_refs])
    grad_residue_ref[...] = norm * pair * scale
    grad_decay_ref[...] = gain * (0.5 * pair - rate * lag_pair) * scale
    grad_skip_ref[...] = tree_sum([ref[pl.ds(4 * modes, SUBS)] for ref in sum_refs]) * scale
    for tile, lanes in lane_tiles(channels):
        rate = jnp.exp(log_ref[:, lanes])
        stretch = jnp.exp(-length * rate)
        power = jnp.exp(-span * rate)
        start = jnp.zeros_like(rate)
        for distance in range(2 * RING - 1, 0, -1):
            start = stretch * start + nearby(sum_refs, distance, -1, 0, modes, lanes)
        for j in range(SUBS - 1, -1, -1):
            lead_ref[tile, pl.ds(j * modes, modes)] = start
            start = power * start + sub_ref[tile, pl.ds(j * modes, modes)]
        decay = [spread(decay_ref, m, lanes) for m in range(modes)]
        gain = [spread(gain_ref, m, lanes) for m in range(modes)]
        skip = spread(skip_ref, 0, lanes)

        def step(i, now):
            place = strided(span - 1 - i, span)
            g = back_ref[tile, place]
            now = [decay[m] * now[m] + g for m in range(modes)]
            drive_grad_ref[tile, place] = tree_sum([gain[m] * now[m] for m in range(modes)]) + skip * g
            return now

        first = [lead_ref[tile, strided(m, modes)] for m in range(modes)]
        lax.fori_loop(0, span, step, first, unroll=4)
        drive_grad = drive_grad_ref[tile]
        grad_key_ref[:, lanes] = (drive_grad * value_ref[:, lanes].astype(F32)).astype(BF16)
        grad_value_ref[:, lanes] = (drive_grad * key_ref[:, lanes].astype(F32)).astype(BF16)


def call(body, args, outs, scratch, micros, name):
    whole = pl.BlockSpec(memory_space=pltpu.VMEM)
    return pl.pallas_call(
        body,
        out_shape=[jax.ShapeDtypeStruct(o.shape, o.dtype) for o in outs],
        in_specs=[whole] * len(args),
        out_specs=[whole] * len(outs),
        scratch_shapes=[pltpu.VMEM(shape, F32) for shape in scratch],
        compiler_params=pltpu.CompilerParams(vmem_limit_bytes=32 * 2**20),
        cost_estimate=pl.CostEstimate(flops=int(micros * 1.15e9), bytes_accessed=0, transcendentals=0),
        name=name,
    )(*args)


def like(shape, dtype):
    return jax.ShapeDtypeStruct(shape, dtype)


def spread_over_x(value):
    return [value] + [hop(value, x=offset) for offset in range(1, RING)]


def together(*values):
    return lax.optimization_barrier(values)


def local(queries, key_proj, value_proj, skip_gain, residue, log_decay, out_weight, cotangent):
    length, channels = queries.shape
    modes = residue.shape[0]
    blocks = lax.axis_size("seq")
    scale = 1.0 / math.sqrt(length * blocks)
    skip_row = skip_gain.reshape(1, channels)
    tiles = channels // LANES
    wide = like((tiles, length, LANES), F32)
    narrow = like((length, channels), BF16)
    table = (modes, channels)

    block = gather_z(cotangent)
    ends, subs, driving = call(
        forward_ends,
        (key_proj, value_proj, log_decay),
        (like((2 * modes, channels), F32), like((tiles, 2 * SUBS * modes, LANES), F32), wide),
        [table, (SUBS, LANES)],
        0.1,
        "forward_ends",
    )
    ends_pair = jnp.concatenate([ends, hop(ends, pair=1)])
    block, ends_pair = together(block, ends_pair)
    near_blocks = [hop(block, y=1), hop(block, y=-1)]
    earlier = spread_over_x(ends_pair)
    gated, turned, pre_gate, lead = call(
        forward_full,
        (queries, driving, subs, log_decay, residue, skip_row, *earlier),
        (narrow, narrow, wide, like((tiles, 2 * SUBS * modes, LANES), F32)),
        [table, table],
        0.1,
        "forward_full",
    )
    turned, *near_blocks = together(turned, *near_blocks)
    near_first, near_rest, far_first, far_rest = project(turned, out_weight)
    got_first, got_rest = hop(far_first, core=1), hop(far_rest, core=1)
    gated_pair = jnp.concatenate([gated, hop(gated, pair=1)])
    opposite = add(near_first, got_first).astype(BF16)
    cot_rows, opposite = gather_y(block, near_blocks, opposite)
    cot_rows, got_rest = together(cot_rows.reshape(2 * length, -1), got_rest)

    half = out_weight.shape[1] // 2
    low_weight = lax.dynamic_slice(out_weight, (0, places()[3] * half), (channels, half))
    weights = {2: weigh(gated_pair, cot_rows, scale, 2)}
    cot_rows, weights[2] = together(cot_rows, weights[2])
    grad_parts = lax.dot_general(cot_rows, low_weight, (((1,), (1,)), ((), ())), preferred_element_type=F32)
    cot_rows, grad_parts = together(cot_rows, grad_parts)
    theirs = hop(grad_parts[length:].astype(BF16), pair=1)
    part = opposite.shape[0] // 2
    low_sum, high_sum = hop(opposite[:part], y=1), hop(opposite[part:], y=-1)
    up_low, up_high, down_low, down_high, own_low, own_high = (
        add(near_rest[i * part : (i + 1) * part], got_rest[i * part : (i + 1) * part]) for i in range(6)
    )
    up_low = add(up_low, low_sum).astype(BF16)
    down_high = add(down_high, high_sum).astype(BF16)
    for r in (1, 3, 0):
        weights[r] = weigh(gated_pair, cot_rows, scale, r)
    cut = channels // 2
    upper, lower = hop(weights[2][:cut], x=1), hop(weights[2][cut:], x=-1)
    weights_up = jnp.concatenate([add(weights[1][:cut], upper).astype(BF16), weights[1][cut:]])
    weights_down = jnp.concatenate([weights[3][:cut], add(weights[3][cut:], lower).astype(BF16)])
    theirs, up_low, down_high, weights_up, weights_down, own_weights = together(
        theirs, up_low, down_high, weights_up, weights_down, weights[0]
    )
    grad_weight = add(own_weights, hop(weights_up, x=1), hop(weights_down, x=-1)).astype(BF16)
    grad_gated = add(grad_parts[:length], theirs)
    other_high = add(own_high, hop(up_high.astype(BF16), y=1), hop(down_high, y=-1)).astype(BF16)
    width = other_high.shape[1] // 2
    crossed = [hop(hop(other_high[:, :width], z=1), z=1), hop(hop(other_high[:, width:], z=-1), z=-1)]
    mixed = add(own_low, hop(up_low, y=1), hop(down_low.astype(BF16), y=-1), jnp.concatenate(crossed, axis=1)).astype(BF16)

    grad_query, back, sums, back_subs = call(
        backward_ends,
        (grad_gated, queries, pre_gate, driving, lead, log_decay),
        (narrow, wide, like((3 * modes + SUBS, channels), F32), like((tiles, SUBS * modes, LANES), F32)),
        [table, (tiles, 2 * SUBS * modes, LANES), (SUBS, LANES)],
        0.1,
        "backward_ends",
    )
    others = hop(sums, pair=1)
    all_sums = spread_over_x(
        jnp.concatenate([sums[:modes], others[:modes], sums[modes:] + others[modes:]])
    )
    grad_key, grad_value, grad_residue, grad_decay, grad_skip = call(
        functools.partial(backward_full, scale=scale),
        (key_proj, value_proj, back, back_subs, log_decay, residue, skip_row, *all_sums),
        (narrow, narrow, like(table, F32), like(table, F32), like((SUBS, channels), F32)),
        [table, table, (tiles, SUBS * modes, LANES), (tiles, length, LANES)],
        0.1,
        "backward_full",
    )
    return (
        mixed,
        grad_query,
        grad_key,
        grad_value,
        grad_weight,
        grad_residue,
        grad_decay,
        grad_skip[0],
    )


def solution(mesh):
    in_specs = (
        P("seq", "chan"),
        P("seq", "chan"),
        P("seq", "chan"),
        P("chan"),
        P(None, "chan"),
        P(None, "chan"),
        P("chan", None),
        P(("seq", "chan"), None),
    )
    out_specs = (
        P(("seq", "chan"), None),
        P("seq", "chan"),
        P("seq", "chan"),
        P("seq", "chan"),
        P("chan", "seq"),
        P(None, "chan"),
        P(None, "chan"),
        P("chan"),
    )
    return jax.shard_map(local, mesh=mesh, in_specs=in_specs, out_specs=out_specs, check_vma=False)
```

```python
import functools
import itertools
import math

import jax
import jax.numpy as jnp
from jax import lax
from jax.experimental import pallas as pl
from jax.experimental.pallas import tpu as pltpu
from jax.sharding import PartitionSpec as P

RING = 4
SUBS = 8
LANES = 128
F32 = jnp.float32
BF16 = jnp.bfloat16


def strided(first, step):
    return pl.ds(first, SUBS, stride=step)


def spread(ref, mode, lanes):
    return jnp.broadcast_to(ref[pl.ds(mode, 1), lanes], (SUBS, LANES))


def tree_sum(parts):
    while len(parts) > 1:
        parts = [a + b for a, b in zip(parts[::2], parts[1::2])] + parts[len(parts) & ~1 :]
    return parts[0]


def lane_tiles(channels):
    return [(tile, pl.ds(tile * LANES, LANES)) for tile in range(channels // LANES)]


def places():
    chan, seq = lax.axis_index("chan"), lax.axis_index("seq")
    return chan // 4, lax.rem(chan // 2, 2), lax.rem(chan, 2), seq // RING, lax.rem(seq, RING)


def hop(value, x=0, y=0, z=0, core=0, pair=0):
    moves = []
    for i, j, k, c in itertools.product(range(RING), range(RING), range(RING), range(2)):
        there = ((i + x) % RING, (j + y) % RING, ((k + z) % RING) ^ pair, c ^ core)
        moves.append(tuple(((b * 2 + d // 2) * 2 + e) * 2 * RING + d % 2 * RING + a for a, b, d, e in ((i, j, k, c), there)))
    return lax.ppermute(value, ("chan", "seq"), moves)


def gather_z(cotangent):
    _, high, _, low, _ = places()
    tokens, width = cotangent.shape
    half = width // 2
    mine = lax.dynamic_slice(cotangent, (0, low * half), (tokens, half))
    theirs = lax.dynamic_slice(cotangent, (0, (1 - low) * half), (tokens, half))
    above, below, across = hop(theirs, z=1), hop(theirs, z=-1), hop(mine, z=2)
    stack = jnp.where(high == 0, jnp.stack([mine, across]), jnp.stack([across, mine]))
    same, differ = jnp.where(low == 1, above, below), jnp.where(low == 1, below, above)
    other = jnp.where(high == 0, jnp.stack([same, differ]), jnp.stack([differ, same]))
    return jnp.stack([stack, other])


def place_blocks(*sides):
    y, _, core, _, _ = places()
    _, tokens, half = sides[0][0].shape
    whole = jnp.zeros((2, RING, 2, 2, tokens, half), BF16)
    for step, blocks in zip((0, RING - 1, 1, 2), zip(*sides)):
        row = lax.rem(y + step, RING)
        for side, block in enumerate(blocks):
            for part, at_core in ((block, core), (hop(block, core=1), 1 - core)):
                whole = lax.dynamic_update_slice(whole, part[None, None, :, None], (side, row, 0, at_core, 0, 0))
    return whole


def add(*parts):
    return functools.reduce(jnp.add, [part.astype(F32) for part in parts])


def project_tile(rows_ref, weight_ref, *out_refs):
    product = jnp.dot(rows_ref[...], weight_ref[...], preferred_element_type=F32).astype(BF16)
    first = 0
    for ref in out_refs:
        ref[...] = product[first : first + ref.shape[0]]
        first += ref.shape[0]


def project(turned, out_weight):
    rows, depth = turned.shape
    width = out_weight.shape[1]
    tile = 1024
    sizes = [rows // 8, 3 * rows // 8] * 2
    return pl.pallas_call(
        project_tile,
        grid=(width // tile,),
        out_shape=[jax.ShapeDtypeStruct((size, width), BF16) for size in sizes],
        in_specs=[pl.BlockSpec((rows, depth), lambda i: (0, 0)), pl.BlockSpec((depth, tile), lambda i: (0, i))],
        out_specs=[pl.BlockSpec((size, tile), lambda i: (0, i)) for size in sizes],
        compiler_params=pltpu.CompilerParams(vmem_limit_bytes=32 * 2**20),
        cost_estimate=pl.CostEstimate(
            flops=2 * rows * depth * width, bytes_accessed=2 * width * (rows + depth), transcendentals=0
        ),
        name="project",
    )(turned, out_weight)


def weigh(gated, cot_rows, scale, r):
    width = cot_rows.shape[1] // RING
    first = lax.rem(places()[4] + r, RING) * width
    columns = lax.dynamic_slice(cot_rows, (0, first), (cot_rows.shape[0], width))
    product = lax.dot_general(gated, columns, (((0,), (0,)), ((), ())), preferred_element_type=F32)
    return (product * scale).astype(BF16)


def nearby(refs, distance, way, first, modes, lanes):
    _, _, _, low, x = places()
    before = x if way == 1 else RING - 1 - x
    other_counts = low == (way + 1) // 2
    other = refs[0].shape[0] // 2 if way == 1 else modes
    step = distance % RING
    ref = refs[way * step % RING]
    mine = ref[pl.ds(first, modes), lanes]
    theirs = jnp.where(other_counts, ref[pl.ds(other + first, modes), lanes], 0.0)
    if distance < RING:
        return jnp.where(step <= before, mine, theirs)
    return jnp.where(step <= before, theirs, 0.0)


def forward_ends(key_ref, value_ref, log_ref, ends_ref, sub_ref, drive_ref, decay_ref, zero_ref):
    length, channels = key_ref.shape
    modes = log_ref.shape[0]
    span = length // SUBS
    decay_ref[...] = jnp.exp(-jnp.exp(log_ref[...]))
    zero_ref[...] = jnp.zeros_like(zero_ref)
    for tile, lanes in lane_tiles(channels):
        drive_ref[tile] = key_ref[:, lanes].astype(F32) * value_ref[:, lanes].astype(F32)
        decay = [spread(decay_ref, m, lanes) for m in range(modes)]

        def step(i, carry):
            now, lag = carry
            u = drive_ref[tile, strided(i, span)]
            lag = [decay[m] * (lag[m] + now[m]) for m in range(modes)]
            now = [decay[m] * now[m] + u for m in range(modes)]
            return now, lag

        zero = [zero_ref[...]] * modes
        now, lag = lax.fori_loop(0, span, step, (zero, zero), unroll=4)
        for m in range(modes):
            sub_ref[tile, strided(m, modes)] = now[m]
            sub_ref[tile, strided(SUBS * modes + m, modes)] = lag[m]
        power = jnp.exp(-span * jnp.exp(log_ref[:, lanes]))
        state = jnp.zeros_like(power)
        lagged = jnp.zeros_like(power)
        for j in range(SUBS):
            lagged = power * (lagged + span * state) + sub_ref[tile, pl.ds((SUBS + j) * modes, modes)]
            state = power * state + sub_ref[tile, pl.ds(j * modes, modes)]
        ends_ref[pl.ds(0, modes), lanes] = state
        ends_ref[pl.ds(modes, modes), lanes] = lagged


def forward_full(*refs):
    (query_ref, drive_ref, sub_ref, log_ref, residue_ref, skip_ref, *end_refs) = refs[:-6]
    (gated_ref, turned_ref, pre_ref, lead_ref, decay_ref, gain_ref) = refs[-6:]
    length, channels = query_ref.shape
    modes = log_ref.shape[0]
    span = length // SUBS
    rate = jnp.exp(log_ref[...])
    decay_ref[...] = jnp.exp(-rate)
    gain_ref[...] = residue_ref[...] * jnp.sqrt(2.0 * rate)
    for tile, lanes in lane_tiles(channels):
        rate = jnp.exp(log_ref[:, lanes])
        stretch = jnp.exp(-length * rate)
        power = jnp.exp(-span * rate)
        state = jnp.zeros_like(rate)
        lagged = jnp.zeros_like(rate)
        for distance in range(2 * RING - 1, 0, -1):
            lagged = stretch * (lagged + length * state) + nearby(end_refs, distance, 1, modes, modes, lanes)
            state = stretch * state + nearby(end_refs, distance, 1, 0, modes, lanes)
        for j in range(SUBS):
            now_rows, lag_rows = (pl.ds((j + k) * modes, modes) for k in (0, SUBS))
            lead_ref[tile, now_rows] = state
            lead_ref[tile, lag_rows] = lagged
            lagged = power * (lagged + span * state) + sub_ref[tile, lag_rows]
            state = power * state + sub_ref[tile, now_rows]
        decay = [spread(decay_ref, m, lanes) for m in range(modes)]
        gain = [spread(gain_ref, m, lanes) for m in range(modes)]
        skip = spread(skip_ref, 0, lanes)

        def step(i, now):
            place = strided(i, span)
            u = drive_ref[tile, place]
            now = [decay[m] * now[m] + u for m in range(modes)]
            pre_ref[tile, place] = tree_sum([gain[m] * now[m] for m in range(modes)]) + skip * u
            return now

        first = [lead_ref[tile, strided(m, modes)] for m in range(modes)]
        lax.fori_loop(0, span, step, first, unroll=4)
        gated_ref[:, lanes] = (query_ref[:, lanes].astype(F32) * pre_ref[tile]).astype(BF16)
    part = length // (RING * 4)
    y, high, core, _, _ = places()
    for i in range(RING * 4):
        on = lax.rem(i // 4 + RING - y, RING)
        there = lax.rem(i % 2 + core, 2) * RING + jnp.where(on == 0, 3, jnp.where(on == 2, 0, (on + 1) // 2))
        there = there * 2 + lax.rem(i // 2 % 2 + high, 2)
        turned_ref[pl.ds(pl.multiple_of(there * part, part), part)] = gated_ref[pl.ds(i * part, part)]


def backward_ends(
    grad_ref, query_ref, pre_ref, drive_ref, lead_ref, log_ref,
    grad_query_ref, back_ref, sums_ref, sub_ref, decay_ref, part_ref, zero_ref,
):
    length, channels = query_ref.shape
    modes = log_ref.shape[0]
    span = length // SUBS
    half = modes // 2
    decay_ref[...] = jnp.exp(-jnp.exp(log_ref[...]))
    zero_ref[...] = jnp.zeros_like(zero_ref)
    for tile, lanes in lane_tiles(channels):
        grad = grad_ref[:, lanes].astype(F32)
        grad_query_ref[:, lanes] = (grad * pre_ref[tile]).astype(BF16)
        back_ref[tile] = grad * query_ref[:, lanes].astype(F32)
        decay = [spread(decay_ref, m, lanes) for m in range(modes)]

        def back_step(i, now):
            g = back_ref[tile, strided(span - 1 - i, span)]
            return [decay[m] * now[m] + g for m in range(modes)]

        zero = [zero_ref[...]] * modes
        now = lax.fori_loop(0, span, back_step, zero, unroll=4)
        for m in range(modes):
            sub_ref[tile, strided(m, modes)] = now[m]
        for low in range(0, modes, half):
            group = range(low, low + half)
            decay = [spread(decay_ref, m, lanes) for m in group]

            def pair_step(i, carry):
                state, lag, pair, lag_pair, skip = carry
                place = strided(i, span)
                u = drive_ref[tile, place]
                g = back_ref[tile, place]
                lag = [decay[m] * (lag[m] + state[m]) for m in range(half)]
                state = [decay[m] * state[m] + u for m in range(half)]
                pair = [pair[m] + g * state[m] for m in range(half)]
                lag_pair = [lag_pair[m] + g * lag[m] for m in range(half)]
                return state, lag, pair, lag_pair, skip + g * u

            state = [lead_ref[tile, strided(m, modes)] for m in group]
            lag = [lead_ref[tile, strided(SUBS * modes + m, modes)] for m in group]
            zero = [zero_ref[...]] * half
            state, lag, pair, lag_pair, skip = lax.fori_loop(
                0, span, pair_step, (state, lag, zero, zero, zero[0]), unroll=4
            )
            for m in range(half):
                part_ref[tile, strided(low + m, modes)] = pair[m]
                part_ref[tile, strided(SUBS * modes + low + m, modes)] = lag_pair[m]
        total = jnp.sum(skip, axis=0, keepdims=True)
        sums_ref[pl.ds(3 * modes, SUBS), lanes] = jnp.broadcast_to(total, (SUBS, LANES))
        power = jnp.exp(-span * jnp.exp(log_ref[:, lanes]))
        start = jnp.zeros_like(power)
        pair = jnp.zeros_like(power)
        lag_pair = jnp.zeros_like(power)
        for j in range(SUBS - 1, -1, -1):
            start = power * start + sub_ref[tile, pl.ds(j * modes, modes)]
            pair = pair + part_ref[tile, pl.ds(j * modes, modes)]
            lag_pair = lag_pair + part_ref[tile, pl.ds((SUBS + j) * modes, modes)]
        sums_ref[pl.ds(0, modes), lanes] = start
        sums_ref[pl.ds(modes, modes), lanes] = pair
        sums_ref[pl.ds(2 * modes, modes), lanes] = lag_pair


def backward_full(*refs, scale):
    (key_ref, value_ref, back_ref, sub_ref, log_ref, residue_ref, skip_ref, *sum_refs) = refs[:-9]
    (grad_key_ref, grad_value_ref, grad_residue_ref, grad_decay_ref, grad_skip_ref) = refs[-9:-4]
    (decay_ref, gain_ref, lead_ref, drive_grad_ref) = refs[-4:]
    length, channels = key_ref.shape
    modes = log_ref.shape[0]
    span = length // SUBS
    rate = jnp.exp(log_ref[...])
    norm = jnp.sqrt(2.0 * rate)
    gain = residue_ref[...] * norm
    decay_ref[...] = jnp.exp(-rate)
    gain_ref[...] = gain
    pair = tree_sum([ref[pl.ds(2 * modes, modes)] for ref in sum_refs])
    lag_pair = tree_sum([ref[pl.ds(3 * modes, modes)] for ref in sum_refs])
    grad_residue_ref[...] = norm * pair * scale
    grad_decay_ref[...] = gain * (0.5 * pair - rate * lag_pair) * scale
    grad_skip_ref[...] = tree_sum([ref[pl.ds(4 * modes, SUBS)] for ref in sum_refs]) * scale
    for tile, lanes in lane_tiles(channels):
        rate = jnp.exp(log_ref[:, lanes])
        stretch = jnp.exp(-length * rate)
        power = jnp.exp(-span * rate)
        start = jnp.zeros_like(rate)
        for distance in range(2 * RING - 1, 0, -1):
            start = stretch * start + nearby(sum_refs, distance, -1, 0, modes, lanes)
        for j in range(SUBS - 1, -1, -1):
            lead_ref[tile, pl.ds(j * modes, modes)] = start
            start = power * start + sub_ref[tile, pl.ds(j * modes, modes)]
        decay = [spread(decay_ref, m, lanes) for m in range(modes)]
        gain = [spread(gain_ref, m, lanes) for m in range(modes)]
        skip = spread(skip_ref, 0, lanes)

        def step(i, now):
            place = strided(span - 1 - i, span)
            g = back_ref[tile, place]
            now = [decay[m] * now[m] + g for m in range(modes)]
            drive_grad_ref[tile, place] = tree_sum([gain[m] * now[m] for m in range(modes)]) + skip * g
            return now

        first = [lead_ref[tile, strided(m, modes)] for m in range(modes)]
        lax.fori_loop(0, span, step, first, unroll=4)
        drive_grad = drive_grad_ref[tile]
        grad_key_ref[:, lanes] = (drive_grad * value_ref[:, lanes].astype(F32)).astype(BF16)
        grad_value_ref[:, lanes] = (drive_grad * key_ref[:, lanes].astype(F32)).astype(BF16)


def call(body, args, outs, scratch, micros, name):
    whole = pl.BlockSpec(memory_space=pltpu.VMEM)
    return pl.pallas_call(
        body,
        out_shape=[jax.ShapeDtypeStruct(o.shape, o.dtype) for o in outs],
        in_specs=[whole] * len(args),
        out_specs=[whole] * len(outs),
        scratch_shapes=[pltpu.VMEM(shape, F32) for shape in scratch],
        compiler_params=pltpu.CompilerParams(vmem_limit_bytes=32 * 2**20),
        cost_estimate=pl.CostEstimate(flops=int(micros * 1.15e9), bytes_accessed=0, transcendentals=0),
        name=name,
    )(*args)


def like(shape, dtype):
    return jax.ShapeDtypeStruct(shape, dtype)


def spread_over_x(value):
    return [value] + [hop(value, x=offset) for offset in range(1, RING)]


def together(*values):
    return lax.optimization_barrier(values)


def local(queries, key_proj, value_proj, skip_gain, residue, log_decay, out_weight, cotangent):
    length, channels = queries.shape
    modes = residue.shape[0]
    blocks = lax.axis_size("seq")
    scale = 1.0 / math.sqrt(length * blocks)
    skip_row = skip_gain.reshape(1, channels)
    tiles = channels // LANES
    wide = like((tiles, length, LANES), F32)
    narrow = like((length, channels), BF16)
    table = (modes, channels)

    block, log_first = together(gather_z(cotangent), log_decay)
    before_own, after_other = hop(block[0], y=1), hop(block[1], y=-1)
    ends, subs, driving = call(
        forward_ends,
        (key_proj, value_proj, log_first),
        (like((2 * modes, channels), F32), like((tiles, 2 * SUBS * modes, LANES), F32), wide),
        [table, (SUBS, LANES)],
        0.1,
        "forward_ends",
    )
    ends_pair = jnp.concatenate([ends, hop(ends, pair=1)])
    before_own, after_other, ends_pair = together(before_own, after_other, ends_pair)
    before_other, after_own = hop(block[1], y=1), hop(block[0], y=-1)
    earlier = spread_over_x(ends_pair)
    gated, turned, pre_gate, lead = call(
        forward_full,
        (queries, driving, subs, log_decay, residue, skip_row, *earlier),
        (narrow, narrow, wide, like((tiles, 2 * SUBS * modes, LANES), F32)),
        [table, table],
        0.1,
        "forward_full",
    )
    before_own, after_other, turned = together(before_own, after_other, turned)
    far_own, far_other = hop(before_own, y=1), hop(after_other, y=-1)
    before_other, after_own, turned = together(before_other, after_own, turned)
    near_first, near_rest, far_first, far_rest = project(turned, out_weight)
    got_first, got_rest = hop(far_first, core=1), hop(far_rest, core=1)
    gated_pair = jnp.concatenate([gated, hop(gated, pair=1)])
    opposite = add(near_first, got_first).astype(BF16)
    far_own, far_other, opposite = together(far_own, far_other, opposite)
    cot_rows = place_blocks(
        (block[0], before_own, after_own, far_own), (block[1], before_other, after_other, far_other)
    )
    cot_rows, got_rest = together(cot_rows.reshape(2 * length, -1), got_rest)

    half = out_weight.shape[1] // 2
    low_weight = lax.dynamic_slice(out_weight, (0, places()[3] * half), (channels, half))
    weights = {2: weigh(gated_pair, cot_rows, scale, 2)}
    cot_rows, weights[2] = together(cot_rows, weights[2])
    grad_parts = lax.dot_general(cot_rows, low_weight, (((1,), (1,)), ((), ())), preferred_element_type=F32)
    cot_rows, grad_parts, got_rest = together(cot_rows, grad_parts, got_rest)
    theirs = hop(grad_parts[length:].astype(BF16), pair=1)
    part = opposite.shape[0] // 2
    low_sum, high_sum = hop(opposite[:part], y=1), hop(opposite[part:], y=-1)
    above, below, own = (
        add(near_rest[i * 2 * part : (i + 1) * 2 * part], got_rest[i * 2 * part : (i + 1) * 2 * part]) for i in range(3)
    )
    above = jnp.concatenate([add(above[:part], low_sum), above[part:]]).astype(BF16)
    below = jnp.concatenate([below[:part], add(below[part:], high_sum)]).astype(BF16)
    for r in (1, 3, 0):
        weights[r] = weigh(gated_pair, cot_rows, scale, r)
    cut = channels // 2
    upper, lower = hop(weights[2][:cut], x=1), hop(weights[2][cut:], x=-1)
    up_sum = add(weights[1][:cut], upper).astype(BF16)
    down_sum = add(weights[3][cut:], lower).astype(BF16)
    up_rest, down_rest = weights[1][cut:], weights[3][:cut]
    theirs, up_sum, down_sum, up_rest, down_rest = together(theirs, up_sum, down_sum, up_rest, down_rest)
    up_rest, down_rest = hop(up_rest, x=1), hop(down_rest, x=-1)
    grad_gated = add(grad_parts[:length], theirs)
    own = add(own, hop(above, y=1), hop(below, y=-1))
    leaving = own[part:].astype(BF16)
    width = leaving.shape[1] // 2
    halfway = hop(leaving[:, width:], z=-1)
    crossed = hop(leaving[:, :width], z=2)

    grad_query, back, sums, back_subs = call(
        backward_ends,
        (grad_gated, queries, pre_gate, driving, lead, log_decay),
        (narrow, wide, like((3 * modes + SUBS, channels), F32), like((tiles, SUBS * modes, LANES), F32)),
        [table, (tiles, 2 * SUBS * modes, LANES), (SUBS, LANES)],
        2.0,
        "backward_ends",
    )
    sums, up_rest, down_rest = together(sums, up_rest, down_rest)
    up_sum, down_sum = hop(up_sum, x=1), hop(down_sum, x=-1)
    others = hop(sums, pair=1)
    sums_pair = jnp.concatenate([sums[:modes], others[:modes], sums[modes:] + others[modes:]])
    sums_pair, up_sum, down_sum = together(sums_pair, up_sum, down_sum)
    crossed = jnp.concatenate([crossed, hop(halfway, z=-1)], axis=1)
    mixed = add(own[:part], crossed).astype(BF16)
    all_sums = spread_over_x(sums_pair)
    grad_weight = jnp.concatenate(
        [add(weights[0][:cut], up_sum, down_rest), add(weights[0][cut:], up_rest, down_sum)]
    ).astype(BF16)
    grad_key, grad_value, grad_residue, grad_decay, grad_skip = call(
        functools.partial(backward_full, scale=scale),
        (key_proj, value_proj, back, back_subs, log_decay, residue, skip_row, *all_sums),
        (narrow, narrow, like(table, F32), like(table, F32), like((SUBS, channels), F32)),
        [table, table, (tiles, SUBS * modes, LANES), (tiles, length, LANES)],
        0.1,
        "backward_full",
    )
    return (
        mixed,
        grad_query,
        grad_key,
        grad_value,
        grad_weight,
        grad_residue,
        grad_decay,
        grad_skip[0],
    )


def solution(mesh):
    in_specs = (
        P("seq", "chan"),
        P("seq", "chan"),
        P("seq", "chan"),
        P("chan"),
        P(None, "chan"),
        P(None, "chan"),
        P("chan", None),
        P(("seq", "chan"), None),
    )
    out_specs = (
        P(("seq", "chan"), None),
        P("seq", "chan"),
        P("seq", "chan"),
        P("seq", "chan"),
        P("chan", "seq"),
        P(None, "chan"),
        P(None, "chan"),
        P("chan"),
    )
    return jax.shard_map(local, mesh=mesh, in_specs=in_specs, out_specs=out_specs, check_vma=False)
```

```python
import functools
import itertools
import math

import jax
import jax.numpy as jnp
from jax import lax
from jax.experimental import pallas as pl
from jax.experimental.pallas import tpu as pltpu
from jax.sharding import PartitionSpec as P

RING = 4
MAIN, OTHER = (1, -1), (-1, 1)
SUBS = 8
LANES = 128
F32 = jnp.float32
BF16 = jnp.bfloat16


def strided(first, step):
    return pl.ds(first, SUBS, stride=step)


def spread(ref, mode, lanes):
    return jnp.broadcast_to(ref[pl.ds(mode, 1), lanes], (SUBS, LANES))


def tree_sum(parts):
    while len(parts) > 1:
        parts = [a + b for a, b in zip(parts[::2], parts[1::2])] + parts[len(parts) & ~1 :]
    return parts[0]


def lane_tiles(channels):
    return [(tile, pl.ds(tile * LANES, LANES)) for tile in range(channels // LANES)]


def places():
    chan, seq = lax.axis_index("chan"), lax.axis_index("seq")
    return chan // 4, lax.rem(chan // 2, 2), lax.rem(chan, 2), seq // RING, lax.rem(seq, RING)


def hop(value, x=0, y=0, z=0, core=0, pair=0):
    moves = []
    for i, j, k, c in itertools.product(range(RING), range(RING), range(RING), range(2)):
        dx, dy, dz = (step[c] if isinstance(step, tuple) else step for step in (x, y, z))
        if None in (dx, dy, dz):
            continue
        there = ((i + dx) % RING, (j + dy) % RING, ((k + dz) % RING) ^ pair, c ^ core)
        moves.append(tuple(((b * 2 + d // 2) * 2 + e) * 2 * RING + d % 2 * RING + a for a, b, d, e in ((i, j, k, c), there)))
    return lax.ppermute(value, ("chan", "seq"), moves)


def by_core(first, second):
    return jnp.where(places()[2] == 0, first, second)


def gather_z(cotangent):
    _, high, _, low, _ = places()
    tokens, width = cotangent.shape
    half = width // 2
    mine = lax.dynamic_slice(cotangent, (0, low * half), (tokens, half))
    theirs = lax.dynamic_slice(cotangent, (0, (1 - low) * half), (tokens, half))
    above, below, across = hop(theirs, z=1), hop(theirs, z=-1), hop(mine, z=2)
    stack = jnp.where(high == 0, jnp.stack([mine, across]), jnp.stack([across, mine]))
    same, differ = jnp.where(low == 1, above, below), jnp.where(low == 1, below, above)
    other = jnp.where(high == 0, jnp.stack([same, differ]), jnp.stack([differ, same]))
    return jnp.stack([stack, other])


def place_blocks(*blocks):
    y, _, core, _, _ = places()
    _, _, tokens, half = blocks[0].shape
    whole = jnp.zeros((2, RING, 2, 2, tokens, half), BF16)
    for block, steps in zip(blocks, ((0, 0), (RING - 1, 1), (1, RING - 1), (2, 2))):
        for part, at_core in ((block, core), (hop(block, core=1), 1 - core)):
            row = lax.rem(y + jnp.where(at_core == 0, *steps), RING)
            whole = lax.dynamic_update_slice(whole, part[:, None, :, None], (0, row, 0, at_core, 0, 0))
    return whole


def add(*parts):
    return functools.reduce(jnp.add, [part.astype(F32) for part in parts])


def project_tile(rows_ref, weight_ref, *out_refs):
    product = jnp.dot(rows_ref[...], weight_ref[...], preferred_element_type=F32).astype(BF16)
    first = 0
    for ref in out_refs:
        ref[...] = product[first : first + ref.shape[0]]
        first += ref.shape[0]


def project(turned, out_weight):
    rows, depth = turned.shape
    width = out_weight.shape[1]
    tile = 1024
    sizes = [rows // 8, 3 * rows // 8] * 2
    return pl.pallas_call(
        project_tile,
        grid=(width // tile,),
        out_shape=[jax.ShapeDtypeStruct((size, width), BF16) for size in sizes],
        in_specs=[pl.BlockSpec((rows, depth), lambda i: (0, 0)), pl.BlockSpec((depth, tile), lambda i: (0, i))],
        out_specs=[pl.BlockSpec((size, tile), lambda i: (0, i)) for size in sizes],
        compiler_params=pltpu.CompilerParams(vmem_limit_bytes=32 * 2**20),
        cost_estimate=pl.CostEstimate(
            flops=2 * rows * depth * width, bytes_accessed=2 * width * (rows + depth), transcendentals=0
        ),
        name="project",
    )(turned, out_weight)


def weigh(gated, cot_rows, scale, block):
    width = cot_rows.shape[1] // RING
    columns = lax.dynamic_slice(cot_rows, (0, block * width), (cot_rows.shape[0], width))
    product = lax.dot_general(gated, columns, (((0,), (0,)), ((), ())), preferred_element_type=F32)
    return (product * scale).astype(BF16)


def nearby(refs, distance, way, first, modes, lanes):
    _, _, _, low, x = places()
    before = x if way == 1 else RING - 1 - x
    other_counts = low == (way + 1) // 2
    other = refs[0].shape[0] // 2 if way == 1 else modes
    step = distance % RING
    ref = refs[way * step % RING]
    mine = ref[pl.ds(first, modes), lanes]
    theirs = jnp.where(other_counts, ref[pl.ds(other + first, modes), lanes], 0.0)
    if distance < RING:
        return jnp.where(step <= before, mine, theirs)
    return jnp.where(step <= before, theirs, 0.0)


def forward_ends(key_ref, value_ref, log_ref, ends_ref, sub_ref, drive_ref, decay_ref, zero_ref):
    length, channels = key_ref.shape
    modes = log_ref.shape[0]
    span = length // SUBS
    decay_ref[...] = jnp.exp(-jnp.exp(log_ref[...]))
    zero_ref[...] = jnp.zeros_like(zero_ref)
    for tile, lanes in lane_tiles(channels):
        drive_ref[tile] = key_ref[:, lanes].astype(F32) * value_ref[:, lanes].astype(F32)
        decay = [spread(decay_ref, m, lanes) for m in range(modes)]

        def step(i, carry):
            now, lag = carry
            u = drive_ref[tile, strided(i, span)]
            lag = [decay[m] * (lag[m] + now[m]) for m in range(modes)]
            now = [decay[m] * now[m] + u for m in range(modes)]
            return now, lag

        zero = [zero_ref[...]] * modes
        now, lag = lax.fori_loop(0, span, step, (zero, zero), unroll=4)
        for m in range(modes):
            sub_ref[tile, strided(m, modes)] = now[m]
            sub_ref[tile, strided(SUBS * modes + m, modes)] = lag[m]
        power = jnp.exp(-span * jnp.exp(log_ref[:, lanes]))
        state = jnp.zeros_like(power)
        lagged = jnp.zeros_like(power)
        for j in range(SUBS):
            lagged = power * (lagged + span * state) + sub_ref[tile, pl.ds((SUBS + j) * modes, modes)]
            state = power * state + sub_ref[tile, pl.ds(j * modes, modes)]
        ends_ref[pl.ds(0, modes), lanes] = state
        ends_ref[pl.ds(modes, modes), lanes] = lagged


def forward_full(*refs):
    (query_ref, drive_ref, sub_ref, log_ref, residue_ref, skip_ref, *end_refs) = refs[:-6]
    (gated_ref, turned_ref, pre_ref, lead_ref, decay_ref, gain_ref) = refs[-6:]
    length, channels = query_ref.shape
    modes = log_ref.shape[0]
    span = length // SUBS
    rate = jnp.exp(log_ref[...])
    decay_ref[...] = jnp.exp(-rate)
    gain_ref[...] = residue_ref[...] * jnp.sqrt(2.0 * rate)
    for tile, lanes in lane_tiles(channels):
        rate = jnp.exp(log_ref[:, lanes])
        stretch = jnp.exp(-length * rate)
        power = jnp.exp(-span * rate)
        state = jnp.zeros_like(rate)
        lagged = jnp.zeros_like(rate)
        for distance in range(2 * RING - 1, 0, -1):
            lagged = stretch * (lagged + length * state) + nearby(end_refs, distance, 1, modes, modes, lanes)
            state = stretch * state + nearby(end_refs, distance, 1, 0, modes, lanes)
        for j in range(SUBS):
            now_rows, lag_rows = (pl.ds((j + k) * modes, modes) for k in (0, SUBS))
            lead_ref[tile, now_rows] = state
            lead_ref[tile, lag_rows] = lagged
            lagged = power * (lagged + span * state) + sub_ref[tile, lag_rows]
            state = power * state + sub_ref[tile, now_rows]
        decay = [spread(decay_ref, m, lanes) for m in range(modes)]
        gain = [spread(gain_ref, m, lanes) for m in range(modes)]
        skip = spread(skip_ref, 0, lanes)

        def step(i, now):
            place = strided(i, span)
            u = drive_ref[tile, place]
            now = [decay[m] * now[m] + u for m in range(modes)]
            pre_ref[tile, place] = tree_sum([gain[m] * now[m] for m in range(modes)]) + skip * u
            return now

        first = [lead_ref[tile, strided(m, modes)] for m in range(modes)]
        lax.fori_loop(0, span, step, first, unroll=4)
        gated_ref[:, lanes] = (query_ref[:, lanes].astype(F32) * pre_ref[tile]).astype(BF16)
    part = length // (RING * 4)
    y, high, core, _, _ = places()
    for i in range(RING * 4):
        on = lax.rem(i // 4 + RING - y, RING)
        kept = lax.rem(i % 2 + core, 2) == 0
        first = jnp.where(kept, 1 + 2 * core, 3 - 2 * core)
        there = jnp.where(on == 0, 3, jnp.where(on == 2, 0, jnp.where(on == first, 1, 2)))
        there = there + jnp.where(kept, 0, RING)
        there = there * 2 + lax.rem(i // 2 % 2 + high, 2)
        turned_ref[pl.ds(pl.multiple_of(there * part, part), part)] = gated_ref[pl.ds(i * part, part)]


def backward_ends(
    grad_ref, query_ref, pre_ref, drive_ref, lead_ref, log_ref,
    grad_query_ref, back_ref, sums_ref, sub_ref, decay_ref, part_ref, zero_ref,
):
    length, channels = query_ref.shape
    modes = log_ref.shape[0]
    span = length // SUBS
    half = modes // 2
    decay_ref[...] = jnp.exp(-jnp.exp(log_ref[...]))
    zero_ref[...] = jnp.zeros_like(zero_ref)
    for tile, lanes in lane_tiles(channels):
        grad = grad_ref[:, lanes].astype(F32)
        grad_query_ref[:, lanes] = (grad * pre_ref[tile]).astype(BF16)
        back_ref[tile] = grad * query_ref[:, lanes].astype(F32)
        decay = [spread(decay_ref, m, lanes) for m in range(modes)]

        def back_step(i, now):
            g = back_ref[tile, strided(span - 1 - i, span)]
            return [decay[m] * now[m] + g for m in range(modes)]

        zero = [zero_ref[...]] * modes
        now = lax.fori_loop(0, span, back_step, zero, unroll=4)
        for m in range(modes):
            sub_ref[tile, strided(m, modes)] = now[m]
        for low in range(0, modes, half):
            group = range(low, low + half)
            decay = [spread(decay_ref, m, lanes) for m in group]

            def pair_step(i, carry):
                state, lag, pair, lag_pair, skip = carry
                place = strided(i, span)
                u = drive_ref[tile, place]
                g = back_ref[tile, place]
                lag = [decay[m] * (lag[m] + state[m]) for m in range(half)]
                state = [decay[m] * state[m] + u for m in range(half)]
                pair = [pair[m] + g * state[m] for m in range(half)]
                lag_pair = [lag_pair[m] + g * lag[m] for m in range(half)]
                return state, lag, pair, lag_pair, skip + g * u

            state = [lead_ref[tile, strided(m, modes)] for m in group]
            lag = [lead_ref[tile, strided(SUBS * modes + m, modes)] for m in group]
            zero = [zero_ref[...]] * half
            state, lag, pair, lag_pair, skip = lax.fori_loop(
                0, span, pair_step, (state, lag, zero, zero, zero[0]), unroll=4
            )
            for m in range(half):
                part_ref[tile, strided(low + m, modes)] = pair[m]
                part_ref[tile, strided(SUBS * modes + low + m, modes)] = lag_pair[m]
        total = jnp.sum(skip, axis=0, keepdims=True)
        sums_ref[pl.ds(3 * modes, SUBS), lanes] = jnp.broadcast_to(total, (SUBS, LANES))
        power = jnp.exp(-span * jnp.exp(log_ref[:, lanes]))
        start = jnp.zeros_like(power)
        pair = jnp.zeros_like(power)
        lag_pair = jnp.zeros_like(power)
        for j in range(SUBS - 1, -1, -1):
            start = power * start + sub_ref[tile, pl.ds(j * modes, modes)]
            pair = pair + part_ref[tile, pl.ds(j * modes, modes)]
            lag_pair = lag_pair + part_ref[tile, pl.ds((SUBS + j) * modes, modes)]
        sums_ref[pl.ds(0, modes), lanes] = start
        sums_ref[pl.ds(modes, modes), lanes] = pair
        sums_ref[pl.ds(2 * modes, modes), lanes] = lag_pair


def backward_full(*refs, scale):
    (key_ref, value_ref, back_ref, sub_ref, log_ref, residue_ref, skip_ref, *sum_refs) = refs[:-9]
    (grad_key_ref, grad_value_ref, grad_residue_ref, grad_decay_ref, grad_skip_ref) = refs[-9:-4]
    (decay_ref, gain_ref, lead_ref, drive_grad_ref) = refs[-4:]
    length, channels = key_ref.shape
    modes = log_ref.shape[0]
    span = length // SUBS
    rate = jnp.exp(log_ref[...])
    norm = jnp.sqrt(2.0 * rate)
    gain = residue_ref[...] * norm
    decay_ref[...] = jnp.exp(-rate)
    gain_ref[...] = gain
    pair = tree_sum([ref[pl.ds(2 * modes, modes)] for ref in sum_refs])
    lag_pair = tree_sum([ref[pl.ds(3 * modes, modes)] for ref in sum_refs])
    grad_residue_ref[...] = norm * pair * scale
    grad_decay_ref[...] = gain * (0.5 * pair - rate * lag_pair) * scale
    grad_skip_ref[...] = tree_sum([ref[pl.ds(4 * modes, SUBS)] for ref in sum_refs]) * scale
    for tile, lanes in lane_tiles(channels):
        rate = jnp.exp(log_ref[:, lanes])
        stretch = jnp.exp(-length * rate)
        power = jnp.exp(-span * rate)
        start = jnp.zeros_like(rate)
        for distance in range(2 * RING - 1, 0, -1):
            start = stretch * start + nearby(sum_refs, distance, -1, 0, modes, lanes)
        for j in range(SUBS - 1, -1, -1):
            lead_ref[tile, pl.ds(j * modes, modes)] = start
            start = power * start + sub_ref[tile, pl.ds(j * modes, modes)]
        decay = [spread(decay_ref, m, lanes) for m in range(modes)]
        gain = [spread(gain_ref, m, lanes) for m in range(modes)]
        skip = spread(skip_ref, 0, lanes)

        def step(i, now):
            place = strided(span - 1 - i, span)
            g = back_ref[tile, place]
            now = [decay[m] * now[m] + g for m in range(modes)]
            drive_grad_ref[tile, place] = tree_sum([gain[m] * now[m] for m in range(modes)]) + skip * g
            return now

        first = [lead_ref[tile, strided(m, modes)] for m in range(modes)]
        lax.fori_loop(0, span, step, first, unroll=4)
        drive_grad = drive_grad_ref[tile]
        grad_key_ref[:, lanes] = (drive_grad * value_ref[:, lanes].astype(F32)).astype(BF16)
        grad_value_ref[:, lanes] = (drive_grad * key_ref[:, lanes].astype(F32)).astype(BF16)


def call(body, args, outs, scratch, micros, name):
    whole = pl.BlockSpec(memory_space=pltpu.VMEM)
    return pl.pallas_call(
        body,
        out_shape=[jax.ShapeDtypeStruct(o.shape, o.dtype) for o in outs],
        in_specs=[whole] * len(args),
        out_specs=[whole] * len(outs),
        scratch_shapes=[pltpu.VMEM(shape, F32) for shape in scratch],
        compiler_params=pltpu.CompilerParams(vmem_limit_bytes=32 * 2**20),
        cost_estimate=pl.CostEstimate(flops=int(micros * 1.15e9), bytes_accessed=0, transcendentals=0),
        name=name,
    )(*args)


def like(shape, dtype):
    return jax.ShapeDtypeStruct(shape, dtype)


def spread_over_x(value):
    return [value] + [hop(value, x=offset) for offset in range(1, RING)]


def together(*values):
    return lax.optimization_barrier(values)


def local(queries, key_proj, value_proj, skip_gain, residue, log_decay, out_weight, cotangent):
    length, channels = queries.shape
    modes = residue.shape[0]
    blocks = lax.axis_size("seq")
    scale = 1.0 / math.sqrt(length * blocks)
    skip_row = skip_gain.reshape(1, channels)
    tiles = channels // LANES
    wide = like((tiles, length, LANES), F32)
    narrow = like((length, channels), BF16)
    table = (modes, channels)

    block, log_first = together(gather_z(cotangent), log_decay)
    main_block, other_block = hop(block, y=MAIN), hop(block, y=OTHER)
    ends, subs, driving = call(
        forward_ends,
        (key_proj, value_proj, log_first),
        (like((2 * modes, channels), F32), like((tiles, 2 * SUBS * modes, LANES), F32), wide),
        [table, (SUBS, LANES)],
        0.1,
        "forward_ends",
    )
    ends_pair = jnp.concatenate([ends, hop(ends, pair=1)])
    earlier = spread_over_x(ends_pair)
    gated, turned, pre_gate, lead = call(
        forward_full,
        (queries, driving, subs, log_decay, residue, skip_row, *earlier),
        (narrow, narrow, wide, like((tiles, 2 * SUBS * modes, LANES), F32)),
        [table, table],
        0.1,
        "forward_full",
    )
    main_block, other_block, turned = together(main_block, other_block, turned)
    far_block = hop(main_block, y=MAIN)
    near_first, near_rest, far_first, far_rest = project(turned, out_weight)
    far_block, far_first, gated_other = together(far_block, far_first, hop(gated, pair=1))
    got_first, got_rest = hop(far_first, core=1), hop(far_rest, core=1)
    gated_pair = jnp.concatenate([gated, gated_other])
    opposite = add(near_first, got_first).astype(BF16)
    cot_rows = place_blocks(block, main_block, other_block, far_block)
    cot_rows, got_rest = together(cot_rows.reshape(2 * length, -1), got_rest)

    _, _, core, low, x = places()
    half = out_weight.shape[1] // 2
    low_weight = lax.dynamic_slice(out_weight, (0, low * half), (channels, half))
    grad_parts = lax.dot_general(cot_rows, low_weight, (((1,), (1,)), ((), ())), preferred_element_type=F32)
    cot_rows, grad_parts = together(cot_rows, grad_parts)
    theirs = hop(grad_parts[length:].astype(BF16), pair=1)

    far_weight = weigh(gated_pair, cot_rows, scale, lax.rem(x + 2, RING))
    cot_rows, far_weight, got_rest = together(cot_rows, far_weight, got_rest)
    main_weight, other_weight, own_weight = (
        weigh(gated_pair, cot_rows, scale, lax.rem(x + r, RING)) for r in (1 + 2 * core, 3 - 2 * core, 0)
    )
    main_weight = add(main_weight, hop(far_weight, x=MAIN)).astype(BF16)

    main, other, own = (add(a, b) for a, b in zip(jnp.split(near_rest, 3), jnp.split(got_rest, 3)))
    main = add(main, hop(opposite, y=MAIN)).astype(BF16)
    other = other.astype(BF16)

    theirs, main_weight, other_weight, main, other = together(theirs, main_weight, other_weight, main, other)
    grad_gated = add(grad_parts[:length], theirs)
    main, other = hop(main, y=MAIN), hop(other, y=OTHER)
    main_weight, other_weight = hop(main_weight, x=MAIN), hop(other_weight, x=OTHER)

    grad_query, back, sums, back_subs = call(
        backward_ends,
        (grad_gated, queries, pre_gate, driving, lead, log_decay),
        (narrow, wide, like((3 * modes + SUBS, channels), F32), like((tiles, SUBS * modes, LANES), F32)),
        [table, (tiles, 2 * SUBS * modes, LANES), (SUBS, LANES)],
        2.0,
        "backward_ends",
    )
    others = hop(sums, pair=1)
    others, main, other, main_weight, other_weight = together(others, main, other, main_weight, other_weight)
    own = add(own, main, other)
    part = own.shape[0] // 2
    leaving = hop(own[part:].astype(BF16), z=(2, -1))
    sums_pair = jnp.concatenate([sums[:modes], others[:modes], sums[modes:] + others[modes:]])
    all_sums = spread_over_x(sums_pair)
    leaving, *_ = together(leaving, *all_sums[1:])
    mixed = add(own[:part], by_core(leaving, hop(leaving, z=(None, -1)))).astype(BF16)
    grad_weight = add(own_weight, main_weight, other_weight).astype(BF16)
    grad_key, grad_value, grad_residue, grad_decay, grad_skip = call(
        functools.partial(backward_full, scale=scale),
        (key_proj, value_proj, back, back_subs, log_decay, residue, skip_row, *all_sums),
        (narrow, narrow, like(table, F32), like(table, F32), like((SUBS, channels), F32)),
        [table, table, (tiles, SUBS * modes, LANES), (tiles, length, LANES)],
        0.1,
        "backward_full",
    )
    return (
        mixed,
        grad_query,
        grad_key,
        grad_value,
        grad_weight,
        grad_residue,
        grad_decay,
        grad_skip[0],
    )


def solution(mesh):
    in_specs = (
        P("seq", "chan"),
        P("seq", "chan"),
        P("seq", "chan"),
        P("chan"),
        P(None, "chan"),
        P(None, "chan"),
        P("chan", None),
        P(("seq", "chan"), None),
    )
    out_specs = (
        P(("seq", "chan"), None),
        P("seq", "chan"),
        P("seq", "chan"),
        P("seq", "chan"),
        P("chan", "seq"),
        P(None, "chan"),
        P(None, "chan"),
        P("chan"),
    )
    return jax.shard_map(local, mesh=mesh, in_specs=in_specs, out_specs=out_specs, check_vma=False)
```

```python
import functools
import itertools
import math

import jax
import jax.numpy as jnp
from jax import lax
from jax.experimental import pallas as pl
from jax.experimental.pallas import tpu as pltpu
from jax.sharding import PartitionSpec as P

RING = 4
MAIN, OTHER = (1, -1), (-1, 1)
SUBS = 8
LANES = 128
F32 = jnp.float32
BF16 = jnp.bfloat16


def strided(first, step):
    return pl.ds(first, SUBS, stride=step)


def spread(ref, mode, lanes):
    return jnp.broadcast_to(ref[pl.ds(mode, 1), lanes], (SUBS, LANES))


def tree_sum(parts):
    while len(parts) > 1:
        parts = [a + b for a, b in zip(parts[::2], parts[1::2])] + parts[len(parts) & ~1 :]
    return parts[0]


def lane_tiles(channels):
    return [(tile, pl.ds(tile * LANES, LANES)) for tile in range(channels // LANES)]


def places():
    chan, seq = lax.axis_index("chan"), lax.axis_index("seq")
    return chan // 4, lax.rem(chan // 2, 2), lax.rem(chan, 2), seq // RING, lax.rem(seq, RING)


def hop(value, x=0, y=0, z=0, core=0, pair=0):
    moves = []
    for i, j, k, c in itertools.product(range(RING), range(RING), range(RING), range(2)):
        dx, dy, dz = (step[c] if isinstance(step, tuple) else step for step in (x, y, z))
        if None in (dx, dy, dz):
            continue
        there = ((i + dx) % RING, (j + dy) % RING, ((k + dz) % RING) ^ pair, c ^ core)
        moves.append(tuple(((b * 2 + d // 2) * 2 + e) * 2 * RING + d % 2 * RING + a for a, b, d, e in ((i, j, k, c), there)))
    return lax.ppermute(value, ("chan", "seq"), moves)


def by_core(first, second):
    return jnp.where(places()[2] == 0, first, second)


def gather_z(cotangent):
    _, high, _, low, _ = places()
    tokens, width = cotangent.shape
    half = width // 2
    mine = lax.dynamic_slice(cotangent, (0, low * half), (tokens, half))
    theirs = lax.dynamic_slice(cotangent, (0, (1 - low) * half), (tokens, half))
    above, below, across = hop(theirs, z=1), hop(theirs, z=-1), hop(mine, z=2)
    stack = jnp.where(high == 0, jnp.stack([mine, across]), jnp.stack([across, mine]))
    same, differ = jnp.where(low == 1, above, below), jnp.where(low == 1, below, above)
    other = jnp.where(high == 0, jnp.stack([same, differ]), jnp.stack([differ, same]))
    return jnp.stack([stack, other])


def place_blocks(*blocks):
    y, _, core, _, _ = places()
    _, _, tokens, half = blocks[0].shape
    whole = jnp.zeros((2, RING, 2, 2, tokens, half), BF16)
    for block, steps in zip(blocks, ((0, 0), (RING - 1, 1), (1, RING - 1), (2, 2))):
        for part, at_core in ((block, core), (hop(block, core=1), 1 - core)):
            row = lax.rem(y + jnp.where(at_core == 0, *steps), RING)
            whole = lax.dynamic_update_slice(whole, part[:, None, :, None], (0, row, 0, at_core, 0, 0))
    return whole


def add(*parts):
    return functools.reduce(jnp.add, [part.astype(F32) for part in parts])


def project_tile(rows_ref, weight_ref, *out_refs):
    product = jnp.dot(rows_ref[...], weight_ref[...], preferred_element_type=F32).astype(BF16)
    first = 0
    for ref in out_refs:
        ref[...] = product[first : first + ref.shape[0]]
        first += ref.shape[0]


def project(turned, out_weight):
    rows, depth = turned.shape
    width = out_weight.shape[1]
    tile = 1024
    sizes = [rows // 8, 3 * rows // 8] * 2
    return pl.pallas_call(
        project_tile,
        grid=(width // tile,),
        out_shape=[jax.ShapeDtypeStruct((size, width), BF16) for size in sizes],
        in_specs=[pl.BlockSpec((rows, depth), lambda i: (0, 0)), pl.BlockSpec((depth, tile), lambda i: (0, i))],
        out_specs=[pl.BlockSpec((size, tile), lambda i: (0, i)) for size in sizes],
        compiler_params=pltpu.CompilerParams(vmem_limit_bytes=12 * 2**20),
        cost_estimate=pl.CostEstimate(
            flops=2 * rows * depth * width, bytes_accessed=2 * width * (rows + depth), transcendentals=0
        ),
        name="project",
    )(turned, out_weight)


def weigh(gated, cot_rows, scale, block):
    width = cot_rows.shape[1] // RING
    columns = lax.dynamic_slice(cot_rows, (0, block * width), (cot_rows.shape[0], width))
    product = lax.dot_general(gated, columns, (((0,), (0,)), ((), ())), preferred_element_type=F32)
    return (product * scale).astype(BF16)


def nearby(refs, distance, way, first, modes, lanes):
    _, _, _, low, x = places()
    before = x if way == 1 else RING - 1 - x
    other_counts = low == (way + 1) // 2
    other = refs[0].shape[0] // 2 if way == 1 else modes
    step = distance % RING
    ref = refs[way * step % RING]
    mine = ref[pl.ds(first, modes), lanes]
    theirs = jnp.where(other_counts, ref[pl.ds(other + first, modes), lanes], 0.0)
    if distance < RING:
        return jnp.where(step <= before, mine, theirs)
    return jnp.where(step <= before, theirs, 0.0)


def forward_ends(key_ref, value_ref, log_ref, ends_ref, sub_ref, drive_ref, decay_ref, zero_ref):
    length, channels = key_ref.shape
    modes = log_ref.shape[0]
    span = length // SUBS
    decay_ref[...] = jnp.exp(-jnp.exp(log_ref[...]))
    zero_ref[...] = jnp.zeros_like(zero_ref)
    for tile, lanes in lane_tiles(channels):
        drive_ref[tile] = key_ref[:, lanes].astype(F32) * value_ref[:, lanes].astype(F32)
        decay = [spread(decay_ref, m, lanes) for m in range(modes)]

        def step(i, carry):
            now, lag = carry
            u = drive_ref[tile, strided(i, span)]
            lag = [decay[m] * (lag[m] + now[m]) for m in range(modes)]
            now = [decay[m] * now[m] + u for m in range(modes)]
            return now, lag

        zero = [zero_ref[...]] * modes
        now, lag = lax.fori_loop(0, span, step, (zero, zero), unroll=4)
        for m in range(modes):
            sub_ref[tile, strided(m, modes)] = now[m]
            sub_ref[tile, strided(SUBS * modes + m, modes)] = lag[m]
        power = jnp.exp(-span * jnp.exp(log_ref[:, lanes]))
        state = jnp.zeros_like(power)
        lagged = jnp.zeros_like(power)
        for j in range(SUBS):
            lagged = power * (lagged + span * state) + sub_ref[tile, pl.ds((SUBS + j) * modes, modes)]
            state = power * state + sub_ref[tile, pl.ds(j * modes, modes)]
        ends_ref[pl.ds(0, modes), lanes] = state
        ends_ref[pl.ds(modes, modes), lanes] = lagged


def forward_full(*refs):
    (query_ref, drive_ref, sub_ref, log_ref, residue_ref, skip_ref, *end_refs) = refs[:-6]
    (gated_ref, turned_ref, pre_ref, lead_ref, decay_ref, gain_ref) = refs[-6:]
    length, channels = query_ref.shape
    modes = log_ref.shape[0]
    span = length // SUBS
    rate = jnp.exp(log_ref[...])
    decay_ref[...] = jnp.exp(-rate)
    gain_ref[...] = residue_ref[...] * jnp.sqrt(2.0 * rate)
    for tile, lanes in lane_tiles(channels):
        rate = jnp.exp(log_ref[:, lanes])
        stretch = jnp.exp(-length * rate)
        power = jnp.exp(-span * rate)
        state = jnp.zeros_like(rate)
        lagged = jnp.zeros_like(rate)
        for distance in range(2 * RING - 1, 0, -1):
            lagged = stretch * (lagged + length * state) + nearby(end_refs, distance, 1, modes, modes, lanes)
            state = stretch * state + nearby(end_refs, distance, 1, 0, modes, lanes)
        for j in range(SUBS):
            now_rows, lag_rows = (pl.ds((j + k) * modes, modes) for k in (0, SUBS))
            lead_ref[tile, now_rows] = state
            lead_ref[tile, lag_rows] = lagged
            lagged = power * (lagged + span * state) + sub_ref[tile, lag_rows]
            state = power * state + sub_ref[tile, now_rows]
        decay = [spread(decay_ref, m, lanes) for m in range(modes)]
        gain = [spread(gain_ref, m, lanes) for m in range(modes)]
        skip = spread(skip_ref, 0, lanes)

        def step(i, now):
            place = strided(i, span)
            u = drive_ref[tile, place]
            now = [decay[m] * now[m] + u for m in range(modes)]
            pre_ref[tile, place] = tree_sum([gain[m] * now[m] for m in range(modes)]) + skip * u
            return now

        first = [lead_ref[tile, strided(m, modes)] for m in range(modes)]
        lax.fori_loop(0, span, step, first, unroll=4)
        gated_ref[:, lanes] = (query_ref[:, lanes].astype(F32) * pre_ref[tile]).astype(BF16)
    part = length // (RING * 4)
    y, high, core, _, _ = places()
    for i in range(RING * 4):
        on = lax.rem(i // 4 + RING - y, RING)
        kept = lax.rem(i % 2 + core, 2) == 0
        first = jnp.where(kept, 1 + 2 * core, 3 - 2 * core)
        there = jnp.where(on == 0, 3, jnp.where(on == 2, 0, jnp.where(on == first, 1, 2)))
        there = there + jnp.where(kept, 0, RING)
        there = there * 2 + lax.rem(i // 2 % 2 + high, 2)
        turned_ref[pl.ds(pl.multiple_of(there * part, part), part)] = gated_ref[pl.ds(i * part, part)]


def backward_ends(
    grad_ref, query_ref, pre_ref, drive_ref, lead_ref, log_ref,
    grad_query_ref, back_ref, sums_ref, sub_ref, decay_ref, part_ref, zero_ref,
):
    length, channels = query_ref.shape
    modes = log_ref.shape[0]
    span = length // SUBS
    half = modes // 2
    decay_ref[...] = jnp.exp(-jnp.exp(log_ref[...]))
    zero_ref[...] = jnp.zeros_like(zero_ref)
    for tile, lanes in lane_tiles(channels):
        grad = grad_ref[:, lanes].astype(F32)
        grad_query_ref[:, lanes] = (grad * pre_ref[tile]).astype(BF16)
        back_ref[tile] = grad * query_ref[:, lanes].astype(F32)
        decay = [spread(decay_ref, m, lanes) for m in range(modes)]

        def back_step(i, now):
            g = back_ref[tile, strided(span - 1 - i, span)]
            return [decay[m] * now[m] + g for m in range(modes)]

        zero = [zero_ref[...]] * modes
        now = lax.fori_loop(0, span, back_step, zero, unroll=4)
        for m in range(modes):
            sub_ref[tile, strided(m, modes)] = now[m]
        for low in range(0, modes, half):
            group = range(low, low + half)
            decay = [spread(decay_ref, m, lanes) for m in group]

            def pair_step(i, carry):
                state, lag, pair, lag_pair, skip = carry
                place = strided(i, span)
                u = drive_ref[tile, place]
                g = back_ref[tile, place]
                lag = [decay[m] * (lag[m] + state[m]) for m in range(half)]
                state = [decay[m] * state[m] + u for m in range(half)]
                pair = [pair[m] + g * state[m] for m in range(half)]
                lag_pair = [lag_pair[m] + g * lag[m] for m in range(half)]
                return state, lag, pair, lag_pair, skip + g * u

            state = [lead_ref[tile, strided(m, modes)] for m in group]
            lag = [lead_ref[tile, strided(SUBS * modes + m, modes)] for m in group]
            zero = [zero_ref[...]] * half
            state, lag, pair, lag_pair, skip = lax.fori_loop(
                0, span, pair_step, (state, lag, zero, zero, zero[0]), unroll=4
            )
            for m in range(half):
                part_ref[tile, strided(low + m, modes)] = pair[m]
                part_ref[tile, strided(SUBS * modes + low + m, modes)] = lag_pair[m]
        total = jnp.sum(skip, axis=0, keepdims=True)
        sums_ref[pl.ds(3 * modes, SUBS), lanes] = jnp.broadcast_to(total, (SUBS, LANES))
        power = jnp.exp(-span * jnp.exp(log_ref[:, lanes]))
        start = jnp.zeros_like(power)
        pair = jnp.zeros_like(power)
        lag_pair = jnp.zeros_like(power)
        for j in range(SUBS - 1, -1, -1):
            start = power * start + sub_ref[tile, pl.ds(j * modes, modes)]
            pair = pair + part_ref[tile, pl.ds(j * modes, modes)]
            lag_pair = lag_pair + part_ref[tile, pl.ds((SUBS + j) * modes, modes)]
        sums_ref[pl.ds(0, modes), lanes] = start
        sums_ref[pl.ds(modes, modes), lanes] = pair
        sums_ref[pl.ds(2 * modes, modes), lanes] = lag_pair


def backward_full(*refs, scale):
    (key_ref, value_ref, back_ref, sub_ref, log_ref, residue_ref, skip_ref, *sum_refs) = refs[:-9]
    (grad_key_ref, grad_value_ref, grad_residue_ref, grad_decay_ref, grad_skip_ref) = refs[-9:-4]
    (decay_ref, gain_ref, lead_ref, drive_grad_ref) = refs[-4:]
    length, channels = key_ref.shape
    modes = log_ref.shape[0]
    span = length // SUBS
    rate = jnp.exp(log_ref[...])
    norm = jnp.sqrt(2.0 * rate)
    gain = residue_ref[...] * norm
    decay_ref[...] = jnp.exp(-rate)
    gain_ref[...] = gain
    pair = tree_sum([ref[pl.ds(2 * modes, modes)] for ref in sum_refs])
    lag_pair = tree_sum([ref[pl.ds(3 * modes, modes)] for ref in sum_refs])
    grad_residue_ref[...] = norm * pair * scale
    grad_decay_ref[...] = gain * (0.5 * pair - rate * lag_pair) * scale
    grad_skip_ref[...] = tree_sum([ref[pl.ds(4 * modes, SUBS)] for ref in sum_refs]) * scale
    for tile, lanes in lane_tiles(channels):
        rate = jnp.exp(log_ref[:, lanes])
        stretch = jnp.exp(-length * rate)
        power = jnp.exp(-span * rate)
        start = jnp.zeros_like(rate)
        for distance in range(2 * RING - 1, 0, -1):
            start = stretch * start + nearby(sum_refs, distance, -1, 0, modes, lanes)
        for j in range(SUBS - 1, -1, -1):
            lead_ref[tile, pl.ds(j * modes, modes)] = start
            start = power * start + sub_ref[tile, pl.ds(j * modes, modes)]
        decay = [spread(decay_ref, m, lanes) for m in range(modes)]
        gain = [spread(gain_ref, m, lanes) for m in range(modes)]
        skip = spread(skip_ref, 0, lanes)

        def step(i, now):
            place = strided(span - 1 - i, span)
            g = back_ref[tile, place]
            now = [decay[m] * now[m] + g for m in range(modes)]
            drive_grad_ref[tile, place] = tree_sum([gain[m] * now[m] for m in range(modes)]) + skip * g
            return now

        first = [lead_ref[tile, strided(m, modes)] for m in range(modes)]
        lax.fori_loop(0, span, step, first, unroll=4)
        drive_grad = drive_grad_ref[tile]
        grad_key_ref[:, lanes] = (drive_grad * value_ref[:, lanes].astype(F32)).astype(BF16)
        grad_value_ref[:, lanes] = (drive_grad * key_ref[:, lanes].astype(F32)).astype(BF16)


def call(body, args, outs, scratch, micros, name):
    whole = pl.BlockSpec(memory_space=pltpu.VMEM)
    return pl.pallas_call(
        body,
        out_shape=[jax.ShapeDtypeStruct(o.shape, o.dtype) for o in outs],
        in_specs=[whole] * len(args),
        out_specs=[whole] * len(outs),
        scratch_shapes=[pltpu.VMEM(shape, F32) for shape in scratch],
        compiler_params=pltpu.CompilerParams(vmem_limit_bytes=6 * 2**20),
        cost_estimate=pl.CostEstimate(flops=int(micros * 1.15e9), bytes_accessed=0, transcendentals=0),
        name=name,
    )(*args)


def like(shape, dtype):
    return jax.ShapeDtypeStruct(shape, dtype)


def spread_over_x(value):
    return [value] + [hop(value, x=offset) for offset in range(1, RING)]


def together(*values):
    return lax.optimization_barrier(values)


def local(queries, key_proj, value_proj, skip_gain, residue, log_decay, out_weight, cotangent):
    length, channels = queries.shape
    modes = residue.shape[0]
    blocks = lax.axis_size("seq")
    scale = 1.0 / math.sqrt(length * blocks)
    skip_row = skip_gain.reshape(1, channels)
    tiles = channels // LANES
    wide = like((tiles, length, LANES), F32)
    narrow = like((length, channels), BF16)
    table = (modes, channels)

    block = gather_z(cotangent)
    ends, subs, driving = call(
        forward_ends,
        (key_proj, value_proj, log_decay),
        (like((2 * modes, channels), F32), like((tiles, 2 * SUBS * modes, LANES), F32), wide),
        [table, (SUBS, LANES)],
        0.1,
        "forward_ends",
    )
    ends_pair = jnp.concatenate([ends, hop(ends, pair=1)])
    block, *earlier = together(block, *spread_over_x(ends_pair))
    main_block, other_block = hop(block, y=MAIN), hop(block, y=OTHER)
    gated, turned, pre_gate, lead = call(
        forward_full,
        (queries, driving, subs, log_decay, residue, skip_row, *earlier),
        (narrow, narrow, wide, like((tiles, 2 * SUBS * modes, LANES), F32)),
        [table, table],
        0.1,
        "forward_full",
    )
    main_block, other_block, turned = together(main_block, other_block, turned)
    far_block = hop(main_block, y=MAIN)
    near_first, near_rest, far_first, far_rest = project(turned, out_weight)
    far_block, far_first, gated_other = together(far_block, far_first, hop(gated, pair=1))
    got_first, got_rest = hop(far_first, core=1), hop(far_rest, core=1)
    gated_pair = jnp.concatenate([gated, gated_other])
    opposite = add(near_first, got_first).astype(BF16)
    cot_rows = place_blocks(block, main_block, other_block, far_block)
    cot_rows, got_rest = together(cot_rows.reshape(2 * length, -1), got_rest)

    _, _, core, low, x = places()
    half = out_weight.shape[1] // 2
    low_weight = lax.dynamic_slice(out_weight, (0, low * half), (channels, half))
    grad_parts = lax.dot_general(cot_rows, low_weight, (((1,), (1,)), ((), ())), preferred_element_type=F32)
    cot_rows, grad_parts = together(cot_rows, grad_parts)
    theirs = hop(grad_parts[length:].astype(BF16), pair=1)

    far_weight = weigh(gated_pair, cot_rows, scale, lax.rem(x + 2, RING))
    cot_rows, far_weight, got_rest = together(cot_rows, far_weight, got_rest)
    main_weight, other_weight, own_weight = (
        weigh(gated_pair, cot_rows, scale, lax.rem(x + r, RING)) for r in (1 + 2 * core, 3 - 2 * core, 0)
    )
    main, other, own = (add(a, b) for a, b in zip(jnp.split(near_rest, 3), jnp.split(got_rest, 3)))
    main = add(main, hop(opposite, y=MAIN)).astype(BF16)
    main, other, main_weight, other_weight, own_weight = together(
        main, other.astype(BF16), main_weight, other_weight, own_weight
    )
    main, other = hop(main, y=MAIN), hop(other, y=OTHER)
    other_weight = hop(other_weight, x=OTHER)
    main_weight = add(main_weight, hop(far_weight, x=MAIN)).astype(BF16)

    theirs, main_weight = together(theirs, main_weight)
    grad_gated = add(grad_parts[:length], theirs)
    main_weight = hop(main_weight, x=MAIN)

    grad_query, back, sums, back_subs = call(
        backward_ends,
        (grad_gated, queries, pre_gate, driving, lead, log_decay),
        (narrow, wide, like((3 * modes + SUBS, channels), F32), like((tiles, SUBS * modes, LANES), F32)),
        [table, (tiles, 2 * SUBS * modes, LANES), (SUBS, LANES)],
        2.0,
        "backward_ends",
    )
    others = hop(sums, pair=1)
    others, main, other, main_weight, other_weight = together(others, main, other, main_weight, other_weight)
    own = add(own, main, other)
    part = own.shape[0] // 2
    leaving = hop(own[part:].astype(BF16), z=(2, -1))
    sums_pair = jnp.concatenate([sums[:modes], others[:modes], sums[modes:] + others[modes:]])
    all_sums = spread_over_x(sums_pair)
    leaving, *_ = together(leaving, *all_sums[1:])
    mixed = add(own[:part], by_core(leaving, hop(leaving, z=(None, -1)))).astype(BF16)
    grad_weight = add(own_weight, main_weight, other_weight).astype(BF16)
    grad_key, grad_value, grad_residue, grad_decay, grad_skip = call(
        functools.partial(backward_full, scale=scale),
        (key_proj, value_proj, back, back_subs, log_decay, residue, skip_row, *all_sums),
        (narrow, narrow, like(table, F32), like(table, F32), like((SUBS, channels), F32)),
        [table, table, (tiles, SUBS * modes, LANES), (tiles, length, LANES)],
        0.1,
        "backward_full",
    )
    return (
        mixed,
        grad_query,
        grad_key,
        grad_value,
        grad_weight,
        grad_residue,
        grad_decay,
        grad_skip[0],
    )


def solution(mesh):
    in_specs = (
        P("seq", "chan"),
        P("seq", "chan"),
        P("seq", "chan"),
        P("chan"),
        P(None, "chan"),
        P(None, "chan"),
        P("chan", None),
        P(("seq", "chan"), None),
    )
    out_specs = (
        P(("seq", "chan"), None),
        P("seq", "chan"),
        P("seq", "chan"),
        P("seq", "chan"),
        P("chan", "seq"),
        P(None, "chan"),
        P(None, "chan"),
        P("chan"),
    )
    return jax.shard_map(local, mesh=mesh, in_specs=in_specs, out_specs=out_specs, check_vma=False)
```

```python
import functools
import itertools
import math

import jax
import jax.numpy as jnp
from jax import lax
from jax.experimental import pallas as pl
from jax.experimental.pallas import tpu as pltpu
from jax.sharding import PartitionSpec as P

RING = 4
MAIN, OTHER = (1, -1), (-1, 1)
SUBS = 8
LANES = 128
F32 = jnp.float32
BF16 = jnp.bfloat16


def strided(first, step):
    return pl.ds(first, SUBS, stride=step)


def spread(ref, mode, lanes):
    return jnp.broadcast_to(ref[pl.ds(mode, 1), lanes], (SUBS, LANES))


def tree_sum(parts):
    while len(parts) > 1:
        parts = [a + b for a, b in zip(parts[::2], parts[1::2])] + parts[len(parts) & ~1 :]
    return parts[0]


def lane_tiles(channels):
    return [(tile, pl.ds(tile * LANES, LANES)) for tile in range(channels // LANES)]


def places():
    chan, seq = lax.axis_index("chan"), lax.axis_index("seq")
    return chan // 4, lax.rem(chan // 2, 2), lax.rem(chan, 2), seq // RING, lax.rem(seq, RING)


def hop(value, x=0, y=0, z=0, core=0, pair=0):
    moves = []
    for i, j, k, c in itertools.product(range(RING), range(RING), range(RING), range(2)):
        dx, dy, dz = (step[c] if isinstance(step, tuple) else step for step in (x, y, z))
        if None in (dx, dy, dz):
            continue
        there = ((i + dx) % RING, (j + dy) % RING, ((k + dz) % RING) ^ pair, c ^ core)
        moves.append(tuple(((b * 2 + d // 2) * 2 + e) * 2 * RING + d % 2 * RING + a for a, b, d, e in ((i, j, k, c), there)))
    return lax.ppermute(value, ("chan", "seq"), moves)


def by_core(first, second):
    return jnp.where(places()[2] == 0, first, second)


def gather_z(cotangent):
    _, high, _, low, _ = places()
    tokens, width = cotangent.shape
    half = width // 2
    mine = lax.dynamic_slice(cotangent, (0, low * half), (tokens, half))
    theirs = lax.dynamic_slice(cotangent, (0, (1 - low) * half), (tokens, half))
    above, below, across = hop(theirs, z=1), hop(theirs, z=-1), hop(mine, z=2)
    stack = jnp.where(high == 0, jnp.stack([mine, across]), jnp.stack([across, mine]))
    same, differ = jnp.where(low == 1, above, below), jnp.where(low == 1, below, above)
    other = jnp.where(high == 0, jnp.stack([same, differ]), jnp.stack([differ, same]))
    return jnp.stack([stack, other])


def place_blocks(*blocks):
    y, _, core, _, _ = places()
    _, _, tokens, half = blocks[0].shape
    whole = jnp.zeros((2, RING, 2, 2, tokens, half), BF16)
    for block, steps in zip(blocks, ((0, 0), (RING - 1, 1), (1, RING - 1), (2, 2))):
        for part, at_core in ((block, core), (hop(block, core=1), 1 - core)):
            row = lax.rem(y + jnp.where(at_core == 0, *steps), RING)
            whole = lax.dynamic_update_slice(whole, part[:, None, :, None], (0, row, 0, at_core, 0, 0))
    return whole


def add(*parts):
    return functools.reduce(jnp.add, [part.astype(F32) for part in parts])


def project_tile(rows_ref, weight_ref, *out_refs):
    product = jnp.dot(rows_ref[...], weight_ref[...], preferred_element_type=F32).astype(BF16)
    first = 0
    for ref in out_refs:
        ref[...] = product[first : first + ref.shape[0]]
        first += ref.shape[0]


def project(turned, out_weight):
    rows, depth = turned.shape
    width = out_weight.shape[1]
    tile = 1024
    sizes = [rows // 8, 3 * rows // 8] * 2
    return pl.pallas_call(
        project_tile,
        grid=(width // tile,),
        out_shape=[jax.ShapeDtypeStruct((size, width), BF16) for size in sizes],
        in_specs=[pl.BlockSpec((rows, depth), lambda i: (0, 0)), pl.BlockSpec((depth, tile), lambda i: (0, i))],
        out_specs=[pl.BlockSpec((size, tile), lambda i: (0, i)) for size in sizes],
        compiler_params=pltpu.CompilerParams(vmem_limit_bytes=12 * 2**20),
        cost_estimate=pl.CostEstimate(
            flops=2 * rows * depth * width, bytes_accessed=2 * width * (rows + depth), transcendentals=0
        ),
        name="project",
    )(turned, out_weight)


def weigh(gated, cot_rows, scale, block):
    width = cot_rows.shape[1] // RING
    columns = lax.dynamic_slice(cot_rows, (0, block * width), (cot_rows.shape[0], width))
    product = lax.dot_general(gated, columns, (((0,), (0,)), ((), ())), preferred_element_type=F32)
    return (product * scale).astype(BF16)


def nearby(refs, distance, way, first, modes, lanes):
    _, _, _, low, x = places()
    before = x if way == 1 else RING - 1 - x
    other_counts = low == (way + 1) // 2
    other = refs[0].shape[0] // 2 if way == 1 else modes
    step = distance % RING
    ref = refs[way * step % RING]
    mine = ref[pl.ds(first, modes), lanes]
    theirs = jnp.where(other_counts, ref[pl.ds(other + first, modes), lanes], 0.0)
    if distance < RING:
        return jnp.where(step <= before, mine, theirs)
    return jnp.where(step <= before, theirs, 0.0)


def forward_ends(key_ref, value_ref, log_ref, ends_ref, sub_ref, drive_ref, decay_ref, zero_ref):
    length, channels = key_ref.shape
    modes = log_ref.shape[0]
    span = length // SUBS
    decay_ref[...] = jnp.exp(-jnp.exp(log_ref[...]))
    zero_ref[...] = jnp.zeros_like(zero_ref)
    for tile, lanes in lane_tiles(channels):
        drive_ref[tile] = key_ref[:, lanes].astype(F32) * value_ref[:, lanes].astype(F32)
        decay = [spread(decay_ref, m, lanes) for m in range(modes)]

        def step(i, carry):
            now, lag = carry
            u = drive_ref[tile, strided(i, span)]
            lag = [decay[m] * (lag[m] + now[m]) for m in range(modes)]
            now = [decay[m] * now[m] + u for m in range(modes)]
            return now, lag

        zero = [zero_ref[...]] * modes
        now, lag = lax.fori_loop(0, span, step, (zero, zero), unroll=8)
        for m in range(modes):
            sub_ref[tile, strided(m, modes)] = now[m]
            sub_ref[tile, strided(SUBS * modes + m, modes)] = lag[m]
        power = jnp.exp(-span * jnp.exp(log_ref[:, lanes]))
        state = jnp.zeros_like(power)
        lagged = jnp.zeros_like(power)
        for j in range(SUBS):
            lagged = power * (lagged + span * state) + sub_ref[tile, pl.ds((SUBS + j) * modes, modes)]
            state = power * state + sub_ref[tile, pl.ds(j * modes, modes)]
        ends_ref[pl.ds(0, modes), lanes] = state
        ends_ref[pl.ds(modes, modes), lanes] = lagged


def forward_full(*refs):
    (query_ref, drive_ref, sub_ref, log_ref, residue_ref, skip_ref, *end_refs) = refs[:-6]
    (gated_ref, turned_ref, pre_ref, lead_ref, decay_ref, gain_ref) = refs[-6:]
    length, channels = query_ref.shape
    modes = log_ref.shape[0]
    span = length // SUBS
    rate = jnp.exp(log_ref[...])
    decay_ref[...] = jnp.exp(-rate)
    gain_ref[...] = residue_ref[...] * jnp.sqrt(2.0 * rate)
    for tile, lanes in lane_tiles(channels):
        rate = jnp.exp(log_ref[:, lanes])
        stretch = jnp.exp(-length * rate)
        power = jnp.exp(-span * rate)
        state = jnp.zeros_like(rate)
        lagged = jnp.zeros_like(rate)
        for distance in range(2 * RING - 1, 0, -1):
            lagged = stretch * (lagged + length * state) + nearby(end_refs, distance, 1, modes, modes, lanes)
            state = stretch * state + nearby(end_refs, distance, 1, 0, modes, lanes)
        for j in range(SUBS):
            now_rows, lag_rows = (pl.ds((j + k) * modes, modes) for k in (0, SUBS))
            lead_ref[tile, now_rows] = state
            lead_ref[tile, lag_rows] = lagged
            lagged = power * (lagged + span * state) + sub_ref[tile, lag_rows]
            state = power * state + sub_ref[tile, now_rows]
        decay = [spread(decay_ref, m, lanes) for m in range(modes)]
        gain = [spread(gain_ref, m, lanes) for m in range(modes)]
        skip = spread(skip_ref, 0, lanes)

        def step(i, now):
            place = strided(i, span)
            u = drive_ref[tile, place]
            now = [decay[m] * now[m] + u for m in range(modes)]
            pre_ref[tile, place] = tree_sum([gain[m] * now[m] for m in range(modes)]) + skip * u
            return now

        first = [lead_ref[tile, strided(m, modes)] for m in range(modes)]
        lax.fori_loop(0, span, step, first, unroll=8)
        gated_ref[:, lanes] = (query_ref[:, lanes].astype(F32) * pre_ref[tile]).astype(BF16)
    part = length // (RING * 4)
    y, high, core, _, _ = places()
    for i in range(RING * 4):
        on = lax.rem(i // 4 + RING - y, RING)
        kept = lax.rem(i % 2 + core, 2) == 0
        first = jnp.where(kept, 1 + 2 * core, 3 - 2 * core)
        there = jnp.where(on == 0, 3, jnp.where(on == 2, 0, jnp.where(on == first, 1, 2)))
        there = there + jnp.where(kept, 0, RING)
        there = there * 2 + lax.rem(i // 2 % 2 + high, 2)
        turned_ref[pl.ds(pl.multiple_of(there * part, part), part)] = gated_ref[pl.ds(i * part, part)]


def backward_ends(
    grad_ref, query_ref, pre_ref, drive_ref, lead_ref, log_ref,
    grad_query_ref, back_ref, sums_ref, sub_ref, decay_ref, part_ref, zero_ref,
):
    length, channels = query_ref.shape
    modes = log_ref.shape[0]
    span = length // SUBS
    half = modes // 2
    decay_ref[...] = jnp.exp(-jnp.exp(log_ref[...]))
    zero_ref[...] = jnp.zeros_like(zero_ref)
    for tile, lanes in lane_tiles(channels):
        grad = grad_ref[:, lanes].astype(F32)
        grad_query_ref[:, lanes] = (grad * pre_ref[tile]).astype(BF16)
        back_ref[tile] = grad * query_ref[:, lanes].astype(F32)
        decay = [spread(decay_ref, m, lanes) for m in range(modes)]

        def back_step(i, now):
            g = back_ref[tile, strided(span - 1 - i, span)]
            return [decay[m] * now[m] + g for m in range(modes)]

        zero = [zero_ref[...]] * modes
        now = lax.fori_loop(0, span, back_step, zero, unroll=8)
        for m in range(modes):
            sub_ref[tile, strided(m, modes)] = now[m]
        for low in range(0, modes, half):
            group = range(low, low + half)
            decay = [spread(decay_ref, m, lanes) for m in group]

            def pair_step(i, carry):
                state, lag, pair, lag_pair, skip = carry
                place = strided(i, span)
                u = drive_ref[tile, place]
                g = back_ref[tile, place]
                lag = [decay[m] * (lag[m] + state[m]) for m in range(half)]
                state = [decay[m] * state[m] + u for m in range(half)]
                pair = [pair[m] + g * state[m] for m in range(half)]
                lag_pair = [lag_pair[m] + g * lag[m] for m in range(half)]
                return state, lag, pair, lag_pair, skip + g * u

            state = [lead_ref[tile, strided(m, modes)] for m in group]
            lag = [lead_ref[tile, strided(SUBS * modes + m, modes)] for m in group]
            zero = [zero_ref[...]] * half
            state, lag, pair, lag_pair, skip = lax.fori_loop(
                0, span, pair_step, (state, lag, zero, zero, zero[0]), unroll=8
            )
            for m in range(half):
                part_ref[tile, strided(low + m, modes)] = pair[m]
                part_ref[tile, strided(SUBS * modes + low + m, modes)] = lag_pair[m]
        total = jnp.sum(skip, axis=0, keepdims=True)
        sums_ref[pl.ds(3 * modes, SUBS), lanes] = jnp.broadcast_to(total, (SUBS, LANES))
        power = jnp.exp(-span * jnp.exp(log_ref[:, lanes]))
        start = jnp.zeros_like(power)
        pair = jnp.zeros_like(power)
        lag_pair = jnp.zeros_like(power)
        for j in range(SUBS - 1, -1, -1):
            start = power * start + sub_ref[tile, pl.ds(j * modes, modes)]
            pair = pair + part_ref[tile, pl.ds(j * modes, modes)]
            lag_pair = lag_pair + part_ref[tile, pl.ds((SUBS + j) * modes, modes)]
        sums_ref[pl.ds(0, modes), lanes] = start
        sums_ref[pl.ds(modes, modes), lanes] = pair
        sums_ref[pl.ds(2 * modes, modes), lanes] = lag_pair


def backward_full(*refs, scale):
    (key_ref, value_ref, back_ref, sub_ref, log_ref, residue_ref, skip_ref, *sum_refs) = refs[:-9]
    (grad_key_ref, grad_value_ref, grad_residue_ref, grad_decay_ref, grad_skip_ref) = refs[-9:-4]
    (decay_ref, gain_ref, lead_ref, drive_grad_ref) = refs[-4:]
    length, channels = key_ref.shape
    modes = log_ref.shape[0]
    span = length // SUBS
    rate = jnp.exp(log_ref[...])
    norm = jnp.sqrt(2.0 * rate)
    gain = residue_ref[...] * norm
    decay_ref[...] = jnp.exp(-rate)
    gain_ref[...] = gain
    pair = tree_sum([ref[pl.ds(2 * modes, modes)] for ref in sum_refs])
    lag_pair = tree_sum([ref[pl.ds(3 * modes, modes)] for ref in sum_refs])
    grad_residue_ref[...] = norm * pair * scale
    grad_decay_ref[...] = gain * (0.5 * pair - rate * lag_pair) * scale
    grad_skip_ref[...] = tree_sum([ref[pl.ds(4 * modes, SUBS)] for ref in sum_refs]) * scale
    for tile, lanes in lane_tiles(channels):
        rate = jnp.exp(log_ref[:, lanes])
        stretch = jnp.exp(-length * rate)
        power = jnp.exp(-span * rate)
        start = jnp.zeros_like(rate)
        for distance in range(2 * RING - 1, 0, -1):
            start = stretch * start + nearby(sum_refs, distance, -1, 0, modes, lanes)
        for j in range(SUBS - 1, -1, -1):
            lead_ref[tile, pl.ds(j * modes, modes)] = start
            start = power * start + sub_ref[tile, pl.ds(j * modes, modes)]
        decay = [spread(decay_ref, m, lanes) for m in range(modes)]
        gain = [spread(gain_ref, m, lanes) for m in range(modes)]
        skip = spread(skip_ref, 0, lanes)

        def step(i, now):
            place = strided(span - 1 - i, span)
            g = back_ref[tile, place]
            now = [decay[m] * now[m] + g for m in range(modes)]
            drive_grad_ref[tile, place] = tree_sum([gain[m] * now[m] for m in range(modes)]) + skip * g
            return now

        first = [lead_ref[tile, strided(m, modes)] for m in range(modes)]
        lax.fori_loop(0, span, step, first, unroll=8)
        drive_grad = drive_grad_ref[tile]
        grad_key_ref[:, lanes] = (drive_grad * value_ref[:, lanes].astype(F32)).astype(BF16)
        grad_value_ref[:, lanes] = (drive_grad * key_ref[:, lanes].astype(F32)).astype(BF16)


def call(body, args, outs, scratch, micros, name):
    whole = pl.BlockSpec(memory_space=pltpu.VMEM)
    return pl.pallas_call(
        body,
        out_shape=[jax.ShapeDtypeStruct(o.shape, o.dtype) for o in outs],
        in_specs=[whole] * len(args),
        out_specs=[whole] * len(outs),
        scratch_shapes=[pltpu.VMEM(shape, F32) for shape in scratch],
        compiler_params=pltpu.CompilerParams(vmem_limit_bytes=6 * 2**20),
        cost_estimate=pl.CostEstimate(flops=int(micros * 1.15e9), bytes_accessed=0, transcendentals=0),
        name=name,
    )(*args)


def like(shape, dtype):
    return jax.ShapeDtypeStruct(shape, dtype)


def spread_over_x(value):
    return [value] + [hop(value, x=offset) for offset in range(1, RING)]


def together(*values):
    return lax.optimization_barrier(values)


def local(queries, key_proj, value_proj, skip_gain, residue, log_decay, out_weight, cotangent):
    length, channels = queries.shape
    modes = residue.shape[0]
    blocks = lax.axis_size("seq")
    scale = 1.0 / math.sqrt(length * blocks)
    skip_row = skip_gain.reshape(1, channels)
    tiles = channels // LANES
    wide = like((tiles, length, LANES), F32)
    narrow = like((length, channels), BF16)
    table = (modes, channels)

    block = gather_z(cotangent)
    ends, subs, driving = call(
        forward_ends,
        (key_proj, value_proj, log_decay),
        (like((2 * modes, channels), F32), like((tiles, 2 * SUBS * modes, LANES), F32), wide),
        [table, (SUBS, LANES)],
        0.1,
        "forward_ends",
    )
    ends_pair = jnp.concatenate([ends, hop(ends, pair=1)])
    block, ends_pair = together(block, ends_pair)
    main_block, other_block = hop(block, y=MAIN), hop(block, y=OTHER)
    earlier = spread_over_x(ends_pair)
    gated, turned, pre_gate, lead = call(
        forward_full,
        (queries, driving, subs, log_decay, residue, skip_row, *earlier),
        (narrow, narrow, wide, like((tiles, 2 * SUBS * modes, LANES), F32)),
        [table, table],
        0.1,
        "forward_full",
    )
    block, gated = together(block, gated)
    main_block, other_block, turned = together(main_block, other_block, turned)
    far_block = hop(main_block, y=MAIN)
    near_first, near_rest, far_first, far_rest = project(turned, out_weight)
    far_block, far_rest, gated_other = together(far_block, far_rest, hop(gated, pair=1))
    got_first, got_rest = hop(far_first, core=1), hop(far_rest, core=1)
    gated_pair = jnp.concatenate([gated, gated_other])
    opposite = add(near_first, got_first).astype(BF16)
    cot_rows = place_blocks(block, main_block, other_block, far_block)
    cot_rows = cot_rows.reshape(2 * length, -1)
    far_weight = weigh(gated_pair, cot_rows, scale, lax.rem(places()[4] + 2, RING))
    cot_rows, far_weight = together(cot_rows, far_weight)

    _, _, core, low, x = places()
    half = out_weight.shape[1] // 2
    low_weight = lax.dynamic_slice(out_weight, (0, low * half), (channels, half))
    grad_parts = lax.dot_general(cot_rows, low_weight, (((1,), (1,)), ((), ())), preferred_element_type=F32)
    grad_parts, got_rest, opposite = together(grad_parts, got_rest, hop(opposite, y=MAIN))
    theirs = hop(grad_parts[length:].astype(BF16), pair=1)
    cot_rows, theirs, far_weight = together(cot_rows, theirs, hop(far_weight, x=MAIN))
    main_weight, other_weight, own_weight = (
        weigh(gated_pair, cot_rows, scale, lax.rem(x + r, RING)) for r in (1 + 2 * core, 3 - 2 * core, 0)
    )

    main, other, own = (add(a, b) for a, b in zip(jnp.split(near_rest, 3), jnp.split(got_rest, 3)))
    main = add(main, opposite).astype(BF16)
    main, other = hop(main, y=MAIN), hop(other.astype(BF16), y=OTHER)
    main_weight = add(main_weight, far_weight).astype(BF16)

    theirs, main_weight, other_weight, own_weight = together(theirs, main_weight, other_weight, own_weight)
    grad_gated = add(grad_parts[:length], theirs)
    main_weight, other_weight = hop(main_weight, x=MAIN), hop(other_weight, x=OTHER)

    grad_query, back, sums, back_subs = call(
        backward_ends,
        (grad_gated, queries, pre_gate, driving, lead, log_decay),
        (narrow, wide, like((3 * modes + SUBS, channels), F32), like((tiles, SUBS * modes, LANES), F32)),
        [table, (tiles, 2 * SUBS * modes, LANES), (SUBS, LANES)],
        2.0,
        "backward_ends",
    )
    others = hop(sums, pair=1)
    others, main, other, main_weight, other_weight = together(others, main, other, main_weight, other_weight)
    own = add(own, main, other)
    part = own.shape[0] // 2
    leaving = hop(own[part:].astype(BF16), z=(2, -1))
    sums_pair = jnp.concatenate([sums[:modes], others[:modes], sums[modes:] + others[modes:]])
    all_sums = spread_over_x(sums_pair)
    leaving, *_ = together(leaving, *all_sums[1:])
    mixed = add(own[:part], by_core(leaving, hop(leaving, z=(None, -1)))).astype(BF16)
    grad_weight = add(own_weight, main_weight, other_weight).astype(BF16)
    grad_key, grad_value, grad_residue, grad_decay, grad_skip = call(
        functools.partial(backward_full, scale=scale),
        (key_proj, value_proj, back, back_subs, log_decay, residue, skip_row, *all_sums),
        (narrow, narrow, like(table, F32), like(table, F32), like((SUBS, channels), F32)),
        [table, table, (tiles, SUBS * modes, LANES), (tiles, length, LANES)],
        0.1,
        "backward_full",
    )
    return (
        mixed,
        grad_query,
        grad_key,
        grad_value,
        grad_weight,
        grad_residue,
        grad_decay,
        grad_skip[0],
    )


def solution(mesh):
    in_specs = (
        P("seq", "chan"),
        P("seq", "chan"),
        P("seq", "chan"),
        P("chan"),
        P(None, "chan"),
        P(None, "chan"),
        P("chan", None),
        P(("seq", "chan"), None),
    )
    out_specs = (
        P(("seq", "chan"), None),
        P("seq", "chan"),
        P("seq", "chan"),
        P("seq", "chan"),
        P("chan", "seq"),
        P(None, "chan"),
        P(None, "chan"),
        P("chan"),
    )
    return jax.shard_map(local, mesh=mesh, in_specs=in_specs, out_specs=out_specs, check_vma=False)
```

```python
import functools
import itertools
import math

import jax
import jax.numpy as jnp
from jax import lax
from jax.experimental import pallas as pl
from jax.experimental.pallas import tpu as pltpu
from jax.sharding import PartitionSpec as P

RING = 4
MAIN, OTHER = (1, -1), (-1, 1)
SUBS = 8
LANES = 128
F32 = jnp.float32
BF16 = jnp.bfloat16


def strided(first, step):
    return pl.ds(first, SUBS, stride=step)


def spread(ref, mode, lanes):
    return jnp.broadcast_to(ref[pl.ds(mode, 1), lanes], (SUBS, LANES))


def tree_sum(parts):
    while len(parts) > 1:
        parts = [a + b for a, b in zip(parts[::2], parts[1::2])] + parts[len(parts) & ~1 :]
    return parts[0]


def lane_tiles(channels):
    return [(tile, pl.ds(tile * LANES, LANES)) for tile in range(channels // LANES)]


def places():
    chan, seq = lax.axis_index("chan"), lax.axis_index("seq")
    return chan // 4, lax.rem(chan // 2, 2), lax.rem(chan, 2), seq // RING, lax.rem(seq, RING)


def hop(value, x=0, y=0, z=0, core=0, pair=0):
    moves = []
    for i, j, k, c in itertools.product(range(RING), range(RING), range(RING), range(2)):
        dx, dy, dz = (step[c] if isinstance(step, tuple) else step for step in (x, y, z))
        if None in (dx, dy, dz):
            continue
        there = ((i + dx) % RING, (j + dy) % RING, ((k + dz) % RING) ^ pair, c ^ core)
        moves.append(tuple(((b * 2 + d // 2) * 2 + e) * 2 * RING + d % 2 * RING + a for a, b, d, e in ((i, j, k, c), there)))
    return lax.ppermute(value, ("chan", "seq"), moves)


def by_core(first, second):
    return jnp.where(places()[2] == 0, first, second)


def gather_z(cotangent):
    _, high, _, low, _ = places()
    tokens, width = cotangent.shape
    half = width // 2
    mine = lax.dynamic_slice(cotangent, (0, low * half), (tokens, half))
    theirs = lax.dynamic_slice(cotangent, (0, (1 - low) * half), (tokens, half))
    above, below, across = hop(theirs, z=1), hop(theirs, z=-1), hop(mine, z=2)
    stack = jnp.where(high == 0, jnp.stack([mine, across]), jnp.stack([across, mine]))
    same, differ = jnp.where(low == 1, above, below), jnp.where(low == 1, below, above)
    other = jnp.where(high == 0, jnp.stack([same, differ]), jnp.stack([differ, same]))
    return jnp.stack([stack, other])


def place_blocks(*blocks):
    y, _, core, _, _ = places()
    _, _, tokens, half = blocks[0].shape
    whole = jnp.zeros((2, RING, 2, 2, tokens, half), BF16)
    for block, steps in zip(blocks, ((0, 0), (RING - 1, 1), (1, RING - 1), (2, 2))):
        for part, at_core in ((block, core), (hop(block, core=1), 1 - core)):
            row = lax.rem(y + jnp.where(at_core == 0, *steps), RING)
            whole = lax.dynamic_update_slice(whole, part[:, None, :, None], (0, row, 0, at_core, 0, 0))
    return whole


def add(*parts):
    return functools.reduce(jnp.add, [part.astype(F32) for part in parts])


def project_tile(rows_ref, weight_ref, *out_refs):
    product = jnp.dot(rows_ref[...], weight_ref[...], preferred_element_type=F32).astype(BF16)
    first = 0
    for ref in out_refs:
        ref[...] = product[first : first + ref.shape[0]]
        first += ref.shape[0]


def project(turned, out_weight):
    rows, depth = turned.shape
    width = out_weight.shape[1]
    tile = 1024
    sizes = [rows // 8, 3 * rows // 8] * 2
    return pl.pallas_call(
        project_tile,
        grid=(width // tile,),
        out_shape=[jax.ShapeDtypeStruct((size, width), BF16) for size in sizes],
        in_specs=[pl.BlockSpec((rows, depth), lambda i: (0, 0)), pl.BlockSpec((depth, tile), lambda i: (0, i))],
        out_specs=[pl.BlockSpec((size, tile), lambda i: (0, i)) for size in sizes],
        compiler_params=pltpu.CompilerParams(vmem_limit_bytes=12 * 2**20),
        cost_estimate=pl.CostEstimate(
            flops=2 * rows * depth * width, bytes_accessed=2 * width * (rows + depth), transcendentals=0
        ),
        name="project",
    )(turned, out_weight)


def weigh(gated, cot_rows, scale, block):
    width = cot_rows.shape[1] // RING
    columns = lax.dynamic_slice(cot_rows, (0, block * width), (cot_rows.shape[0], width))
    product = lax.dot_general(gated, columns, (((0,), (0,)), ((), ())), preferred_element_type=F32)
    return (product * scale).astype(BF16)


def nearby(refs, distance, way, first, modes, lanes):
    _, _, _, low, x = places()
    before = x if way == 1 else RING - 1 - x
    other_counts = low == (way + 1) // 2
    other = refs[0].shape[0] // 2 if way == 1 else modes
    step = distance % RING
    ref = refs[way * step % RING]
    mine = ref[pl.ds(first, modes), lanes]
    theirs = jnp.where(other_counts, ref[pl.ds(other + first, modes), lanes], 0.0)
    if distance < RING:
        return jnp.where(step <= before, mine, theirs)
    return jnp.where(step <= before, theirs, 0.0)


def forward_ends(key_ref, value_ref, log_ref, ends_ref, sub_ref, drive_ref, decay_ref, zero_ref):
    length, channels = key_ref.shape
    modes = log_ref.shape[0]
    span = length // SUBS
    decay_ref[...] = jnp.exp(-jnp.exp(log_ref[...]))
    zero_ref[...] = jnp.zeros_like(zero_ref)
    for tile, lanes in lane_tiles(channels):
        drive_ref[tile] = key_ref[:, lanes].astype(F32) * value_ref[:, lanes].astype(F32)
        decay = [spread(decay_ref, m, lanes) for m in range(modes)]

        def step(i, carry):
            now, lag = carry
            u = drive_ref[tile, strided(i, span)]
            lag = [decay[m] * (lag[m] + now[m]) for m in range(modes)]
            now = [decay[m] * now[m] + u for m in range(modes)]
            return now, lag

        zero = [zero_ref[...]] * modes
        now, lag = lax.fori_loop(0, span, step, (zero, zero), unroll=8)
        for m in range(modes):
            sub_ref[tile, strided(m, modes)] = now[m]
            sub_ref[tile, strided(SUBS * modes + m, modes)] = lag[m]
        power = jnp.exp(-span * jnp.exp(log_ref[:, lanes]))
        state = jnp.zeros_like(power)
        lagged = jnp.zeros_like(power)
        for j in range(SUBS):
            lagged = power * (lagged + span * state) + sub_ref[tile, pl.ds((SUBS + j) * modes, modes)]
            state = power * state + sub_ref[tile, pl.ds(j * modes, modes)]
        ends_ref[pl.ds(0, modes), lanes] = state
        ends_ref[pl.ds(modes, modes), lanes] = lagged


def forward_full(*refs):
    (query_ref, drive_ref, sub_ref, log_ref, residue_ref, skip_ref, *end_refs) = refs[:-6]
    (gated_ref, turned_ref, pre_ref, lead_ref, decay_ref, gain_ref) = refs[-6:]
    length, channels = query_ref.shape
    modes = log_ref.shape[0]
    span = length // SUBS
    rate = jnp.exp(log_ref[...])
    decay_ref[...] = jnp.exp(-rate)
    gain_ref[...] = residue_ref[...] * jnp.sqrt(2.0 * rate)
    for tile, lanes in lane_tiles(channels):
        rate = jnp.exp(log_ref[:, lanes])
        stretch = jnp.exp(-length * rate)
        power = jnp.exp(-span * rate)
        state = jnp.zeros_like(rate)
        lagged = jnp.zeros_like(rate)
        for distance in range(2 * RING - 1, 0, -1):
            lagged = stretch * (lagged + length * state) + nearby(end_refs, distance, 1, modes, modes, lanes)
            state = stretch * state + nearby(end_refs, distance, 1, 0, modes, lanes)
        for j in range(SUBS):
            now_rows, lag_rows = (pl.ds((j + k) * modes, modes) for k in (0, SUBS))
            lead_ref[tile, now_rows] = state
            lead_ref[tile, lag_rows] = lagged
            lagged = power * (lagged + span * state) + sub_ref[tile, lag_rows]
            state = power * state + sub_ref[tile, now_rows]
        decay = [spread(decay_ref, m, lanes) for m in range(modes)]
        gain = [spread(gain_ref, m, lanes) for m in range(modes)]
        skip = spread(skip_ref, 0, lanes)

        def step(i, now):
            place = strided(i, span)
            u = drive_ref[tile, place]
            now = [decay[m] * now[m] + u for m in range(modes)]
            pre_ref[tile, place] = tree_sum([gain[m] * now[m] for m in range(modes)]) + skip * u
            return now

        first = [lead_ref[tile, strided(m, modes)] for m in range(modes)]
        lax.fori_loop(0, span, step, first, unroll=8)
        gated_ref[:, lanes] = (query_ref[:, lanes].astype(F32) * pre_ref[tile]).astype(BF16)
    part = length // (RING * 4)
    y, high, core, _, _ = places()
    for i in range(RING * 4):
        on = lax.rem(i // 4 + RING - y, RING)
        kept = lax.rem(i % 2 + core, 2) == 0
        first = jnp.where(kept, 1 + 2 * core, 3 - 2 * core)
        there = jnp.where(on == 0, 3, jnp.where(on == 2, 0, jnp.where(on == first, 1, 2)))
        there = there + jnp.where(kept, 0, RING)
        there = there * 2 + lax.rem(i // 2 % 2 + high, 2)
        turned_ref[pl.ds(pl.multiple_of(there * part, part), part)] = gated_ref[pl.ds(i * part, part)]


def backward_ends(
    grad_ref, query_ref, pre_ref, drive_ref, lead_ref, log_ref,
    grad_query_ref, back_ref, sums_ref, sub_ref, decay_ref, part_ref, zero_ref,
):
    length, channels = query_ref.shape
    modes = log_ref.shape[0]
    span = length // SUBS
    half = modes // 2
    decay_ref[...] = jnp.exp(-jnp.exp(log_ref[...]))
    zero_ref[...] = jnp.zeros_like(zero_ref)
    for tile, lanes in lane_tiles(channels):
        grad = grad_ref[:, lanes].astype(F32)
        grad_query_ref[:, lanes] = (grad * pre_ref[tile]).astype(BF16)
        back_ref[tile] = grad * query_ref[:, lanes].astype(F32)
        decay = [spread(decay_ref, m, lanes) for m in range(modes)]

        def back_step(i, now):
            g = back_ref[tile, strided(span - 1 - i, span)]
            return [decay[m] * now[m] + g for m in range(modes)]

        zero = [zero_ref[...]] * modes
        now = lax.fori_loop(0, span, back_step, zero, unroll=8)
        for m in range(modes):
            sub_ref[tile, strided(m, modes)] = now[m]
        for low in range(0, modes, half):
            group = range(low, low + half)
            decay = [spread(decay_ref, m, lanes) for m in group]

            def pair_step(i, carry):
                state, lag, pair, lag_pair, skip = carry
                place = strided(i, span)
                u = drive_ref[tile, place]
                g = back_ref[tile, place]
                lag = [decay[m] * (lag[m] + state[m]) for m in range(half)]
                state = [decay[m] * state[m] + u for m in range(half)]
                pair = [pair[m] + g * state[m] for m in range(half)]
                lag_pair = [lag_pair[m] + g * lag[m] for m in range(half)]
                return state, lag, pair, lag_pair, skip + g * u

            state = [lead_ref[tile, strided(m, modes)] for m in group]
            lag = [lead_ref[tile, strided(SUBS * modes + m, modes)] for m in group]
            zero = [zero_ref[...]] * half
            state, lag, pair, lag_pair, skip = lax.fori_loop(
                0, span, pair_step, (state, lag, zero, zero, zero[0]), unroll=8
            )
            for m in range(half):
                part_ref[tile, strided(low + m, modes)] = pair[m]
                part_ref[tile, strided(SUBS * modes + low + m, modes)] = lag_pair[m]
        total = jnp.sum(skip, axis=0, keepdims=True)
        sums_ref[pl.ds(3 * modes, SUBS), lanes] = jnp.broadcast_to(total, (SUBS, LANES))
        power = jnp.exp(-span * jnp.exp(log_ref[:, lanes]))
        start = jnp.zeros_like(power)
        pair = jnp.zeros_like(power)
        lag_pair = jnp.zeros_like(power)
        for j in range(SUBS - 1, -1, -1):
            start = power * start + sub_ref[tile, pl.ds(j * modes, modes)]
            pair = pair + part_ref[tile, pl.ds(j * modes, modes)]
            lag_pair = lag_pair + part_ref[tile, pl.ds((SUBS + j) * modes, modes)]
        sums_ref[pl.ds(0, modes), lanes] = start
        sums_ref[pl.ds(modes, modes), lanes] = pair
        sums_ref[pl.ds(2 * modes, modes), lanes] = lag_pair


def backward_full(*refs, scale):
    (key_ref, value_ref, back_ref, sub_ref, log_ref, residue_ref, skip_ref, *sum_refs) = refs[:-9]
    (grad_key_ref, grad_value_ref, grad_residue_ref, grad_decay_ref, grad_skip_ref) = refs[-9:-4]
    (decay_ref, gain_ref, lead_ref, drive_grad_ref) = refs[-4:]
    length, channels = key_ref.shape
    modes = log_ref.shape[0]
    span = length // SUBS
    rate = jnp.exp(log_ref[...])
    norm = jnp.sqrt(2.0 * rate)
    gain = residue_ref[...] * norm
    decay_ref[...] = jnp.exp(-rate)
    gain_ref[...] = gain
    pair = tree_sum([ref[pl.ds(2 * modes, modes)] for ref in sum_refs])
    lag_pair = tree_sum([ref[pl.ds(3 * modes, modes)] for ref in sum_refs])
    grad_residue_ref[...] = norm * pair * scale
    grad_decay_ref[...] = gain * (0.5 * pair - rate * lag_pair) * scale
    grad_skip_ref[...] = tree_sum([ref[pl.ds(4 * modes, SUBS)] for ref in sum_refs]) * scale
    for tile, lanes in lane_tiles(channels):
        rate = jnp.exp(log_ref[:, lanes])
        stretch = jnp.exp(-length * rate)
        power = jnp.exp(-span * rate)
        start = jnp.zeros_like(rate)
        for distance in range(2 * RING - 1, 0, -1):
            start = stretch * start + nearby(sum_refs, distance, -1, 0, modes, lanes)
        for j in range(SUBS - 1, -1, -1):
            lead_ref[tile, pl.ds(j * modes, modes)] = start
            start = power * start + sub_ref[tile, pl.ds(j * modes, modes)]
        decay = [spread(decay_ref, m, lanes) for m in range(modes)]
        gain = [spread(gain_ref, m, lanes) for m in range(modes)]
        skip = spread(skip_ref, 0, lanes)

        def step(i, now):
            place = strided(span - 1 - i, span)
            g = back_ref[tile, place]
            now = [decay[m] * now[m] + g for m in range(modes)]
            drive_grad_ref[tile, place] = tree_sum([gain[m] * now[m] for m in range(modes)]) + skip * g
            return now

        first = [lead_ref[tile, strided(m, modes)] for m in range(modes)]
        lax.fori_loop(0, span, step, first, unroll=8)
        drive_grad = drive_grad_ref[tile]
        grad_key_ref[:, lanes] = (drive_grad * value_ref[:, lanes].astype(F32)).astype(BF16)
        grad_value_ref[:, lanes] = (drive_grad * key_ref[:, lanes].astype(F32)).astype(BF16)


def call(body, args, outs, scratch, micros, name):
    whole = pl.BlockSpec(memory_space=pltpu.VMEM)
    return pl.pallas_call(
        body,
        out_shape=[jax.ShapeDtypeStruct(o.shape, o.dtype) for o in outs],
        in_specs=[whole] * len(args),
        out_specs=[whole] * len(outs),
        scratch_shapes=[pltpu.VMEM(shape, F32) for shape in scratch],
        compiler_params=pltpu.CompilerParams(vmem_limit_bytes=6 * 2**20),
        cost_estimate=pl.CostEstimate(flops=int(micros * 1.15e9), bytes_accessed=0, transcendentals=0),
        name=name,
    )(*args)


def like(shape, dtype):
    return jax.ShapeDtypeStruct(shape, dtype)


def spread_over_x(value):
    return [value] + [hop(value, x=offset) for offset in range(1, RING)]


def together(*values):
    return lax.optimization_barrier(values)


def local(queries, key_proj, value_proj, skip_gain, residue, log_decay, out_weight, cotangent):
    length, channels = queries.shape
    modes = residue.shape[0]
    blocks = lax.axis_size("seq")
    scale = 1.0 / math.sqrt(length * blocks)
    skip_row = skip_gain.reshape(1, channels)
    tiles = channels // LANES
    wide = like((tiles, length, LANES), F32)
    narrow = like((length, channels), BF16)
    table = (modes, channels)

    block = gather_z(cotangent)
    ends, subs, driving = call(
        forward_ends,
        (key_proj, value_proj, log_decay),
        (like((2 * modes, channels), F32), like((tiles, 2 * SUBS * modes, LANES), F32), wide),
        [table, (SUBS, LANES)],
        0.1,
        "forward_ends",
    )
    ends_pair = jnp.concatenate([ends, hop(ends, pair=1)])
    main_block, other_block = hop(block, y=MAIN), hop(block, y=OTHER)
    main_block, other_block, ends_pair = together(main_block, other_block, ends_pair)
    far_block = hop(main_block, y=MAIN)
    earlier = spread_over_x(ends_pair)
    gated, turned, pre_gate, lead = call(
        forward_full,
        (queries, driving, subs, log_decay, residue, skip_row, *earlier),
        (narrow, narrow, wide, like((tiles, 2 * SUBS * modes, LANES), F32)),
        [table, table],
        0.1,
        "forward_full",
    )
    block, gated = together(block, gated)
    far_block, turned = together(far_block, turned)
    near_first, near_rest, far_first, far_rest = project(turned, out_weight)
    far_first, gated_other = together(far_first, hop(gated, pair=1))
    got_first, far_rest = together(hop(far_first, core=1), far_rest)
    got_rest = hop(far_rest, core=1)
    gated_pair = jnp.concatenate([gated, gated_other])
    opposite = add(near_first, got_first).astype(BF16)
    cot_rows = place_blocks(block, main_block, other_block, far_block)
    cot_rows, opposite = together(cot_rows.reshape(2 * length, -1), opposite)

    _, _, core, low, x = places()
    half = out_weight.shape[1] // 2
    low_weight = lax.dynamic_slice(out_weight, (0, low * half), (channels, half))
    grad_parts = lax.dot_general(cot_rows, low_weight, (((1,), (1,)), ((), ())), preferred_element_type=F32)
    cot_rows, grad_parts = together(cot_rows, grad_parts)
    theirs = hop(grad_parts[length:].astype(BF16), pair=1)

    far_weight = weigh(gated_pair, cot_rows, scale, lax.rem(x + 2, RING))
    cot_rows, far_weight = together(cot_rows, far_weight)
    got_rest, _ = together(got_rest, far_weight)
    main_weight, other_weight, own_weight = (
        weigh(gated_pair, cot_rows, scale, lax.rem(x + r, RING)) for r in (1 + 2 * core, 3 - 2 * core, 0)
    )
    main, other, own = (add(a, b) for a, b in zip(jnp.split(near_rest, 3), jnp.split(got_rest, 3)))
    main = add(main, hop(opposite, y=MAIN)).astype(BF16)
    main, other, main_weight, other_weight, own_weight = together(
        main, other.astype(BF16), main_weight, other_weight, own_weight
    )
    main, other = hop(main, y=MAIN), hop(other, y=OTHER)
    other_weight = hop(other_weight, x=OTHER)
    main_weight = add(main_weight, hop(far_weight, x=MAIN)).astype(BF16)

    theirs, main_weight = together(theirs, main_weight)
    grad_gated = add(grad_parts[:length], theirs)
    main_weight = hop(main_weight, x=MAIN)

    grad_query, back, sums, back_subs = call(
        backward_ends,
        (grad_gated, queries, pre_gate, driving, lead, log_decay),
        (narrow, wide, like((3 * modes + SUBS, channels), F32), like((tiles, SUBS * modes, LANES), F32)),
        [table, (tiles, 2 * SUBS * modes, LANES), (SUBS, LANES)],
        2.0,
        "backward_ends",
    )
    others = hop(sums, pair=1)
    others, main, other, main_weight, other_weight = together(others, main, other, main_weight, other_weight)
    own = add(own, main, other)
    part = own.shape[0] // 2
    leaving = hop(own[part:].astype(BF16), z=(2, -1))
    sums_pair = jnp.concatenate([sums[:modes], others[:modes], sums[modes:] + others[modes:]])
    all_sums = spread_over_x(sums_pair)
    leaving, *_ = together(leaving, *all_sums[1:])
    mixed = add(own[:part], by_core(leaving, hop(leaving, z=(None, -1)))).astype(BF16)
    grad_weight = add(own_weight, main_weight, other_weight).astype(BF16)
    grad_key, grad_value, grad_residue, grad_decay, grad_skip = call(
        functools.partial(backward_full, scale=scale),
        (key_proj, value_proj, back, back_subs, log_decay, residue, skip_row, *all_sums),
        (narrow, narrow, like(table, F32), like(table, F32), like((SUBS, channels), F32)),
        [table, table, (tiles, SUBS * modes, LANES), (tiles, length, LANES)],
        0.1,
        "backward_full",
    )
    return (
        mixed,
        grad_query,
        grad_key,
        grad_value,
        grad_weight,
        grad_residue,
        grad_decay,
        grad_skip[0],
    )


def solution(mesh):
    in_specs = (
        P("seq", "chan"),
        P("seq", "chan"),
        P("seq", "chan"),
        P("chan"),
        P(None, "chan"),
        P(None, "chan"),
        P("chan", None),
        P(("seq", "chan"), None),
    )
    out_specs = (
        P(("seq", "chan"), None),
        P("seq", "chan"),
        P("seq", "chan"),
        P("seq", "chan"),
        P("chan", "seq"),
        P(None, "chan"),
        P(None, "chan"),
        P("chan"),
    )
    return jax.shard_map(local, mesh=mesh, in_specs=in_specs, out_specs=out_specs, check_vma=False)
```

```python
import functools
import itertools
import math

import jax
import jax.numpy as jnp
from jax import lax
from jax.experimental import pallas as pl
from jax.experimental.pallas import tpu as pltpu
from jax.sharding import PartitionSpec as P

RING = 4
MAIN, OTHER = (1, -1), (-1, 1)
SUBS = 8
LANES = 128
F32 = jnp.float32
BF16 = jnp.bfloat16


def strided(first, step):
    return pl.ds(first, SUBS, stride=step)


def spread(ref, mode, lanes):
    return jnp.broadcast_to(ref[pl.ds(mode, 1), lanes], (SUBS, LANES))


def tree_sum(parts):
    while len(parts) > 1:
        parts = [a + b for a, b in zip(parts[::2], parts[1::2])] + parts[len(parts) & ~1 :]
    return parts[0]


def lane_tiles(channels):
    return [(tile, pl.ds(tile * LANES, LANES)) for tile in range(channels // LANES)]


def places():
    chan, seq = lax.axis_index("chan"), lax.axis_index("seq")
    return chan // 4, lax.rem(chan // 2, 2), lax.rem(chan, 2), seq // RING, lax.rem(seq, RING)


def hop(value, x=0, y=0, z=0, core=0, pair=0):
    moves = []
    for i, j, k, c in itertools.product(range(RING), range(RING), range(RING), range(2)):
        dx, dy, dz = (step[c] if isinstance(step, tuple) else step for step in (x, y, z))
        if None in (dx, dy, dz):
            continue
        there = ((i + dx) % RING, (j + dy) % RING, ((k + dz) % RING) ^ pair, c ^ core)
        moves.append(tuple(((b * 2 + d // 2) * 2 + e) * 2 * RING + d % 2 * RING + a for a, b, d, e in ((i, j, k, c), there)))
    return lax.ppermute(value, ("chan", "seq"), moves)


def by_core(first, second):
    return jnp.where(places()[2] == 0, first, second)


def gather_z(cotangent):
    _, high, _, low, _ = places()
    tokens, width = cotangent.shape
    half = width // 2
    mine = lax.dynamic_slice(cotangent, (0, low * half), (tokens, half))
    theirs = lax.dynamic_slice(cotangent, (0, (1 - low) * half), (tokens, half))
    above, below, across = hop(theirs, z=1), hop(theirs, z=-1), hop(mine, z=2)
    stack = jnp.where(high == 0, jnp.stack([mine, across]), jnp.stack([across, mine]))
    same, differ = jnp.where(low == 1, above, below), jnp.where(low == 1, below, above)
    other = jnp.where(high == 0, jnp.stack([same, differ]), jnp.stack([differ, same]))
    return jnp.stack([stack, other])


def place_blocks(*blocks):
    y, _, core, _, _ = places()
    _, _, tokens, half = blocks[0].shape
    whole = jnp.zeros((2, RING, 2, 2, tokens, half), BF16)
    for block, steps in zip(blocks, ((0, 0), (RING - 1, 1), (1, RING - 1), (2, 2))):
        for part, at_core in ((block, core), (hop(block, core=1), 1 - core)):
            row = lax.rem(y + jnp.where(at_core == 0, *steps), RING)
            whole = lax.dynamic_update_slice(whole, part[:, None, :, None], (0, row, 0, at_core, 0, 0))
    return whole


def add(*parts):
    return functools.reduce(jnp.add, [part.astype(F32) for part in parts])


def project_tile(rows_ref, weight_ref, *out_refs):
    product = jnp.dot(rows_ref[...], weight_ref[...], preferred_element_type=F32).astype(BF16)
    first = 0
    for ref in out_refs:
        ref[...] = product[first : first + ref.shape[0]]
        first += ref.shape[0]


def project(turned, out_weight):
    rows, depth = turned.shape
    width = out_weight.shape[1]
    tile = 1024
    sizes = [rows // 8, 3 * rows // 8] * 2
    return pl.pallas_call(
        project_tile,
        grid=(width // tile,),
        out_shape=[jax.ShapeDtypeStruct((size, width), BF16) for size in sizes],
        in_specs=[pl.BlockSpec((rows, depth), lambda i: (0, 0)), pl.BlockSpec((depth, tile), lambda i: (0, i))],
        out_specs=[pl.BlockSpec((size, tile), lambda i: (0, i)) for size in sizes],
        compiler_params=pltpu.CompilerParams(vmem_limit_bytes=12 * 2**20),
        cost_estimate=pl.CostEstimate(
            flops=2 * rows * depth * width, bytes_accessed=2 * width * (rows + depth), transcendentals=0
        ),
        name="project",
    )(turned, out_weight)


def weigh(gated, cot_rows, scale, block):
    width = cot_rows.shape[1] // RING
    columns = lax.dynamic_slice(cot_rows, (0, block * width), (cot_rows.shape[0], width))
    product = lax.dot_general(gated, columns, (((0,), (0,)), ((), ())), preferred_element_type=F32)
    return (product * scale).astype(BF16)


def nearby(refs, distance, way, first, modes, lanes):
    _, _, _, low, x = places()
    before = x if way == 1 else RING - 1 - x
    other_counts = low == (way + 1) // 2
    other = refs[0].shape[0] // 2 if way == 1 else modes
    step = distance % RING
    ref = refs[way * step % RING]
    mine = ref[pl.ds(first, modes), lanes]
    theirs = jnp.where(other_counts, ref[pl.ds(other + first, modes), lanes], 0.0)
    if distance < RING:
        return jnp.where(step <= before, mine, theirs)
    return jnp.where(step <= before, theirs, 0.0)


def forward_ends(key_ref, value_ref, log_ref, ends_ref, sub_ref, drive_ref, decay_ref, zero_ref):
    length, channels = key_ref.shape
    modes = log_ref.shape[0]
    span = length // SUBS
    decay_ref[...] = jnp.exp(-jnp.exp(log_ref[...]))
    zero_ref[...] = jnp.zeros_like(zero_ref)
    for tile, lanes in lane_tiles(channels):
        drive_ref[tile] = key_ref[:, lanes].astype(F32) * value_ref[:, lanes].astype(F32)
        decay = [spread(decay_ref, m, lanes) for m in range(modes)]

        def step(i, carry):
            now, lag = carry
            u = drive_ref[tile, strided(i, span)]
            lag = [decay[m] * (lag[m] + now[m]) for m in range(modes)]
            now = [decay[m] * now[m] + u for m in range(modes)]
            return now, lag

        zero = [zero_ref[...]] * modes
        now, lag = lax.fori_loop(0, span, step, (zero, zero), unroll=8)
        for m in range(modes):
            sub_ref[tile, strided(m, modes)] = now[m]
            sub_ref[tile, strided(SUBS * modes + m, modes)] = lag[m]
        power = jnp.exp(-span * jnp.exp(log_ref[:, lanes]))
        state = jnp.zeros_like(power)
        lagged = jnp.zeros_like(power)
        for j in range(SUBS):
            lagged = power * (lagged + span * state) + sub_ref[tile, pl.ds((SUBS + j) * modes, modes)]
            state = power * state + sub_ref[tile, pl.ds(j * modes, modes)]
        ends_ref[pl.ds(0, modes), lanes] = state
        ends_ref[pl.ds(modes, modes), lanes] = lagged


def forward_full(*refs):
    (query_ref, drive_ref, sub_ref, log_ref, residue_ref, skip_ref, *end_refs) = refs[:-6]
    (gated_ref, turned_ref, pre_ref, lead_ref, decay_ref, gain_ref) = refs[-6:]
    length, channels = query_ref.shape
    modes = log_ref.shape[0]
    span = length // SUBS
    rate = jnp.exp(log_ref[...])
    decay_ref[...] = jnp.exp(-rate)
    gain_ref[...] = residue_ref[...] * jnp.sqrt(2.0 * rate)
    for tile, lanes in lane_tiles(channels):
        rate = jnp.exp(log_ref[:, lanes])
        stretch = jnp.exp(-length * rate)
        power = jnp.exp(-span * rate)
        state = jnp.zeros_like(rate)
        lagged = jnp.zeros_like(rate)
        for distance in range(2 * RING - 1, 0, -1):
            lagged = stretch * (lagged + length * state) + nearby(end_refs, distance, 1, modes, modes, lanes)
            state = stretch * state + nearby(end_refs, distance, 1, 0, modes, lanes)
        for j in range(SUBS):
            now_rows, lag_rows = (pl.ds((j + k) * modes, modes) for k in (0, SUBS))
            lead_ref[tile, now_rows] = state
            lead_ref[tile, lag_rows] = lagged
            lagged = power * (lagged + span * state) + sub_ref[tile, lag_rows]
            state = power * state + sub_ref[tile, now_rows]
        decay = [spread(decay_ref, m, lanes) for m in range(modes)]
        gain = [spread(gain_ref, m, lanes) for m in range(modes)]
        skip = spread(skip_ref, 0, lanes)

        def step(i, now):
            place = strided(i, span)
            u = drive_ref[tile, place]
            now = [decay[m] * now[m] + u for m in range(modes)]
            pre_ref[tile, place] = tree_sum([gain[m] * now[m] for m in range(modes)]) + skip * u
            return now

        first = [lead_ref[tile, strided(m, modes)] for m in range(modes)]
        lax.fori_loop(0, span, step, first, unroll=8)
        gated_ref[:, lanes] = (query_ref[:, lanes].astype(F32) * pre_ref[tile]).astype(BF16)
    part = length // (RING * 4)
    y, high, core, _, _ = places()
    for i in range(RING * 4):
        on = lax.rem(i // 4 + RING - y, RING)
        kept = lax.rem(i % 2 + core, 2) == 0
        first = jnp.where(kept, 1 + 2 * core, 3 - 2 * core)
        there = jnp.where(on == 0, 3, jnp.where(on == 2, 0, jnp.where(on == first, 1, 2)))
        there = there + jnp.where(kept, 0, RING)
        there = there * 2 + lax.rem(i // 2 % 2 + high, 2)
        turned_ref[pl.ds(pl.multiple_of(there * part, part), part)] = gated_ref[pl.ds(i * part, part)]


def backward_ends(
    grad_ref, query_ref, pre_ref, drive_ref, lead_ref, log_ref,
    grad_query_ref, back_ref, sums_ref, sub_ref, decay_ref, part_ref, zero_ref,
):
    length, channels = query_ref.shape
    modes = log_ref.shape[0]
    span = length // SUBS
    half = modes // 2
    decay_ref[...] = jnp.exp(-jnp.exp(log_ref[...]))
    zero_ref[...] = jnp.zeros_like(zero_ref)
    for tile, lanes in lane_tiles(channels):
        grad = grad_ref[:, lanes].astype(F32)
        grad_query_ref[:, lanes] = (grad * pre_ref[tile]).astype(BF16)
        back_ref[tile] = grad * query_ref[:, lanes].astype(F32)
        decay = [spread(decay_ref, m, lanes) for m in range(modes)]

        def back_step(i, now):
            g = back_ref[tile, strided(span - 1 - i, span)]
            return [decay[m] * now[m] + g for m in range(modes)]

        zero = [zero_ref[...]] * modes
        now = lax.fori_loop(0, span, back_step, zero, unroll=8)
        for m in range(modes):
            sub_ref[tile, strided(m, modes)] = now[m]
        for low in range(0, modes, half):
            group = range(low, low + half)
            decay = [spread(decay_ref, m, lanes) for m in group]

            def pair_step(i, carry):
                state, lag, pair, lag_pair, skip = carry
                place = strided(i, span)
                u = drive_ref[tile, place]
                g = back_ref[tile, place]
                lag = [decay[m] * (lag[m] + state[m]) for m in range(half)]
                state = [decay[m] * state[m] + u for m in range(half)]
                pair = [pair[m] + g * state[m] for m in range(half)]
                lag_pair = [lag_pair[m] + g * lag[m] for m in range(half)]
                return state, lag, pair, lag_pair, skip + g * u

            state = [lead_ref[tile, strided(m, modes)] for m in group]
            lag = [lead_ref[tile, strided(SUBS * modes + m, modes)] for m in group]
            zero = [zero_ref[...]] * half
            state, lag, pair, lag_pair, skip = lax.fori_loop(
                0, span, pair_step, (state, lag, zero, zero, zero[0]), unroll=8
            )
            for m in range(half):
                part_ref[tile, strided(low + m, modes)] = pair[m]
                part_ref[tile, strided(SUBS * modes + low + m, modes)] = lag_pair[m]
        total = jnp.sum(skip, axis=0, keepdims=True)
        sums_ref[pl.ds(3 * modes, SUBS), lanes] = jnp.broadcast_to(total, (SUBS, LANES))
        power = jnp.exp(-span * jnp.exp(log_ref[:, lanes]))
        start = jnp.zeros_like(power)
        pair = jnp.zeros_like(power)
        lag_pair = jnp.zeros_like(power)
        for j in range(SUBS - 1, -1, -1):
            start = power * start + sub_ref[tile, pl.ds(j * modes, modes)]
            pair = pair + part_ref[tile, pl.ds(j * modes, modes)]
            lag_pair = lag_pair + part_ref[tile, pl.ds((SUBS + j) * modes, modes)]
        sums_ref[pl.ds(0, modes), lanes] = start
        sums_ref[pl.ds(modes, modes), lanes] = pair
        sums_ref[pl.ds(2 * modes, modes), lanes] = lag_pair


def backward_full(*refs, scale):
    (key_ref, value_ref, back_ref, sub_ref, log_ref, residue_ref, skip_ref, *sum_refs) = refs[:-9]
    (grad_key_ref, grad_value_ref, grad_residue_ref, grad_decay_ref, grad_skip_ref) = refs[-9:-4]
    (decay_ref, gain_ref, lead_ref, drive_grad_ref) = refs[-4:]
    length, channels = key_ref.shape
    modes = log_ref.shape[0]
    span = length // SUBS
    rate = jnp.exp(log_ref[...])
    norm = jnp.sqrt(2.0 * rate)
    gain = residue_ref[...] * norm
    decay_ref[...] = jnp.exp(-rate)
    gain_ref[...] = gain
    pair = tree_sum([ref[pl.ds(2 * modes, modes)] for ref in sum_refs])
    lag_pair = tree_sum([ref[pl.ds(3 * modes, modes)] for ref in sum_refs])
    grad_residue_ref[...] = norm * pair * scale
    grad_decay_ref[...] = gain * (0.5 * pair - rate * lag_pair) * scale
    grad_skip_ref[...] = tree_sum([ref[pl.ds(4 * modes, SUBS)] for ref in sum_refs]) * scale
    for tile, lanes in lane_tiles(channels):
        rate = jnp.exp(log_ref[:, lanes])
        stretch = jnp.exp(-length * rate)
        power = jnp.exp(-span * rate)
        start = jnp.zeros_like(rate)
        for distance in range(2 * RING - 1, 0, -1):
            start = stretch * start + nearby(sum_refs, distance, -1, 0, modes, lanes)
        for j in range(SUBS - 1, -1, -1):
            lead_ref[tile, pl.ds(j * modes, modes)] = start
            start = power * start + sub_ref[tile, pl.ds(j * modes, modes)]
        decay = [spread(decay_ref, m, lanes) for m in range(modes)]
        gain = [spread(gain_ref, m, lanes) for m in range(modes)]
        skip = spread(skip_ref, 0, lanes)

        def step(i, now):
            place = strided(span - 1 - i, span)
            g = back_ref[tile, place]
            now = [decay[m] * now[m] + g for m in range(modes)]
            drive_grad_ref[tile, place] = tree_sum([gain[m] * now[m] for m in range(modes)]) + skip * g
            return now

        first = [lead_ref[tile, strided(m, modes)] for m in range(modes)]
        lax.fori_loop(0, span, step, first, unroll=8)
        drive_grad = drive_grad_ref[tile]
        grad_key_ref[:, lanes] = (drive_grad * value_ref[:, lanes].astype(F32)).astype(BF16)
        grad_value_ref[:, lanes] = (drive_grad * key_ref[:, lanes].astype(F32)).astype(BF16)


def call(body, args, outs, scratch, micros, name):
    whole = pl.BlockSpec(memory_space=pltpu.VMEM)
    return pl.pallas_call(
        body,
        out_shape=[jax.ShapeDtypeStruct(o.shape, o.dtype) for o in outs],
        in_specs=[whole] * len(args),
        out_specs=[whole] * len(outs),
        scratch_shapes=[pltpu.VMEM(shape, F32) for shape in scratch],
        compiler_params=pltpu.CompilerParams(vmem_limit_bytes=6 * 2**20),
        cost_estimate=pl.CostEstimate(flops=int(micros * 1.15e9), bytes_accessed=0, transcendentals=0),
        name=name,
    )(*args)


def like(shape, dtype):
    return jax.ShapeDtypeStruct(shape, dtype)


def spread_over_x(value):
    return [value] + [hop(value, x=offset) for offset in range(1, RING)]


def together(*values):
    return lax.optimization_barrier(values)


def local(queries, key_proj, value_proj, skip_gain, residue, log_decay, out_weight, cotangent):
    length, channels = queries.shape
    modes = residue.shape[0]
    blocks = lax.axis_size("seq")
    scale = 1.0 / math.sqrt(length * blocks)
    skip_row = skip_gain.reshape(1, channels)
    tiles = channels // LANES
    wide = like((tiles, length, LANES), F32)
    narrow = like((length, channels), BF16)
    table = (modes, channels)

    block = gather_z(cotangent)
    ends, subs, driving = call(
        forward_ends,
        (key_proj, value_proj, log_decay),
        (like((2 * modes, channels), F32), like((tiles, 2 * SUBS * modes, LANES), F32), wide),
        [table, (SUBS, LANES)],
        0.1,
        "forward_ends",
    )
    ends_pair = jnp.concatenate([ends, hop(ends, pair=1)])
    block, *earlier = together(block, *spread_over_x(ends_pair))
    main_block, other_block = hop(block, y=MAIN), hop(block, y=OTHER)
    gated, turned, pre_gate, lead = call(
        forward_full,
        (queries, driving, subs, log_decay, residue, skip_row, *earlier),
        (narrow, narrow, wide, like((tiles, 2 * SUBS * modes, LANES), F32)),
        [table, table],
        0.1,
        "forward_full",
    )
    main_block, other_block, turned = together(main_block, other_block, turned)
    far_block = hop(main_block, y=MAIN)
    near_first, near_rest, far_first, far_rest = project(turned, out_weight)
    far_block, far_rest, gated_other = together(far_block, far_rest, hop(gated, pair=1))
    got_first, far_rest = together(hop(far_first, core=1), far_rest)
    got_rest = hop(far_rest, core=1)
    gated_pair = jnp.concatenate([gated, gated_other])
    opposite = add(near_first, got_first).astype(BF16)
    cot_rows = place_blocks(block, main_block, other_block, far_block)
    cot_rows = cot_rows.reshape(2 * length, -1)

    _, _, core, low, x = places()
    half = out_weight.shape[1] // 2
    low_weight = lax.dynamic_slice(out_weight, (0, low * half), (channels, half))
    grad_parts = lax.dot_general(cot_rows, low_weight, (((1,), (1,)), ((), ())), preferred_element_type=F32)
    cot_rows, grad_parts, opposite = together(cot_rows, grad_parts, hop(opposite, y=MAIN))
    theirs = hop(grad_parts[length:].astype(BF16), pair=1)

    far_weight = weigh(gated_pair, cot_rows, scale, lax.rem(x + 2, RING))
    cot_rows, far_weight = together(cot_rows, far_weight)
    got_rest, _ = together(got_rest, far_weight)
    main_weight, other_weight, own_weight = (
        weigh(gated_pair, cot_rows, scale, lax.rem(x + r, RING)) for r in (1 + 2 * core, 3 - 2 * core, 0)
    )
    main, other, own = (add(a, b) for a, b in zip(jnp.split(near_rest, 3), jnp.split(got_rest, 3)))
    main = add(main, opposite).astype(BF16)
    main, other, main_weight, other_weight, own_weight = together(
        main, other.astype(BF16), main_weight, other_weight, own_weight
    )
    main, other = hop(main, y=MAIN), hop(other, y=OTHER)
    other_weight = hop(other_weight, x=OTHER)
    main_weight = add(main_weight, hop(far_weight, x=MAIN)).astype(BF16)

    theirs, main_weight = together(theirs, main_weight)
    grad_gated = add(grad_parts[:length], theirs)
    main_weight = hop(main_weight, x=MAIN)

    grad_query, back, sums, back_subs = call(
        backward_ends,
        (grad_gated, queries, pre_gate, driving, lead, log_decay),
        (narrow, wide, like((3 * modes + SUBS, channels), F32), like((tiles, SUBS * modes, LANES), F32)),
        [table, (tiles, 2 * SUBS * modes, LANES), (SUBS, LANES)],
        2.0,
        "backward_ends",
    )
    others = hop(sums, pair=1)
    others, main, other, main_weight, other_weight = together(others, main, other, main_weight, other_weight)
    own = add(own, main, other)
    part = own.shape[0] // 2
    leaving = hop(own[part:].astype(BF16), z=(2, -1))
    sums_pair = jnp.concatenate([sums[:modes], others[:modes], sums[modes:] + others[modes:]])
    all_sums = spread_over_x(sums_pair)
    leaving, *_ = together(leaving, *all_sums[1:])
    mixed = add(own[:part], by_core(leaving, hop(leaving, z=(None, -1)))).astype(BF16)
    grad_weight = add(own_weight, main_weight, other_weight).astype(BF16)
    grad_key, grad_value, grad_residue, grad_decay, grad_skip = call(
        functools.partial(backward_full, scale=scale),
        (key_proj, value_proj, back, back_subs, log_decay, residue, skip_row, *all_sums),
        (narrow, narrow, like(table, F32), like(table, F32), like((SUBS, channels), F32)),
        [table, table, (tiles, SUBS * modes, LANES), (tiles, length, LANES)],
        0.1,
        "backward_full",
    )
    return (
        mixed,
        grad_query,
        grad_key,
        grad_value,
        grad_weight,
        grad_residue,
        grad_decay,
        grad_skip[0],
    )


def solution(mesh):
    in_specs = (
        P("seq", "chan"),
        P("seq", "chan"),
        P("seq", "chan"),
        P("chan"),
        P(None, "chan"),
        P(None, "chan"),
        P("chan", None),
        P(("seq", "chan"), None),
    )
    out_specs = (
        P(("seq", "chan"), None),
        P("seq", "chan"),
        P("seq", "chan"),
        P("seq", "chan"),
        P("chan", "seq"),
        P(None, "chan"),
        P(None, "chan"),
        P("chan"),
    )
    return jax.shard_map(local, mesh=mesh, in_specs=in_specs, out_specs=out_specs, check_vma=False)
```

```python
import functools
import itertools
import math

import jax
import jax.numpy as jnp
from jax import lax
from jax.experimental import pallas as pl
from jax.experimental.pallas import tpu as pltpu
from jax.sharding import PartitionSpec as P

RING = 4
MAIN, OTHER = (1, -1), (-1, 1)
SUBS = 8
LANES = 128
F32 = jnp.float32
BF16 = jnp.bfloat16


def strided(first, step):
    return pl.ds(first, SUBS, stride=step)


def spread(ref, mode, lanes):
    return jnp.broadcast_to(ref[pl.ds(mode, 1), lanes], (SUBS, LANES))


def tree_sum(parts):
    while len(parts) > 1:
        parts = [a + b for a, b in zip(parts[::2], parts[1::2])] + parts[len(parts) & ~1 :]
    return parts[0]


def lane_tiles(channels):
    return [(tile, pl.ds(tile * LANES, LANES)) for tile in range(channels // LANES)]


def places():
    chan, seq = lax.axis_index("chan"), lax.axis_index("seq")
    return chan // 4, lax.rem(chan // 2, 2), lax.rem(chan, 2), seq // RING, lax.rem(seq, RING)


def hop(value, x=0, y=0, z=0, core=0, pair=0):
    moves = []
    for i, j, k, c in itertools.product(range(RING), range(RING), range(RING), range(2)):
        dx, dy, dz = (step[c] if isinstance(step, tuple) else step for step in (x, y, z))
        if None in (dx, dy, dz):
            continue
        there = ((i + dx) % RING, (j + dy) % RING, ((k + dz) % RING) ^ pair, c ^ core)
        moves.append(tuple(((b * 2 + d // 2) * 2 + e) * 2 * RING + d % 2 * RING + a for a, b, d, e in ((i, j, k, c), there)))
    return lax.ppermute(value, ("chan", "seq"), moves)


def by_core(first, second):
    return jnp.where(places()[2] == 0, first, second)


def gather_z(cotangent):
    _, high, _, low, _ = places()
    tokens, width = cotangent.shape
    half = width // 2
    mine = lax.dynamic_slice(cotangent, (0, low * half), (tokens, half))
    theirs = lax.dynamic_slice(cotangent, (0, (1 - low) * half), (tokens, half))
    above, below, across = hop(theirs, z=1), hop(theirs, z=-1), hop(mine, z=2)
    stack = jnp.where(high == 0, jnp.stack([mine, across]), jnp.stack([across, mine]))
    same, differ = jnp.where(low == 1, above, below), jnp.where(low == 1, below, above)
    other = jnp.where(high == 0, jnp.stack([same, differ]), jnp.stack([differ, same]))
    return jnp.stack([stack, other])


def put_in_place(*refs):
    gated_ref, gated_other_ref, *block_refs = refs[:-3]
    whole_ref, pair_ref, sems = refs[-3:]
    y, _, core, _, _ = places()
    rows = gated_ref.shape[0]
    copies = [
        pltpu.make_async_copy(gated_ref, pair_ref.at[pl.ds(0, rows)], sems.at[0]),
        pltpu.make_async_copy(gated_other_ref, pair_ref.at[pl.ds(rows, rows)], sems.at[1]),
    ]
    steps = ((0, 0), (RING - 1, 1), (1, RING - 1), (2, 2))
    for i, ref in enumerate(block_refs):
        at_core = core if i % 2 == 0 else 1 - core
        row = lax.rem(y + jnp.where(at_core == 0, *steps[i // 2]), RING)
        copies.append(pltpu.make_async_copy(ref, whole_ref.at[:, row, :, at_core], sems.at[2 + i]))
    for copy in copies:
        copy.start()
    for copy in copies:
        copy.wait()


def place_blocks(gated, gated_other, blocks):
    _, _, tokens, half = blocks[0].shape
    parts = [part for block in blocks for part in (block, hop(block, core=1))]
    rows, channels = gated.shape
    whole = (2, RING, 2, 2, tokens, half)
    moved = 4 * math.prod(whole)
    cot, pair = pl.pallas_call(
        put_in_place,
        out_shape=[jax.ShapeDtypeStruct(whole, BF16), jax.ShapeDtypeStruct((2 * rows, channels), BF16)],
        in_specs=[pl.BlockSpec(memory_space=pl.ANY)] * (2 + len(parts)),
        out_specs=[pl.BlockSpec(memory_space=pltpu.VMEM)] * 2,
        scratch_shapes=[pltpu.SemaphoreType.DMA((2 + len(parts),))],
        compiler_params=pltpu.CompilerParams(vmem_limit_bytes=16 * 2**20),
        cost_estimate=pl.CostEstimate(flops=0, bytes_accessed=moved, transcendentals=0),
        name="put_in_place",
    )(gated, gated_other, *parts)
    return cot.reshape(-1, half), pair


def add(*parts):
    return functools.reduce(jnp.add, [part.astype(F32) for part in parts])


def project_tile(rows_ref, weight_ref, *out_refs):
    product = jnp.dot(rows_ref[...], weight_ref[...], preferred_element_type=F32).astype(BF16)
    first = 0
    for ref in out_refs:
        ref[...] = product[first : first + ref.shape[0]]
        first += ref.shape[0]


def project(turned, out_weight):
    rows, depth = turned.shape
    width = out_weight.shape[1]
    tile = 1024
    sizes = [rows // 8, 3 * rows // 8] * 2
    return pl.pallas_call(
        project_tile,
        grid=(width // tile,),
        out_shape=[jax.ShapeDtypeStruct((size, width), BF16) for size in sizes],
        in_specs=[pl.BlockSpec((rows, depth), lambda i: (0, 0)), pl.BlockSpec((depth, tile), lambda i: (0, i))],
        out_specs=[pl.BlockSpec((size, tile), lambda i: (0, i)) for size in sizes],
        compiler_params=pltpu.CompilerParams(vmem_limit_bytes=12 * 2**20),
        cost_estimate=pl.CostEstimate(
            flops=2 * rows * depth * width, bytes_accessed=2 * width * (rows + depth), transcendentals=0
        ),
        name="project",
    )(turned, out_weight)


def weigh(gated, cot_rows, scale, block):
    width = cot_rows.shape[1] // RING
    columns = lax.dynamic_slice(cot_rows, (0, block * width), (cot_rows.shape[0], width))
    product = lax.dot_general(gated, columns, (((0,), (0,)), ((), ())), preferred_element_type=F32)
    return (product * scale).astype(BF16)


def nearby(refs, distance, way, first, modes, lanes):
    _, _, _, low, x = places()
    before = x if way == 1 else RING - 1 - x
    other_counts = low == (way + 1) // 2
    other = refs[0].shape[0] // 2 if way == 1 else modes
    step = distance % RING
    ref = refs[way * step % RING]
    mine = ref[pl.ds(first, modes), lanes]
    theirs = jnp.where(other_counts, ref[pl.ds(other + first, modes), lanes], 0.0)
    if distance < RING:
        return jnp.where(step <= before, mine, theirs)
    return jnp.where(step <= before, theirs, 0.0)


def forward_ends(key_ref, value_ref, log_ref, ends_ref, sub_ref, drive_ref, decay_ref, zero_ref):
    length, channels = key_ref.shape
    modes = log_ref.shape[0]
    span = length // SUBS
    decay_ref[...] = jnp.exp(-jnp.exp(log_ref[...]))
    zero_ref[...] = jnp.zeros_like(zero_ref)
    for tile, lanes in lane_tiles(channels):
        drive_ref[tile] = key_ref[:, lanes].astype(F32) * value_ref[:, lanes].astype(F32)
        decay = [spread(decay_ref, m, lanes) for m in range(modes)]

        def step(i, carry):
            now, lag = carry
            u = drive_ref[tile, strided(i, span)]
            lag = [decay[m] * (lag[m] + now[m]) for m in range(modes)]
            now = [decay[m] * now[m] + u for m in range(modes)]
            return now, lag

        zero = [zero_ref[...]] * modes
        now, lag = lax.fori_loop(0, span, step, (zero, zero), unroll=8)
        for m in range(modes):
            sub_ref[tile, strided(m, modes)] = now[m]
            sub_ref[tile, strided(SUBS * modes + m, modes)] = lag[m]
        power = jnp.exp(-span * jnp.exp(log_ref[:, lanes]))
        state = jnp.zeros_like(power)
        lagged = jnp.zeros_like(power)
        for j in range(SUBS):
            lagged = power * (lagged + span * state) + sub_ref[tile, pl.ds((SUBS + j) * modes, modes)]
            state = power * state + sub_ref[tile, pl.ds(j * modes, modes)]
        ends_ref[pl.ds(0, modes), lanes] = state
        ends_ref[pl.ds(modes, modes), lanes] = lagged


def forward_full(*refs):
    (query_ref, drive_ref, sub_ref, log_ref, residue_ref, skip_ref, *end_refs) = refs[:-6]
    (gated_ref, turned_ref, pre_ref, lead_ref, decay_ref, gain_ref) = refs[-6:]
    length, channels = query_ref.shape
    modes = log_ref.shape[0]
    span = length // SUBS
    rate = jnp.exp(log_ref[...])
    decay_ref[...] = jnp.exp(-rate)
    gain_ref[...] = residue_ref[...] * jnp.sqrt(2.0 * rate)
    for tile, lanes in lane_tiles(channels):
        rate = jnp.exp(log_ref[:, lanes])
        stretch = jnp.exp(-length * rate)
        power = jnp.exp(-span * rate)
        state = jnp.zeros_like(rate)
        lagged = jnp.zeros_like(rate)
        for distance in range(2 * RING - 1, 0, -1):
            lagged = stretch * (lagged + length * state) + nearby(end_refs, distance, 1, modes, modes, lanes)
            state = stretch * state + nearby(end_refs, distance, 1, 0, modes, lanes)
        for j in range(SUBS):
            now_rows, lag_rows = (pl.ds((j + k) * modes, modes) for k in (0, SUBS))
            lead_ref[tile, now_rows] = state
            lead_ref[tile, lag_rows] = lagged
            lagged = power * (lagged + span * state) + sub_ref[tile, lag_rows]
            state = power * state + sub_ref[tile, now_rows]
        decay = [spread(decay_ref, m, lanes) for m in range(modes)]
        gain = [spread(gain_ref, m, lanes) for m in range(modes)]
        skip = spread(skip_ref, 0, lanes)

        def step(i, now):
            place = strided(i, span)
            u = drive_ref[tile, place]
            now = [decay[m] * now[m] + u for m in range(modes)]
            pre_ref[tile, place] = tree_sum([gain[m] * now[m] for m in range(modes)]) + skip * u
            return now

        first = [lead_ref[tile, strided(m, modes)] for m in range(modes)]
        lax.fori_loop(0, span, step, first, unroll=8)
        gated_ref[:, lanes] = (query_ref[:, lanes].astype(F32) * pre_ref[tile]).astype(BF16)
    part = length // (RING * 4)
    y, high, core, _, _ = places()
    for i in range(RING * 4):
        on = lax.rem(i // 4 + RING - y, RING)
        kept = lax.rem(i % 2 + core, 2) == 0
        first = jnp.where(kept, 1 + 2 * core, 3 - 2 * core)
        there = jnp.where(on == 0, 3, jnp.where(on == 2, 0, jnp.where(on == first, 1, 2)))
        there = there + jnp.where(kept, 0, RING)
        there = there * 2 + lax.rem(i // 2 % 2 + high, 2)
        turned_ref[pl.ds(pl.multiple_of(there * part, part), part)] = gated_ref[pl.ds(i * part, part)]


def backward_ends(
    grad_ref, query_ref, pre_ref, drive_ref, lead_ref, log_ref,
    grad_query_ref, back_ref, sums_ref, sub_ref, decay_ref, part_ref, zero_ref,
):
    length, channels = query_ref.shape
    modes = log_ref.shape[0]
    span = length // SUBS
    half = modes // 2
    decay_ref[...] = jnp.exp(-jnp.exp(log_ref[...]))
    zero_ref[...] = jnp.zeros_like(zero_ref)
    for tile, lanes in lane_tiles(channels):
        grad = grad_ref[:, lanes].astype(F32)
        grad_query_ref[:, lanes] = (grad * pre_ref[tile]).astype(BF16)
        back_ref[tile] = grad * query_ref[:, lanes].astype(F32)
        decay = [spread(decay_ref, m, lanes) for m in range(modes)]

        def back_step(i, now):
            g = back_ref[tile, strided(span - 1 - i, span)]
            return [decay[m] * now[m] + g for m in range(modes)]

        zero = [zero_ref[...]] * modes
        now = lax.fori_loop(0, span, back_step, zero, unroll=8)
        for m in range(modes):
            sub_ref[tile, strided(m, modes)] = now[m]
        for low in range(0, modes, half):
            group = range(low, low + half)
            decay = [spread(decay_ref, m, lanes) for m in group]

            def pair_step(i, carry):
                state, lag, pair, lag_pair, skip = carry
                place = strided(i, span)
                u = drive_ref[tile, place]
                g = back_ref[tile, place]
                lag = [decay[m] * (lag[m] + state[m]) for m in range(half)]
                state = [decay[m] * state[m] + u for m in range(half)]
                pair = [pair[m] + g * state[m] for m in range(half)]
                lag_pair = [lag_pair[m] + g * lag[m] for m in range(half)]
                return state, lag, pair, lag_pair, skip + g * u

            state = [lead_ref[tile, strided(m, modes)] for m in group]
            lag = [lead_ref[tile, strided(SUBS * modes + m, modes)] for m in group]
            zero = [zero_ref[...]] * half
            state, lag, pair, lag_pair, skip = lax.fori_loop(
                0, span, pair_step, (state, lag, zero, zero, zero[0]), unroll=8
            )
            for m in range(half):
                part_ref[tile, strided(low + m, modes)] = pair[m]
                part_ref[tile, strided(SUBS * modes + low + m, modes)] = lag_pair[m]
        total = jnp.sum(skip, axis=0, keepdims=True)
        sums_ref[pl.ds(3 * modes, SUBS), lanes] = jnp.broadcast_to(total, (SUBS, LANES))
        power = jnp.exp(-span * jnp.exp(log_ref[:, lanes]))
        start = jnp.zeros_like(power)
        pair = jnp.zeros_like(power)
        lag_pair = jnp.zeros_like(power)
        for j in range(SUBS - 1, -1, -1):
            start = power * start + sub_ref[tile, pl.ds(j * modes, modes)]
            pair = pair + part_ref[tile, pl.ds(j * modes, modes)]
            lag_pair = lag_pair + part_ref[tile, pl.ds((SUBS + j) * modes, modes)]
        sums_ref[pl.ds(0, modes), lanes] = start
        sums_ref[pl.ds(modes, modes), lanes] = pair
        sums_ref[pl.ds(2 * modes, modes), lanes] = lag_pair


def backward_full(*refs, scale):
    (key_ref, value_ref, back_ref, sub_ref, log_ref, residue_ref, skip_ref, *sum_refs) = refs[:-9]
    (grad_key_ref, grad_value_ref, grad_residue_ref, grad_decay_ref, grad_skip_ref) = refs[-9:-4]
    (decay_ref, gain_ref, lead_ref, drive_grad_ref) = refs[-4:]
    length, channels = key_ref.shape
    modes = log_ref.shape[0]
    span = length // SUBS
    rate = jnp.exp(log_ref[...])
    norm = jnp.sqrt(2.0 * rate)
    gain = residue_ref[...] * norm
    decay_ref[...] = jnp.exp(-rate)
    gain_ref[...] = gain
    pair = tree_sum([ref[pl.ds(2 * modes, modes)] for ref in sum_refs])
    lag_pair = tree_sum([ref[pl.ds(3 * modes, modes)] for ref in sum_refs])
    grad_residue_ref[...] = norm * pair * scale
    grad_decay_ref[...] = gain * (0.5 * pair - rate * lag_pair) * scale
    grad_skip_ref[...] = tree_sum([ref[pl.ds(4 * modes, SUBS)] for ref in sum_refs]) * scale
    for tile, lanes in lane_tiles(channels):
        rate = jnp.exp(log_ref[:, lanes])
        stretch = jnp.exp(-length * rate)
        power = jnp.exp(-span * rate)
        start = jnp.zeros_like(rate)
        for distance in range(2 * RING - 1, 0, -1):
            start = stretch * start + nearby(sum_refs, distance, -1, 0, modes, lanes)
        for j in range(SUBS - 1, -1, -1):
            lead_ref[tile, pl.ds(j * modes, modes)] = start
            start = power * start + sub_ref[tile, pl.ds(j * modes, modes)]
        decay = [spread(decay_ref, m, lanes) for m in range(modes)]
        gain = [spread(gain_ref, m, lanes) for m in range(modes)]
        skip = spread(skip_ref, 0, lanes)

        def step(i, now):
            place = strided(span - 1 - i, span)
            g = back_ref[tile, place]
            now = [decay[m] * now[m] + g for m in range(modes)]
            drive_grad_ref[tile, place] = tree_sum([gain[m] * now[m] for m in range(modes)]) + skip * g
            return now

        first = [lead_ref[tile, strided(m, modes)] for m in range(modes)]
        lax.fori_loop(0, span, step, first, unroll=8)
        drive_grad = drive_grad_ref[tile]
        grad_key_ref[:, lanes] = (drive_grad * value_ref[:, lanes].astype(F32)).astype(BF16)
        grad_value_ref[:, lanes] = (drive_grad * key_ref[:, lanes].astype(F32)).astype(BF16)


def call(body, args, outs, scratch, micros, name):
    whole = pl.BlockSpec(memory_space=pltpu.VMEM)
    return pl.pallas_call(
        body,
        out_shape=[jax.ShapeDtypeStruct(o.shape, o.dtype) for o in outs],
        in_specs=[whole] * len(args),
        out_specs=[whole] * len(outs),
        scratch_shapes=[pltpu.VMEM(shape, F32) for shape in scratch],
        compiler_params=pltpu.CompilerParams(vmem_limit_bytes=6 * 2**20),
        cost_estimate=pl.CostEstimate(flops=int(micros * 1.15e9), bytes_accessed=0, transcendentals=0),
        name=name,
    )(*args)


def like(shape, dtype):
    return jax.ShapeDtypeStruct(shape, dtype)


def spread_over_x(value):
    return [value] + [hop(value, x=offset) for offset in range(1, RING)]


def together(*values):
    return lax.optimization_barrier(values)


def local(queries, key_proj, value_proj, skip_gain, residue, log_decay, out_weight, cotangent):
    length, channels = queries.shape
    modes = residue.shape[0]
    blocks = lax.axis_size("seq")
    scale = 1.0 / math.sqrt(length * blocks)
    skip_row = skip_gain.reshape(1, channels)
    tiles = channels // LANES
    wide = like((tiles, length, LANES), F32)
    narrow = like((length, channels), BF16)
    table = (modes, channels)

    block = gather_z(cotangent)
    ends, subs, driving = call(
        forward_ends,
        (key_proj, value_proj, log_decay),
        (like((2 * modes, channels), F32), like((tiles, 2 * SUBS * modes, LANES), F32), wide),
        [table, (SUBS, LANES)],
        0.1,
        "forward_ends",
    )
    ends_pair = jnp.concatenate([ends, hop(ends, pair=1)])
    block, *earlier = together(block, *spread_over_x(ends_pair))
    main_block, other_block = hop(block, y=MAIN), hop(block, y=OTHER)
    gated, turned, pre_gate, lead = call(
        forward_full,
        (queries, driving, subs, log_decay, residue, skip_row, *earlier),
        (narrow, narrow, wide, like((tiles, 2 * SUBS * modes, LANES), F32)),
        [table, table],
        0.1,
        "forward_full",
    )
    main_block, other_block, turned = together(main_block, other_block, turned)
    far_block = hop(main_block, y=MAIN)
    near_first, near_rest, far_first, far_rest = project(turned, out_weight)
    far_block, far_rest, gated_other = together(far_block, far_rest, hop(gated, pair=1))
    got_first, far_rest = together(hop(far_first, core=1), far_rest)
    got_rest = hop(far_rest, core=1)
    opposite = add(near_first, got_first).astype(BF16)
    cot_rows, gated_pair = place_blocks(gated, gated_other, (block, main_block, other_block, far_block))

    _, _, core, low, x = places()
    half = out_weight.shape[1] // 2
    low_weight = lax.dynamic_slice(out_weight, (0, low * half), (channels, half))
    grad_parts = lax.dot_general(cot_rows, low_weight, (((1,), (1,)), ((), ())), preferred_element_type=F32)
    cot_rows, grad_parts, opposite = together(cot_rows, grad_parts, hop(opposite, y=MAIN))
    theirs = hop(grad_parts[length:].astype(BF16), pair=1)

    far_weight = weigh(gated_pair, cot_rows, scale, lax.rem(x + 2, RING))
    cot_rows, far_weight = together(cot_rows, far_weight)
    got_rest, _ = together(got_rest, far_weight)
    main_weight, other_weight, own_weight = (
        weigh(gated_pair, cot_rows, scale, lax.rem(x + r, RING)) for r in (1 + 2 * core, 3 - 2 * core, 0)
    )
    main, other, own = (add(a, b) for a, b in zip(jnp.split(near_rest, 3), jnp.split(got_rest, 3)))
    main = add(main, opposite).astype(BF16)
    main, other, main_weight, other_weight, own_weight = together(
        main, other.astype(BF16), main_weight, other_weight, own_weight
    )
    main, other = hop(main, y=MAIN), hop(other, y=OTHER)
    other_weight = hop(other_weight, x=OTHER)
    main_weight = add(main_weight, hop(far_weight, x=MAIN)).astype(BF16)

    theirs, main_weight = together(theirs, main_weight)
    grad_gated = add(grad_parts[:length], theirs)
    main_weight = hop(main_weight, x=MAIN)

    grad_query, back, sums, back_subs = call(
        backward_ends,
        (grad_gated, queries, pre_gate, driving, lead, log_decay),
        (narrow, wide, like((3 * modes + SUBS, channels), F32), like((tiles, SUBS * modes, LANES), F32)),
        [table, (tiles, 2 * SUBS * modes, LANES), (SUBS, LANES)],
        0.1,
        "backward_ends",
    )
    sums, main, other = together(sums, main, other)
    others = hop(sums, pair=1)
    others, main, other, main_weight, other_weight = together(others, main, other, main_weight, other_weight)
    own = add(own, main, other)
    part = own.shape[0] // 2
    leaving = hop(own[part:].astype(BF16), z=(2, -1))
    sums_pair = jnp.concatenate([sums[:modes], others[:modes], sums[modes:] + others[modes:]])
    all_sums = spread_over_x(sums_pair)
    leaving, *_ = together(leaving, *all_sums[1:])
    mixed = add(own[:part], by_core(leaving, hop(leaving, z=(None, -1)))).astype(BF16)
    grad_weight = add(own_weight, main_weight, other_weight).astype(BF16)
    grad_key, grad_value, grad_residue, grad_decay, grad_skip = call(
        functools.partial(backward_full, scale=scale),
        (key_proj, value_proj, back, back_subs, log_decay, residue, skip_row, *all_sums),
        (narrow, narrow, like(table, F32), like(table, F32), like((SUBS, channels), F32)),
        [table, table, (tiles, SUBS * modes, LANES), (tiles, length, LANES)],
        0.1,
        "backward_full",
    )
    return (
        mixed,
        grad_query,
        grad_key,
        grad_value,
        grad_weight,
        grad_residue,
        grad_decay,
        grad_skip[0],
    )


def solution(mesh):
    in_specs = (
        P("seq", "chan"),
        P("seq", "chan"),
        P("seq", "chan"),
        P("chan"),
        P(None, "chan"),
        P(None, "chan"),
        P("chan", None),
        P(("seq", "chan"), None),
    )
    out_specs = (
        P(("seq", "chan"), None),
        P("seq", "chan"),
        P("seq", "chan"),
        P("seq", "chan"),
        P("chan", "seq"),
        P(None, "chan"),
        P(None, "chan"),
        P("chan"),
    )
    return jax.shard_map(local, mesh=mesh, in_specs=in_specs, out_specs=out_specs, check_vma=False)
```

```python
import functools
import itertools
import math

import jax
import jax.numpy as jnp
from jax import lax
from jax.experimental import pallas as pl
from jax.experimental.pallas import tpu as pltpu
from jax.sharding import PartitionSpec as P

RING = 4
MAIN, OTHER = (1, -1), (-1, 1)
SUBS = 8
LANES = 128
F32 = jnp.float32
BF16 = jnp.bfloat16


def strided(first, step):
    return pl.ds(first, SUBS, stride=step)


def spread(ref, mode, lanes):
    return jnp.broadcast_to(ref[pl.ds(mode, 1), lanes], (SUBS, LANES))


def tree_sum(parts):
    while len(parts) > 1:
        parts = [a + b for a, b in zip(parts[::2], parts[1::2])] + parts[len(parts) & ~1 :]
    return parts[0]


def lane_tiles(channels):
    return [(tile, pl.ds(tile * LANES, LANES)) for tile in range(channels // LANES)]


def places():
    chan, seq = lax.axis_index("chan"), lax.axis_index("seq")
    return chan // 4, lax.rem(chan // 2, 2), lax.rem(chan, 2), seq // RING, lax.rem(seq, RING)


def hop(value, x=0, y=0, z=0, core=0, pair=0):
    moves = []
    for i, j, k, c in itertools.product(range(RING), range(RING), range(RING), range(2)):
        dx, dy, dz = (step[c] if isinstance(step, tuple) else step for step in (x, y, z))
        if None in (dx, dy, dz):
            continue
        there = ((i + dx) % RING, (j + dy) % RING, ((k + dz) % RING) ^ pair, c ^ core)
        moves.append(tuple(((b * 2 + d // 2) * 2 + e) * 2 * RING + d % 2 * RING + a for a, b, d, e in ((i, j, k, c), there)))
    return lax.ppermute(value, ("chan", "seq"), moves)


def by_core(first, second):
    return jnp.where(places()[2] == 0, first, second)


def gather_z(cotangent):
    _, high, _, low, _ = places()
    tokens, width = cotangent.shape
    half = width // 2
    mine = lax.dynamic_slice(cotangent, (0, low * half), (tokens, half))
    theirs = lax.dynamic_slice(cotangent, (0, (1 - low) * half), (tokens, half))
    above, below, across = hop(theirs, z=1), hop(theirs, z=-1), hop(mine, z=2)
    stack = jnp.where(high == 0, jnp.stack([mine, across]), jnp.stack([across, mine]))
    same, differ = jnp.where(low == 1, above, below), jnp.where(low == 1, below, above)
    other = jnp.where(high == 0, jnp.stack([same, differ]), jnp.stack([differ, same]))
    return jnp.stack([stack, other])


def put_in_place(*refs, spots):
    gated_ref, gated_other_ref, *block_refs = refs[:-3]
    whole_ref, pair_ref, sems = refs[-3:]
    y, _, core, _, _ = places()
    rows = gated_ref.shape[0]
    copies = [
        pltpu.make_async_copy(gated_ref, pair_ref.at[pl.ds(0, rows)], sems.at[0]),
        pltpu.make_async_copy(gated_other_ref, pair_ref.at[pl.ds(rows, rows)], sems.at[1]),
    ]
    for i, (ref, (first, steps)) in enumerate(zip(block_refs, spots)):
        at_core = core if i % 2 == 0 else 1 - core
        row = lax.rem(y + jnp.where(at_core == 0, *steps), RING)
        spot = whole_ref.at[pl.ds(first, ref.shape[0]), row, :, at_core]
        copies.append(pltpu.make_async_copy(ref, spot, sems.at[2 + i]))
    for copy in copies:
        copy.start()
    for copy in copies:
        copy.wait()


def place_blocks(gated, gated_other, own, main, other, far):
    _, _, tokens, half = own.shape
    blocks = [(own, 0, (0, 0)), (main, 0, (RING - 1, 1))]
    blocks += [(part, i, (1, RING - 1)) for i, part in enumerate(other)] + [(far, 0, (2, 2))]
    parts = [part for block, _, _ in blocks for part in (block, hop(block, core=1))]
    spots = [(first, steps) for _, first, steps in blocks for _ in range(2)]
    rows, channels = gated.shape
    whole = (2, RING, 2, 2, tokens, half)
    moved = 4 * math.prod(whole)
    cot, pair = pl.pallas_call(
        functools.partial(put_in_place, spots=spots),
        out_shape=[jax.ShapeDtypeStruct(whole, BF16), jax.ShapeDtypeStruct((2 * rows, channels), BF16)],
        in_specs=[pl.BlockSpec(memory_space=pl.ANY)] * (2 + len(parts)),
        out_specs=[pl.BlockSpec(memory_space=pltpu.VMEM)] * 2,
        scratch_shapes=[pltpu.SemaphoreType.DMA((2 + len(parts),))],
        compiler_params=pltpu.CompilerParams(vmem_limit_bytes=2 * 2**20),
        cost_estimate=pl.CostEstimate(flops=0, bytes_accessed=moved, transcendentals=0),
        name="put_in_place",
    )(gated, gated_other, *parts)
    return cot.reshape(-1, half), pair


def add(*parts):
    return functools.reduce(jnp.add, [part.astype(F32) for part in parts])


def project_tile(rows_ref, weight_ref, *out_refs):
    product = jnp.dot(rows_ref[...], weight_ref[...], preferred_element_type=F32).astype(BF16)
    first = 0
    for ref in out_refs:
        ref[...] = product[first : first + ref.shape[0]]
        first += ref.shape[0]


def project(turned, out_weight):
    rows, depth = turned.shape
    width = out_weight.shape[1]
    tile = 1024
    sizes = [rows // 8, 3 * rows // 8] * 2
    return pl.pallas_call(
        project_tile,
        grid=(width // tile,),
        out_shape=[jax.ShapeDtypeStruct((size, width), BF16) for size in sizes],
        in_specs=[pl.BlockSpec((rows, depth), lambda i: (0, 0)), pl.BlockSpec((depth, tile), lambda i: (0, i))],
        out_specs=[pl.BlockSpec((size, tile), lambda i: (0, i)) for size in sizes],
        compiler_params=pltpu.CompilerParams(vmem_limit_bytes=10 * 2**20),
        cost_estimate=pl.CostEstimate(
            flops=2 * rows * depth * width, bytes_accessed=2 * width * (rows + depth), transcendentals=0
        ),
        name="project",
    )(turned, out_weight)


def weigh(gated, cot_rows, scale, block):
    width = cot_rows.shape[1] // RING
    columns = lax.dynamic_slice(cot_rows, (0, block * width), (cot_rows.shape[0], width))
    product = lax.dot_general(gated, columns, (((0,), (0,)), ((), ())), preferred_element_type=F32)
    return (product * scale).astype(BF16)


def nearby(refs, distance, way, first, modes, lanes):
    _, _, _, low, x = places()
    before = x if way == 1 else RING - 1 - x
    other_counts = low == (way + 1) // 2
    other = refs[0].shape[0] // 2 if way == 1 else modes
    step = distance % RING
    ref = refs[way * step % RING]
    mine = ref[pl.ds(first, modes), lanes]
    theirs = jnp.where(other_counts, ref[pl.ds(other + first, modes), lanes], 0.0)
    if distance < RING:
        return jnp.where(step <= before, mine, theirs)
    return jnp.where(step <= before, theirs, 0.0)


def forward_ends(key_ref, value_ref, log_ref, ends_ref, sub_ref, drive_ref, decay_ref, zero_ref):
    length, channels = key_ref.shape
    modes = log_ref.shape[0]
    span = length // SUBS
    decay_ref[...] = jnp.exp(-jnp.exp(log_ref[...]))
    zero_ref[...] = jnp.zeros_like(zero_ref)
    for tile, lanes in lane_tiles(channels):
        drive_ref[tile] = key_ref[:, lanes].astype(F32) * value_ref[:, lanes].astype(F32)
        decay = [spread(decay_ref, m, lanes) for m in range(modes)]

        def step(i, carry):
            now, lag = carry
            u = drive_ref[tile, strided(i, span)]
            lag = [decay[m] * (lag[m] + now[m]) for m in range(modes)]
            now = [decay[m] * now[m] + u for m in range(modes)]
            return now, lag

        zero = [zero_ref[...]] * modes
        now, lag = lax.fori_loop(0, span, step, (zero, zero), unroll=8)
        for m in range(modes):
            sub_ref[tile, strided(m, modes)] = now[m]
            sub_ref[tile, strided(SUBS * modes + m, modes)] = lag[m]
        power = jnp.exp(-span * jnp.exp(log_ref[:, lanes]))
        state = jnp.zeros_like(power)
        lagged = jnp.zeros_like(power)
        for j in range(SUBS):
            lagged = power * (lagged + span * state) + sub_ref[tile, pl.ds((SUBS + j) * modes, modes)]
            state = power * state + sub_ref[tile, pl.ds(j * modes, modes)]
        ends_ref[pl.ds(0, modes), lanes] = state
        ends_ref[pl.ds(modes, modes), lanes] = lagged


def forward_full(*refs):
    (query_ref, drive_ref, sub_ref, log_ref, residue_ref, skip_ref, *end_refs) = refs[:-6]
    (gated_ref, turned_ref, pre_ref, lead_ref, decay_ref, gain_ref) = refs[-6:]
    length, channels = query_ref.shape
    modes = log_ref.shape[0]
    span = length // SUBS
    rate = jnp.exp(log_ref[...])
    decay_ref[...] = jnp.exp(-rate)
    gain_ref[...] = residue_ref[...] * jnp.sqrt(2.0 * rate)
    for tile, lanes in lane_tiles(channels):
        rate = jnp.exp(log_ref[:, lanes])
        stretch = jnp.exp(-length * rate)
        power = jnp.exp(-span * rate)
        state = jnp.zeros_like(rate)
        lagged = jnp.zeros_like(rate)
        for distance in range(2 * RING - 1, 0, -1):
            lagged = stretch * (lagged + length * state) + nearby(end_refs, distance, 1, modes, modes, lanes)
            state = stretch * state + nearby(end_refs, distance, 1, 0, modes, lanes)
        for j in range(SUBS):
            now_rows, lag_rows = (pl.ds((j + k) * modes, modes) for k in (0, SUBS))
            lead_ref[tile, now_rows] = state
            lead_ref[tile, lag_rows] = lagged
            lagged = power * (lagged + span * state) + sub_ref[tile, lag_rows]
            state = power * state + sub_ref[tile, now_rows]
        decay = [spread(decay_ref, m, lanes) for m in range(modes)]
        gain = [spread(gain_ref, m, lanes) for m in range(modes)]
        skip = spread(skip_ref, 0, lanes)

        def step(i, now):
            place = strided(i, span)
            u = drive_ref[tile, place]
            now = [decay[m] * now[m] + u for m in range(modes)]
            pre_ref[tile, place] = tree_sum([gain[m] * now[m] for m in range(modes)]) + skip * u
            return now

        first = [lead_ref[tile, strided(m, modes)] for m in range(modes)]
        lax.fori_loop(0, span, step, first, unroll=8)
        gated_ref[:, lanes] = (query_ref[:, lanes].astype(F32) * pre_ref[tile]).astype(BF16)
    part = length // (RING * 4)
    y, high, core, _, _ = places()
    for i in range(RING * 4):
        on = lax.rem(i // 4 + RING - y, RING)
        kept = lax.rem(i % 2 + core, 2) == 0
        first = jnp.where(kept, 1 + 2 * core, 3 - 2 * core)
        there = jnp.where(on == 0, 3, jnp.where(on == 2, 0, jnp.where(on == first, 1, 2)))
        there = there + jnp.where(kept, 0, RING)
        there = there * 2 + lax.rem(i // 2 % 2 + high, 2)
        turned_ref[pl.ds(pl.multiple_of(there * part, part), part)] = gated_ref[pl.ds(i * part, part)]


def backward_ends(
    grad_ref, query_ref, pre_ref, drive_ref, lead_ref, log_ref,
    grad_query_ref, back_ref, sums_ref, sub_ref, decay_ref, part_ref, zero_ref,
):
    length, channels = query_ref.shape
    modes = log_ref.shape[0]
    span = length // SUBS
    half = modes // 2
    decay_ref[...] = jnp.exp(-jnp.exp(log_ref[...]))
    zero_ref[...] = jnp.zeros_like(zero_ref)
    for tile, lanes in lane_tiles(channels):
        grad = grad_ref[:, lanes].astype(F32)
        grad_query_ref[:, lanes] = (grad * pre_ref[tile]).astype(BF16)
        back_ref[tile] = grad * query_ref[:, lanes].astype(F32)
        decay = [spread(decay_ref, m, lanes) for m in range(modes)]

        def back_step(i, now):
            g = back_ref[tile, strided(span - 1 - i, span)]
            return [decay[m] * now[m] + g for m in range(modes)]

        zero = [zero_ref[...]] * modes
        now = lax.fori_loop(0, span, back_step, zero, unroll=8)
        for m in range(modes):
            sub_ref[tile, strided(m, modes)] = now[m]
        for low in range(0, modes, half):
            group = range(low, low + half)
            decay = [spread(decay_ref, m, lanes) for m in group]

            def pair_step(i, carry):
                state, lag, pair, lag_pair, skip = carry
                place = strided(i, span)
                u = drive_ref[tile, place]
                g = back_ref[tile, place]
                lag = [decay[m] * (lag[m] + state[m]) for m in range(half)]
                state = [decay[m] * state[m] + u for m in range(half)]
                pair = [pair[m] + g * state[m] for m in range(half)]
                lag_pair = [lag_pair[m] + g * lag[m] for m in range(half)]
                return state, lag, pair, lag_pair, skip + g * u

            state = [lead_ref[tile, strided(m, modes)] for m in group]
            lag = [lead_ref[tile, strided(SUBS * modes + m, modes)] for m in group]
            zero = [zero_ref[...]] * half
            state, lag, pair, lag_pair, skip = lax.fori_loop(
                0, span, pair_step, (state, lag, zero, zero, zero[0]), unroll=8
            )
            for m in range(half):
                part_ref[tile, strided(low + m, modes)] = pair[m]
                part_ref[tile, strided(SUBS * modes + low + m, modes)] = lag_pair[m]
        total = jnp.sum(skip, axis=0, keepdims=True)
        sums_ref[pl.ds(3 * modes, SUBS), lanes] = jnp.broadcast_to(total, (SUBS, LANES))
        power = jnp.exp(-span * jnp.exp(log_ref[:, lanes]))
        start = jnp.zeros_like(power)
        pair = jnp.zeros_like(power)
        lag_pair = jnp.zeros_like(power)
        for j in range(SUBS - 1, -1, -1):
            start = power * start + sub_ref[tile, pl.ds(j * modes, modes)]
            pair = pair + part_ref[tile, pl.ds(j * modes, modes)]
            lag_pair = lag_pair + part_ref[tile, pl.ds((SUBS + j) * modes, modes)]
        sums_ref[pl.ds(0, modes), lanes] = start
        sums_ref[pl.ds(modes, modes), lanes] = pair
        sums_ref[pl.ds(2 * modes, modes), lanes] = lag_pair


def backward_full(*refs, scale):
    (key_ref, value_ref, back_ref, sub_ref, log_ref, residue_ref, skip_ref, *sum_refs) = refs[:-9]
    (grad_key_ref, grad_value_ref, grad_residue_ref, grad_decay_ref, grad_skip_ref) = refs[-9:-4]
    (decay_ref, gain_ref, lead_ref, drive_grad_ref) = refs[-4:]
    length, channels = key_ref.shape
    modes = log_ref.shape[0]
    span = length // SUBS
    rate = jnp.exp(log_ref[...])
    norm = jnp.sqrt(2.0 * rate)
    gain = residue_ref[...] * norm
    decay_ref[...] = jnp.exp(-rate)
    gain_ref[...] = gain
    pair = tree_sum([ref[pl.ds(2 * modes, modes)] for ref in sum_refs])
    lag_pair = tree_sum([ref[pl.ds(3 * modes, modes)] for ref in sum_refs])
    grad_residue_ref[...] = norm * pair * scale
    grad_decay_ref[...] = gain * (0.5 * pair - rate * lag_pair) * scale
    grad_skip_ref[...] = tree_sum([ref[pl.ds(4 * modes, SUBS)] for ref in sum_refs]) * scale
    for tile, lanes in lane_tiles(channels):
        rate = jnp.exp(log_ref[:, lanes])
        stretch = jnp.exp(-length * rate)
        power = jnp.exp(-span * rate)
        start = jnp.zeros_like(rate)
        for distance in range(2 * RING - 1, 0, -1):
            start = stretch * start + nearby(sum_refs, distance, -1, 0, modes, lanes)
        for j in range(SUBS - 1, -1, -1):
            lead_ref[tile, pl.ds(j * modes, modes)] = start
            start = power * start + sub_ref[tile, pl.ds(j * modes, modes)]
        decay = [spread(decay_ref, m, lanes) for m in range(modes)]
        gain = [spread(gain_ref, m, lanes) for m in range(modes)]
        skip = spread(skip_ref, 0, lanes)

        def step(i, now):
            place = strided(span - 1 - i, span)
            g = back_ref[tile, place]
            now = [decay[m] * now[m] + g for m in range(modes)]
            drive_grad_ref[tile, place] = tree_sum([gain[m] * now[m] for m in range(modes)]) + skip * g
            return now

        first = [lead_ref[tile, strided(m, modes)] for m in range(modes)]
        lax.fori_loop(0, span, step, first, unroll=8)
        drive_grad = drive_grad_ref[tile]
        grad_key_ref[:, lanes] = (drive_grad * value_ref[:, lanes].astype(F32)).astype(BF16)
        grad_value_ref[:, lanes] = (drive_grad * key_ref[:, lanes].astype(F32)).astype(BF16)


def call(body, args, outs, scratch, micros, name):
    whole = pl.BlockSpec(memory_space=pltpu.VMEM)
    return pl.pallas_call(
        body,
        out_shape=[jax.ShapeDtypeStruct(o.shape, o.dtype) for o in outs],
        in_specs=[whole] * len(args),
        out_specs=[whole] * len(outs),
        scratch_shapes=[pltpu.VMEM(shape, F32) for shape in scratch],
        compiler_params=pltpu.CompilerParams(vmem_limit_bytes=6 * 2**20),
        cost_estimate=pl.CostEstimate(flops=int(micros * 1.15e9), bytes_accessed=0, transcendentals=0),
        name=name,
    )(*args)


def like(shape, dtype):
    return jax.ShapeDtypeStruct(shape, dtype)


def spread_over_x(value):
    return [value] + [hop(value, x=offset) for offset in range(1, RING)]


def together(*values):
    return lax.optimization_barrier(values)


def local(queries, key_proj, value_proj, skip_gain, residue, log_decay, out_weight, cotangent):
    length, channels = queries.shape
    modes = residue.shape[0]
    blocks = lax.axis_size("seq")
    scale = 1.0 / math.sqrt(length * blocks)
    skip_row = skip_gain.reshape(1, channels)
    tiles = channels // LANES
    wide = like((tiles, length, LANES), F32)
    narrow = like((length, channels), BF16)
    table = (modes, channels)

    block = gather_z(cotangent)
    ends, subs, driving = call(
        forward_ends,
        (key_proj, value_proj, log_decay),
        (like((2 * modes, channels), F32), like((tiles, 2 * SUBS * modes, LANES), F32), wide),
        [table, (SUBS, LANES)],
        0.1,
        "forward_ends",
    )
    ends_pair = jnp.concatenate([ends, hop(ends, pair=1)])
    main_block = hop(block, y=MAIN)
    other_block = [hop(block[:1], y=OTHER), hop(block[1:], y=OTHER)]
    other_block[0], ends_pair = together(other_block[0], ends_pair)
    earlier = spread_over_x(ends_pair)
    gated, turned, pre_gate, lead = call(
        forward_full,
        (queries, driving, subs, log_decay, residue, skip_row, *earlier),
        (narrow, narrow, wide, like((tiles, 2 * SUBS * modes, LANES), F32)),
        [table, table],
        0.1,
        "forward_full",
    )
    block, gated = together(block, gated)
    main_block, other_block, turned, gated_other = together(main_block, other_block, turned, hop(gated, pair=1))
    far_block = hop(main_block, y=MAIN)
    near_first, near_rest, far_first, far_rest = project(turned, out_weight)
    far_block, far_rest = together(far_block, far_rest)
    got_first, far_rest = together(hop(far_first, core=1), far_rest)
    got_rest = hop(far_rest, core=1)
    opposite = add(near_first, got_first).astype(BF16)
    cot_rows, gated_pair = place_blocks(gated, gated_other, block, main_block, other_block, far_block)

    _, _, core, low, x = places()
    half = out_weight.shape[1] // 2
    low_weight = lax.dynamic_slice(out_weight, (0, low * half), (channels, half))
    grad_parts = lax.dot_general(cot_rows, low_weight, (((1,), (1,)), ((), ())), preferred_element_type=F32)
    cot_rows, grad_parts, opposite = together(cot_rows, grad_parts, hop(opposite, y=MAIN))
    theirs = hop(grad_parts[length:].astype(BF16), pair=1)

    far_weight = weigh(gated_pair, cot_rows, scale, lax.rem(x + 2, RING))
    cot_rows, far_weight = together(cot_rows, far_weight)
    got_rest, _ = together(got_rest, far_weight)
    main_weight, other_weight, own_weight = (
        weigh(gated_pair, cot_rows, scale, lax.rem(x + r, RING)) for r in (1 + 2 * core, 3 - 2 * core, 0)
    )
    main, other, own = (add(a, b) for a, b in zip(jnp.split(near_rest, 3), jnp.split(got_rest, 3)))
    main = add(main, opposite).astype(BF16)
    main, other, main_weight, other_weight, own_weight = together(
        main, other.astype(BF16), main_weight, other_weight, own_weight
    )
    main, other = hop(main, y=MAIN), hop(other, y=OTHER)
    other_weight = hop(other_weight, x=OTHER)
    main_weight = add(main_weight, hop(far_weight, x=MAIN)).astype(BF16)

    theirs, main_weight = together(theirs, main_weight)
    grad_gated = add(grad_parts[:length], theirs)
    main_weight = hop(main_weight, x=MAIN)

    grad_query, back, sums, back_subs = call(
        backward_ends,
        (grad_gated, queries, pre_gate, driving, lead, log_decay),
        (narrow, wide, like((3 * modes + SUBS, channels), F32), like((tiles, SUBS * modes, LANES), F32)),
        [table, (tiles, 2 * SUBS * modes, LANES), (SUBS, LANES)],
        0.1,
        "backward_ends",
    )
    sums, main, other = together(sums, main, other)
    others = hop(sums, pair=1)
    others, main, other, main_weight, other_weight = together(others, main, other, main_weight, other_weight)
    own = add(own, main, other)
    part = own.shape[0] // 2
    leaving = hop(own[part:].astype(BF16), z=(2, -1))
    sums_pair = jnp.concatenate([sums[:modes], others[:modes], sums[modes:] + others[modes:]])
    all_sums = spread_over_x(sums_pair)
    leaving, *_ = together(leaving, *all_sums[1:])
    mixed = add(own[:part], by_core(leaving, hop(leaving, z=(None, -1)))).astype(BF16)
    grad_weight = add(own_weight, main_weight, other_weight).astype(BF16)
    grad_key, grad_value, grad_residue, grad_decay, grad_skip = call(
        functools.partial(backward_full, scale=scale),
        (key_proj, value_proj, back, back_subs, log_decay, residue, skip_row, *all_sums),
        (narrow, narrow, like(table, F32), like(table, F32), like((SUBS, channels), F32)),
        [table, table, (tiles, SUBS * modes, LANES), (tiles, length, LANES)],
        0.1,
        "backward_full",
    )
    return (
        mixed,
        grad_query,
        grad_key,
        grad_value,
        grad_weight,
        grad_residue,
        grad_decay,
        grad_skip[0],
    )


def solution(mesh):
    in_specs = (
        P("seq", "chan"),
        P("seq", "chan"),
        P("seq", "chan"),
        P("chan"),
        P(None, "chan"),
        P(None, "chan"),
        P("chan", None),
        P(("seq", "chan"), None),
    )
    out_specs = (
        P(("seq", "chan"), None),
        P("seq", "chan"),
        P("seq", "chan"),
        P("seq", "chan"),
        P("chan", "seq"),
        P(None, "chan"),
        P(None, "chan"),
        P("chan"),
    )
    return jax.shard_map(local, mesh=mesh, in_specs=in_specs, out_specs=out_specs, check_vma=False)
```

```python
import functools
import itertools
import math

import jax
import jax.numpy as jnp
from jax import lax
from jax.experimental import pallas as pl
from jax.experimental.pallas import tpu as pltpu
from jax.sharding import PartitionSpec as P

RING = 4
SUBS = 8
LANES = 128
F32 = jnp.float32
BF16 = jnp.bfloat16


def strided(first, step):
    return pl.ds(first, SUBS, stride=step)


def spread(ref, mode, lanes):
    return jnp.broadcast_to(ref[pl.ds(mode, 1), lanes], (SUBS, LANES))


def tree_sum(parts):
    while len(parts) > 1:
        parts = [a + b for a, b in zip(parts[::2], parts[1::2])] + parts[len(parts) & ~1 :]
    return parts[0]


def lane_tiles(channels):
    return [(tile, pl.ds(tile * LANES, LANES)) for tile in range(channels // LANES)]


def places():
    chan, seq = lax.axis_index("chan"), lax.axis_index("seq")
    return chan // 4, lax.rem(chan // 2, 2), lax.rem(chan, 2), seq // RING, lax.rem(seq, RING)


def hop(value, x=0, y=0, z=0, core=0, pair=0):
    moves = []
    for i, j, k, c in itertools.product(range(RING), range(RING), range(RING), range(2)):
        there = ((i + x) % RING, (j + y) % RING, ((k + z) % RING) ^ pair, c ^ core)
        moves.append(tuple(((b * 2 + d // 2) * 2 + e) * 2 * RING + d % 2 * RING + a for a, b, d, e in ((i, j, k, c), there)))
    return lax.ppermute(value, ("chan", "seq"), moves)


def gather_z(cotangent):
    _, high, _, low, _ = places()
    tokens, width = cotangent.shape
    half = width // 2
    mine = lax.dynamic_slice(cotangent, (0, low * half), (tokens, half))
    theirs = lax.dynamic_slice(cotangent, (0, (1 - low) * half), (tokens, half))
    above, below, across = hop(theirs, z=1), hop(theirs, z=-1), hop(mine, z=2)
    stack = jnp.where(high == 0, jnp.stack([mine, across]), jnp.stack([across, mine]))
    same, differ = jnp.where(low == 1, above, below), jnp.where(low == 1, below, above)
    other = jnp.where(high == 0, jnp.stack([same, differ]), jnp.stack([differ, same]))
    return jnp.stack([stack, other])


def place_blocks(*sides):
    y, _, core, _, _ = places()
    _, tokens, half = sides[0][0].shape
    whole = jnp.zeros((2, RING, 2, 2, tokens, half), BF16)
    for step, blocks in zip((0, RING - 1, 1, 2), zip(*sides)):
        row = lax.rem(y + step, RING)
        for side, block in enumerate(blocks):
            for part, at_core in ((block, core), (hop(block, core=1), 1 - core)):
                whole = lax.dynamic_update_slice(whole, part[None, None, :, None], (side, row, 0, at_core, 0, 0))
    return whole


def add(*parts):
    return functools.reduce(jnp.add, [part.astype(F32) for part in parts])


def project_tile(rows_ref, weight_ref, *out_refs):
    product = jnp.dot(rows_ref[...], weight_ref[...], preferred_element_type=F32).astype(BF16)
    first = 0
    for ref in out_refs:
        ref[...] = product[first : first + ref.shape[0]]
        first += ref.shape[0]


def project(turned, out_weight):
    rows, depth = turned.shape
    width = out_weight.shape[1]
    tile = 1024
    sizes = [rows // 8, 3 * rows // 8] * 2
    return pl.pallas_call(
        project_tile,
        grid=(width // tile,),
        out_shape=[jax.ShapeDtypeStruct((size, width), BF16) for size in sizes],
        in_specs=[pl.BlockSpec((rows, depth), lambda i: (0, 0)), pl.BlockSpec((depth, tile), lambda i: (0, i))],
        out_specs=[pl.BlockSpec((size, tile), lambda i: (0, i)) for size in sizes],
        compiler_params=pltpu.CompilerParams(vmem_limit_bytes=32 * 2**20),
        cost_estimate=pl.CostEstimate(
            flops=2 * rows * depth * width, bytes_accessed=2 * width * (rows + depth), transcendentals=0
        ),
        name="project",
    )(turned, out_weight)


def weigh(gated, cot_rows, scale, r):
    width = cot_rows.shape[1] // RING
    first = lax.rem(places()[4] + r, RING) * width
    columns = lax.dynamic_slice(cot_rows, (0, first), (cot_rows.shape[0], width))
    product = lax.dot_general(gated, columns, (((0,), (0,)), ((), ())), preferred_element_type=F32)
    return (product * scale).astype(BF16)


def nearby(refs, distance, way, first, modes, lanes):
    _, _, _, low, x = places()
    before = x if way == 1 else RING - 1 - x
    other_counts = low == (way + 1) // 2
    other = refs[0].shape[0] // 2 if way == 1 else modes
    step = distance % RING
    ref = refs[way * step % RING]
    mine = ref[pl.ds(first, modes), lanes]
    theirs = jnp.where(other_counts, ref[pl.ds(other + first, modes), lanes], 0.0)
    if distance < RING:
        return jnp.where(step <= before, mine, theirs)
    return jnp.where(step <= before, theirs, 0.0)


def forward_ends(key_ref, value_ref, log_ref, ends_ref, sub_ref, drive_ref, decay_ref, zero_ref):
    length, channels = key_ref.shape
    modes = log_ref.shape[0]
    span = length // SUBS
    decay_ref[...] = jnp.exp(-jnp.exp(log_ref[...]))
    zero_ref[...] = jnp.zeros_like(zero_ref)
    for tile, lanes in lane_tiles(channels):
        drive_ref[tile] = key_ref[:, lanes].astype(F32) * value_ref[:, lanes].astype(F32)
        decay = [spread(decay_ref, m, lanes) for m in range(modes)]

        def step(i, carry):
            now, lag = carry
            u = drive_ref[tile, strided(i, span)]
            lag = [decay[m] * (lag[m] + now[m]) for m in range(modes)]
            now = [decay[m] * now[m] + u for m in range(modes)]
            return now, lag

        zero = [zero_ref[...]] * modes
        now, lag = lax.fori_loop(0, span, step, (zero, zero), unroll=8)
        for m in range(modes):
            sub_ref[tile, strided(m, modes)] = now[m]
            sub_ref[tile, strided(SUBS * modes + m, modes)] = lag[m]
        power = jnp.exp(-span * jnp.exp(log_ref[:, lanes]))
        state = jnp.zeros_like(power)
        lagged = jnp.zeros_like(power)
        for j in range(SUBS):
            lagged = power * (lagged + span * state) + sub_ref[tile, pl.ds((SUBS + j) * modes, modes)]
            state = power * state + sub_ref[tile, pl.ds(j * modes, modes)]
        ends_ref[pl.ds(0, modes), lanes] = state
        ends_ref[pl.ds(modes, modes), lanes] = lagged


def forward_full(*refs):
    (query_ref, drive_ref, sub_ref, log_ref, residue_ref, skip_ref, *end_refs) = refs[:-6]
    (gated_ref, turned_ref, pre_ref, lead_ref, decay_ref, gain_ref) = refs[-6:]
    length, channels = query_ref.shape
    modes = log_ref.shape[0]
    span = length // SUBS
    rate = jnp.exp(log_ref[...])
    decay_ref[...] = jnp.exp(-rate)
    gain_ref[...] = residue_ref[...] * jnp.sqrt(2.0 * rate)
    for tile, lanes in lane_tiles(channels):
        rate = jnp.exp(log_ref[:, lanes])
        stretch = jnp.exp(-length * rate)
        power = jnp.exp(-span * rate)
        state = jnp.zeros_like(rate)
        lagged = jnp.zeros_like(rate)
        for distance in range(2 * RING - 1, 0, -1):
            lagged = stretch * (lagged + length * state) + nearby(end_refs, distance, 1, modes, modes, lanes)
            state = stretch * state + nearby(end_refs, distance, 1, 0, modes, lanes)
        for j in range(SUBS):
            now_rows, lag_rows = (pl.ds((j + k) * modes, modes) for k in (0, SUBS))
            lead_ref[tile, now_rows] = state
            lead_ref[tile, lag_rows] = lagged
            lagged = power * (lagged + span * state) + sub_ref[tile, lag_rows]
            state = power * state + sub_ref[tile, now_rows]
        decay = [spread(decay_ref, m, lanes) for m in range(modes)]
        gain = [spread(gain_ref, m, lanes) for m in range(modes)]
        skip = spread(skip_ref, 0, lanes)

        def step(i, now):
            place = strided(i, span)
            u = drive_ref[tile, place]
            now = [decay[m] * now[m] + u for m in range(modes)]
            pre_ref[tile, place] = tree_sum([gain[m] * now[m] for m in range(modes)]) + skip * u
            return now

        first = [lead_ref[tile, strided(m, modes)] for m in range(modes)]
        lax.fori_loop(0, span, step, first, unroll=8)
        gated_ref[:, lanes] = (query_ref[:, lanes].astype(F32) * pre_ref[tile]).astype(BF16)
    part = length // (RING * 4)
    y, high, core, _, _ = places()
    for i in range(RING * 4):
        on = lax.rem(i // 4 + RING - y, RING)
        there = lax.rem(i % 2 + core, 2) * RING + jnp.where(on == 0, 3, jnp.where(on == 2, 0, (on + 1) // 2))
        there = there * 2 + lax.rem(i // 2 % 2 + high, 2)
        turned_ref[pl.ds(pl.multiple_of(there * part, part), part)] = gated_ref[pl.ds(i * part, part)]


def backward_ends(
    grad_ref, query_ref, pre_ref, drive_ref, lead_ref, log_ref,
    grad_query_ref, back_ref, sums_ref, sub_ref, decay_ref, part_ref, zero_ref,
):
    length, channels = query_ref.shape
    modes = log_ref.shape[0]
    span = length // SUBS
    half = modes // 2
    decay_ref[...] = jnp.exp(-jnp.exp(log_ref[...]))
    zero_ref[...] = jnp.zeros_like(zero_ref)
    for tile, lanes in lane_tiles(channels):
        grad = grad_ref[:, lanes].astype(F32)
        grad_query_ref[:, lanes] = (grad * pre_ref[tile]).astype(BF16)
        back_ref[tile] = grad * query_ref[:, lanes].astype(F32)
        decay = [spread(decay_ref, m, lanes) for m in range(modes)]

        def back_step(i, now):
            g = back_ref[tile, strided(span - 1 - i, span)]
            return [decay[m] * now[m] + g for m in range(modes)]

        zero = [zero_ref[...]] * modes
        now = lax.fori_loop(0, span, back_step, zero, unroll=8)
        for m in range(modes):
            sub_ref[tile, strided(m, modes)] = now[m]
        for low in range(0, modes, half):
            group = range(low, low + half)
            decay = [spread(decay_ref, m, lanes) for m in group]

            def pair_step(i, carry):
                state, lag, pair, lag_pair, skip = carry
                place = strided(i, span)
                u = drive_ref[tile, place]
                g = back_ref[tile, place]
                lag = [decay[m] * (lag[m] + state[m]) for m in range(half)]
                state = [decay[m] * state[m] + u for m in range(half)]
                pair = [pair[m] + g * state[m] for m in range(half)]
                lag_pair = [lag_pair[m] + g * lag[m] for m in range(half)]
                return state, lag, pair, lag_pair, skip + g * u

            state = [lead_ref[tile, strided(m, modes)] for m in group]
            lag = [lead_ref[tile, strided(SUBS * modes + m, modes)] for m in group]
            zero = [zero_ref[...]] * half
            state, lag, pair, lag_pair, skip = lax.fori_loop(
                0, span, pair_step, (state, lag, zero, zero, zero[0]), unroll=8
            )
            for m in range(half):
                part_ref[tile, strided(low + m, modes)] = pair[m]
                part_ref[tile, strided(SUBS * modes + low + m, modes)] = lag_pair[m]
        total = jnp.sum(skip, axis=0, keepdims=True)
        sums_ref[pl.ds(3 * modes, SUBS), lanes] = jnp.broadcast_to(total, (SUBS, LANES))
        power = jnp.exp(-span * jnp.exp(log_ref[:, lanes]))
        start = jnp.zeros_like(power)
        pair = jnp.zeros_like(power)
        lag_pair = jnp.zeros_like(power)
        for j in range(SUBS - 1, -1, -1):
            start = power * start + sub_ref[tile, pl.ds(j * modes, modes)]
            pair = pair + part_ref[tile, pl.ds(j * modes, modes)]
            lag_pair = lag_pair + part_ref[tile, pl.ds((SUBS + j) * modes, modes)]
        sums_ref[pl.ds(0, modes), lanes] = start
        sums_ref[pl.ds(modes, modes), lanes] = pair
        sums_ref[pl.ds(2 * modes, modes), lanes] = lag_pair


def backward_full(*refs, scale):
    (key_ref, value_ref, back_ref, sub_ref, log_ref, residue_ref, skip_ref, *sum_refs) = refs[:-9]
    (grad_key_ref, grad_value_ref, grad_residue_ref, grad_decay_ref, grad_skip_ref) = refs[-9:-4]
    (decay_ref, gain_ref, lead_ref, drive_grad_ref) = refs[-4:]
    length, channels = key_ref.shape
    modes = log_ref.shape[0]
    span = length // SUBS
    rate = jnp.exp(log_ref[...])
    norm = jnp.sqrt(2.0 * rate)
    gain = residue_ref[...] * norm
    decay_ref[...] = jnp.exp(-rate)
    gain_ref[...] = gain
    pair = tree_sum([ref[pl.ds(2 * modes, modes)] for ref in sum_refs])
    lag_pair = tree_sum([ref[pl.ds(3 * modes, modes)] for ref in sum_refs])
    grad_residue_ref[...] = norm * pair * scale
    grad_decay_ref[...] = gain * (0.5 * pair - rate * lag_pair) * scale
    grad_skip_ref[...] = tree_sum([ref[pl.ds(4 * modes, SUBS)] for ref in sum_refs]) * scale
    for tile, lanes in lane_tiles(channels):
        rate = jnp.exp(log_ref[:, lanes])
        stretch = jnp.exp(-length * rate)
        power = jnp.exp(-span * rate)
        start = jnp.zeros_like(rate)
        for distance in range(2 * RING - 1, 0, -1):
            start = stretch * start + nearby(sum_refs, distance, -1, 0, modes, lanes)
        for j in range(SUBS - 1, -1, -1):
            lead_ref[tile, pl.ds(j * modes, modes)] = start
            start = power * start + sub_ref[tile, pl.ds(j * modes, modes)]
        decay = [spread(decay_ref, m, lanes) for m in range(modes)]
        gain = [spread(gain_ref, m, lanes) for m in range(modes)]
        skip = spread(skip_ref, 0, lanes)

        def step(i, now):
            place = strided(span - 1 - i, span)
            g = back_ref[tile, place]
            now = [decay[m] * now[m] + g for m in range(modes)]
            drive_grad_ref[tile, place] = tree_sum([gain[m] * now[m] for m in range(modes)]) + skip * g
            return now

        first = [lead_ref[tile, strided(m, modes)] for m in range(modes)]
        lax.fori_loop(0, span, step, first, unroll=8)
        drive_grad = drive_grad_ref[tile]
        grad_key_ref[:, lanes] = (drive_grad * value_ref[:, lanes].astype(F32)).astype(BF16)
        grad_value_ref[:, lanes] = (drive_grad * key_ref[:, lanes].astype(F32)).astype(BF16)


def call(body, args, outs, scratch, micros, name):
    whole = pl.BlockSpec(memory_space=pltpu.VMEM)
    return pl.pallas_call(
        body,
        out_shape=[jax.ShapeDtypeStruct(o.shape, o.dtype) for o in outs],
        in_specs=[whole] * len(args),
        out_specs=[whole] * len(outs),
        scratch_shapes=[pltpu.VMEM(shape, F32) for shape in scratch],
        compiler_params=pltpu.CompilerParams(vmem_limit_bytes=32 * 2**20),
        cost_estimate=pl.CostEstimate(flops=int(micros * 1.15e9), bytes_accessed=0, transcendentals=0),
        name=name,
    )(*args)


def like(shape, dtype):
    return jax.ShapeDtypeStruct(shape, dtype)


def spread_over_x(value):
    return [value] + [hop(value, x=offset) for offset in range(1, RING)]


def together(*values):
    return lax.optimization_barrier(values)


def local(queries, key_proj, value_proj, skip_gain, residue, log_decay, out_weight, cotangent):
    length, channels = queries.shape
    modes = residue.shape[0]
    blocks = lax.axis_size("seq")
    scale = 1.0 / math.sqrt(length * blocks)
    skip_row = skip_gain.reshape(1, channels)
    tiles = channels // LANES
    wide = like((tiles, length, LANES), F32)
    narrow = like((length, channels), BF16)
    table = (modes, channels)

    block, log_first = together(gather_z(cotangent), log_decay)
    before_own, after_other = hop(block[0], y=1), hop(block[1], y=-1)
    ends, subs, driving = call(
        forward_ends,
        (key_proj, value_proj, log_first),
        (like((2 * modes, channels), F32), like((tiles, 2 * SUBS * modes, LANES), F32), wide),
        [table, (SUBS, LANES)],
        0.1,
        "forward_ends",
    )
    ends_pair = jnp.concatenate([ends, hop(ends, pair=1)])
    before_own, after_other, ends_pair = together(before_own, after_other, ends_pair)
    before_other, after_own = hop(block[1], y=1), hop(block[0], y=-1)
    earlier = spread_over_x(ends_pair)
    gated, turned, pre_gate, lead = call(
        forward_full,
        (queries, driving, subs, log_decay, residue, skip_row, *earlier),
        (narrow, narrow, wide, like((tiles, 2 * SUBS * modes, LANES), F32)),
        [table, table],
        0.1,
        "forward_full",
    )
    before_own, after_other, turned = together(before_own, after_other, turned)
    far_own, far_other = hop(before_own, y=1), hop(after_other, y=-1)
    before_other, after_own, turned = together(before_other, after_own, turned)
    near_first, near_rest, far_first, far_rest = project(turned, out_weight)
    got_first, got_rest = hop(far_first, core=1), hop(far_rest, core=1)
    gated_pair = jnp.concatenate([gated, hop(gated, pair=1)])
    opposite = add(near_first, got_first).astype(BF16)
    far_own, far_other, opposite = together(far_own, far_other, opposite)
    cot_rows = place_blocks(
        (block[0], before_own, after_own, far_own), (block[1], before_other, after_other, far_other)
    )
    cot_rows, got_rest = together(cot_rows.reshape(2 * length, -1), got_rest)

    half = out_weight.shape[1] // 2
    low_weight = lax.dynamic_slice(out_weight, (0, places()[3] * half), (channels, half))
    weights = {2: weigh(gated_pair, cot_rows, scale, 2)}
    cot_rows, weights[2] = together(cot_rows, weights[2])
    grad_parts = lax.dot_general(cot_rows, low_weight, (((1,), (1,)), ((), ())), preferred_element_type=F32)
    cot_rows, grad_parts = together(cot_rows, grad_parts)
    theirs = hop(grad_parts[length:].astype(BF16), pair=1)
    for r in (1, 3, 0):
        weights[r] = weigh(gated_pair, cot_rows, scale, r)
    got_rest, _ = together(got_rest, theirs)
    part = opposite.shape[0] // 2
    low_sum, high_sum = hop(opposite[:part], y=1), hop(opposite[part:], y=-1)
    above, below, own = (
        add(near_rest[i * 2 * part : (i + 1) * 2 * part], got_rest[i * 2 * part : (i + 1) * 2 * part]) for i in range(3)
    )
    above = jnp.concatenate([add(above[:part], low_sum), above[part:]]).astype(BF16)
    below = jnp.concatenate([below[:part], add(below[part:], high_sum)]).astype(BF16)
    cut = channels // 2
    upper, lower = hop(weights[2][:cut], x=1), hop(weights[2][cut:], x=-1)
    up_sum = add(weights[1][:cut], upper).astype(BF16)
    down_sum = add(weights[3][cut:], lower).astype(BF16)
    up_rest, down_rest = weights[1][cut:], weights[3][:cut]
    theirs, up_sum, down_sum, up_rest, down_rest = together(theirs, up_sum, down_sum, up_rest, down_rest)
    up_rest, down_rest = hop(up_rest, x=1), hop(down_rest, x=-1)
    grad_gated = add(grad_parts[:length], theirs)
    own = add(own, hop(above, y=1), hop(below, y=-1))
    leaving = own[part:].astype(BF16)
    width = leaving.shape[1] // 2
    halfway = hop(leaving[:, width:], z=-1)
    crossed = hop(leaving[:, :width], z=2)

    grad_query, back, sums, back_subs = call(
        backward_ends,
        (grad_gated, queries, pre_gate, driving, lead, log_decay),
        (narrow, wide, like((3 * modes + SUBS, channels), F32), like((tiles, SUBS * modes, LANES), F32)),
        [table, (tiles, 2 * SUBS * modes, LANES), (SUBS, LANES)],
        2.0,
        "backward_ends",
    )
    sums, up_rest, down_rest = together(sums, up_rest, down_rest)
    up_sum, down_sum = hop(up_sum, x=1), hop(down_sum, x=-1)
    others = hop(sums, pair=1)
    sums_pair = jnp.concatenate([sums[:modes], others[:modes], sums[modes:] + others[modes:]])
    sums_pair, up_sum, down_sum = together(sums_pair, up_sum, down_sum)
    crossed = jnp.concatenate([crossed, hop(halfway, z=-1)], axis=1)
    mixed = add(own[:part], crossed).astype(BF16)
    all_sums = spread_over_x(sums_pair)
    grad_weight = jnp.concatenate(
        [add(weights[0][:cut], up_sum, down_rest), add(weights[0][cut:], up_rest, down_sum)]
    ).astype(BF16)
    grad_key, grad_value, grad_residue, grad_decay, grad_skip = call(
        functools.partial(backward_full, scale=scale),
        (key_proj, value_proj, back, back_subs, log_decay, residue, skip_row, *all_sums),
        (narrow, narrow, like(table, F32), like(table, F32), like((SUBS, channels), F32)),
        [table, table, (tiles, SUBS * modes, LANES), (tiles, length, LANES)],
        0.1,
        "backward_full",
    )
    return (
        mixed,
        grad_query,
        grad_key,
        grad_value,
        grad_weight,
        grad_residue,
        grad_decay,
        grad_skip[0],
    )


def solution(mesh):
    in_specs = (
        P("seq", "chan"),
        P("seq", "chan"),
        P("seq", "chan"),
        P("chan"),
        P(None, "chan"),
        P(None, "chan"),
        P("chan", None),
        P(("seq", "chan"), None),
    )
    out_specs = (
        P(("seq", "chan"), None),
        P("seq", "chan"),
        P("seq", "chan"),
        P("seq", "chan"),
        P("chan", "seq"),
        P(None, "chan"),
        P(None, "chan"),
        P("chan"),
    )
    return jax.shard_map(local, mesh=mesh, in_specs=in_specs, out_specs=out_specs, check_vma=False)
```

```python
import functools
import itertools
import math

import jax
import jax.numpy as jnp
from jax import lax
from jax.experimental import pallas as pl
from jax.experimental.pallas import tpu as pltpu
from jax.sharding import PartitionSpec as P

RING = 4
SUBS = 8
LANES = 128
F32 = jnp.float32
BF16 = jnp.bfloat16


def strided(first, step):
    return pl.ds(first, SUBS, stride=step)


def spread(ref, mode, lanes):
    return jnp.broadcast_to(ref[pl.ds(mode, 1), lanes], (SUBS, LANES))


def tree_sum(parts):
    while len(parts) > 1:
        parts = [a + b for a, b in zip(parts[::2], parts[1::2])] + parts[len(parts) & ~1 :]
    return parts[0]


def lane_tiles(channels):
    return [(tile, pl.ds(tile * LANES, LANES)) for tile in range(channels // LANES)]


def places():
    chan, seq = lax.axis_index("chan"), lax.axis_index("seq")
    return chan // 4, lax.rem(chan // 2, 2), lax.rem(chan, 2), seq // RING, lax.rem(seq, RING)


def hop(value, x=0, y=0, z=0, core=0, pair=0):
    moves = []
    for i, j, k, c in itertools.product(range(RING), range(RING), range(RING), range(2)):
        there = ((i + x) % RING, (j + y) % RING, ((k + z) % RING) ^ pair, c ^ core)
        moves.append(tuple(((b * 2 + d // 2) * 2 + e) * 2 * RING + d % 2 * RING + a for a, b, d, e in ((i, j, k, c), there)))
    return lax.ppermute(value, ("chan", "seq"), moves)


def gather_z(cotangent):
    _, high, _, low, _ = places()
    tokens, width = cotangent.shape
    half = width // 2
    mine = lax.dynamic_slice(cotangent, (0, low * half), (tokens, half))
    theirs = lax.dynamic_slice(cotangent, (0, (1 - low) * half), (tokens, half))
    above, below, across = hop(theirs, z=1), hop(theirs, z=-1), hop(mine, z=2)
    stack = jnp.where(high == 0, jnp.stack([mine, across]), jnp.stack([across, mine]))
    same, differ = jnp.where(low == 1, above, below), jnp.where(low == 1, below, above)
    other = jnp.where(high == 0, jnp.stack([same, differ]), jnp.stack([differ, same]))
    return jnp.stack([stack, other])


def place_blocks(*sides):
    y, _, core, _, _ = places()
    _, tokens, half = sides[0][0].shape
    whole = jnp.zeros((2, RING, 2, 2, tokens, half), BF16)
    for step, blocks in zip((0, RING - 1, 1, 2), zip(*sides)):
        row = lax.rem(y + step, RING)
        for side, block in enumerate(blocks):
            for part, at_core in ((block, core), (hop(block, core=1), 1 - core)):
                whole = lax.dynamic_update_slice(whole, part[None, None, :, None], (side, row, 0, at_core, 0, 0))
    return whole


def add(*parts):
    return functools.reduce(jnp.add, [part.astype(F32) for part in parts])


def project_tile(rows_ref, weight_ref, *out_refs):
    product = jnp.dot(rows_ref[...], weight_ref[...], preferred_element_type=F32).astype(BF16)
    first = 0
    for ref in out_refs:
        ref[...] = product[first : first + ref.shape[0]]
        first += ref.shape[0]


def project(turned, out_weight):
    rows, depth = turned.shape
    width = out_weight.shape[1]
    tile = 1024
    sizes = [rows // 8, 3 * rows // 8] * 2
    return pl.pallas_call(
        project_tile,
        grid=(width // tile,),
        out_shape=[jax.ShapeDtypeStruct((size, width), BF16) for size in sizes],
        in_specs=[pl.BlockSpec((rows, depth), lambda i: (0, 0)), pl.BlockSpec((depth, tile), lambda i: (0, i))],
        out_specs=[pl.BlockSpec((size, tile), lambda i: (0, i)) for size in sizes],
        compiler_params=pltpu.CompilerParams(vmem_limit_bytes=32 * 2**20),
        cost_estimate=pl.CostEstimate(
            flops=2 * rows * depth * width, bytes_accessed=2 * width * (rows + depth), transcendentals=0
        ),
        name="project",
    )(turned, out_weight)


def weigh(gated, cot_rows, scale, r):
    width = cot_rows.shape[1] // RING
    first = lax.rem(places()[4] + r, RING) * width
    columns = lax.dynamic_slice(cot_rows, (0, first), (cot_rows.shape[0], width))
    product = lax.dot_general(gated, columns, (((0,), (0,)), ((), ())), preferred_element_type=F32)
    return (product * scale).astype(BF16)


def nearby(refs, distance, way, first, modes, lanes):
    _, _, _, low, x = places()
    before = x if way == 1 else RING - 1 - x
    other_counts = low == (way + 1) // 2
    other = refs[0].shape[0] // 2 if way == 1 else modes
    step = distance % RING
    ref = refs[way * step % RING]
    mine = ref[pl.ds(first, modes), lanes]
    theirs = jnp.where(other_counts, ref[pl.ds(other + first, modes), lanes], 0.0)
    if distance < RING:
        return jnp.where(step <= before, mine, theirs)
    return jnp.where(step <= before, theirs, 0.0)


def forward_ends(key_ref, value_ref, log_ref, ends_ref, sub_ref, drive_ref, decay_ref, zero_ref):
    length, channels = key_ref.shape
    modes = log_ref.shape[0]
    span = length // SUBS
    decay_ref[...] = jnp.exp(-jnp.exp(log_ref[...]))
    zero_ref[...] = jnp.zeros_like(zero_ref)
    for tile, lanes in lane_tiles(channels):
        drive_ref[tile] = key_ref[:, lanes].astype(F32) * value_ref[:, lanes].astype(F32)
        decay = [spread(decay_ref, m, lanes) for m in range(modes)]

        def step(i, carry):
            now, lag = carry
            u = drive_ref[tile, strided(i, span)]
            lag = [decay[m] * (lag[m] + now[m]) for m in range(modes)]
            now = [decay[m] * now[m] + u for m in range(modes)]
            return now, lag

        zero = [zero_ref[...]] * modes
        now, lag = lax.fori_loop(0, span, step, (zero, zero), unroll=8)
        for m in range(modes):
            sub_ref[tile, strided(m, modes)] = now[m]
            sub_ref[tile, strided(SUBS * modes + m, modes)] = lag[m]
        power = jnp.exp(-span * jnp.exp(log_ref[:, lanes]))
        state = jnp.zeros_like(power)
        lagged = jnp.zeros_like(power)
        for j in range(SUBS):
            lagged = power * (lagged + span * state) + sub_ref[tile, pl.ds((SUBS + j) * modes, modes)]
            state = power * state + sub_ref[tile, pl.ds(j * modes, modes)]
        ends_ref[pl.ds(0, modes), lanes] = state
        ends_ref[pl.ds(modes, modes), lanes] = lagged


def forward_full(*refs):
    (query_ref, drive_ref, sub_ref, log_ref, residue_ref, skip_ref, *end_refs) = refs[:-6]
    (gated_ref, turned_ref, pre_ref, lead_ref, decay_ref, gain_ref) = refs[-6:]
    length, channels = query_ref.shape
    modes = log_ref.shape[0]
    span = length // SUBS
    rate = jnp.exp(log_ref[...])
    decay_ref[...] = jnp.exp(-rate)
    gain_ref[...] = residue_ref[...] * jnp.sqrt(2.0 * rate)
    for tile, lanes in lane_tiles(channels):
        rate = jnp.exp(log_ref[:, lanes])
        stretch = jnp.exp(-length * rate)
        power = jnp.exp(-span * rate)
        state = jnp.zeros_like(rate)
        lagged = jnp.zeros_like(rate)
        for distance in range(2 * RING - 1, 0, -1):
            lagged = stretch * (lagged + length * state) + nearby(end_refs, distance, 1, modes, modes, lanes)
            state = stretch * state + nearby(end_refs, distance, 1, 0, modes, lanes)
        for j in range(SUBS):
            now_rows, lag_rows = (pl.ds((j + k) * modes, modes) for k in (0, SUBS))
            lead_ref[tile, now_rows] = state
            lead_ref[tile, lag_rows] = lagged
            lagged = power * (lagged + span * state) + sub_ref[tile, lag_rows]
            state = power * state + sub_ref[tile, now_rows]
        decay = [spread(decay_ref, m, lanes) for m in range(modes)]
        gain = [spread(gain_ref, m, lanes) for m in range(modes)]
        skip = spread(skip_ref, 0, lanes)

        def step(i, now):
            place = strided(i, span)
            u = drive_ref[tile, place]
            now = [decay[m] * now[m] + u for m in range(modes)]
            pre_ref[tile, place] = tree_sum([gain[m] * now[m] for m in range(modes)]) + skip * u
            return now

        first = [lead_ref[tile, strided(m, modes)] for m in range(modes)]
        lax.fori_loop(0, span, step, first, unroll=8)
        gated_ref[:, lanes] = (query_ref[:, lanes].astype(F32) * pre_ref[tile]).astype(BF16)
    part = length // (RING * 4)
    y, high, core, _, _ = places()
    for i in range(RING * 4):
        on = lax.rem(i // 4 + RING - y, RING)
        there = lax.rem(i % 2 + core, 2) * RING + jnp.where(on == 0, 3, jnp.where(on == 2, 0, (on + 1) // 2))
        there = there * 2 + lax.rem(i // 2 % 2 + high, 2)
        turned_ref[pl.ds(pl.multiple_of(there * part, part), part)] = gated_ref[pl.ds(i * part, part)]


def backward_ends(
    grad_ref, query_ref, pre_ref, drive_ref, lead_ref, log_ref,
    grad_query_ref, back_ref, sums_ref, sub_ref, decay_ref, part_ref, zero_ref,
):
    length, channels = query_ref.shape
    modes = log_ref.shape[0]
    span = length // SUBS
    half = modes // 2
    decay_ref[...] = jnp.exp(-jnp.exp(log_ref[...]))
    zero_ref[...] = jnp.zeros_like(zero_ref)
    for tile, lanes in lane_tiles(channels):
        grad = grad_ref[:, lanes].astype(F32)
        grad_query_ref[:, lanes] = (grad * pre_ref[tile]).astype(BF16)
        back_ref[tile] = grad * query_ref[:, lanes].astype(F32)
        skip = zero_ref[...]
        for low in range(0, modes, half):
            group = range(low, low + half)
            decay = [spread(decay_ref, m, lanes) for m in group]

            def back_step(i, carry):
                start, lag, pair, lag_pair, skip = carry
                place = strided(span - 1 - i, span)
                u = drive_ref[tile, place]
                g = back_ref[tile, place]
                lag = [decay[m] * (lag[m] + start[m]) for m in range(half)]
                start = [decay[m] * start[m] + g for m in range(half)]
                pair = [pair[m] + u * start[m] for m in range(half)]
                lag_pair = [lag_pair[m] + u * lag[m] for m in range(half)]
                return start, lag, pair, lag_pair, (skip + g * u if low == 0 else skip)

            zero = [zero_ref[...]] * half
            start, lag, pair, lag_pair, skip = lax.fori_loop(
                0, span, back_step, (zero, zero, zero, zero, skip), unroll=8
            )
            for m in range(half):
                state = lead_ref[tile, strided(low + m, modes)]
                lagged = lead_ref[tile, strided(SUBS * modes + low + m, modes)]
                once = decay[m] * start[m]
                twice = decay[m] * (lag[m] + start[m])
                sub_ref[tile, strided(low + m, modes)] = start[m]
                part_ref[tile, strided(low + m, modes)] = pair[m] + state * once
                part_ref[tile, strided(SUBS * modes + low + m, modes)] = lag_pair[m] + state * twice + lagged * once
        total = jnp.sum(skip, axis=0, keepdims=True)
        sums_ref[pl.ds(3 * modes, SUBS), lanes] = jnp.broadcast_to(total, (SUBS, LANES))
        power = jnp.exp(-span * jnp.exp(log_ref[:, lanes]))
        start = jnp.zeros_like(power)
        pair = jnp.zeros_like(power)
        lag_pair = jnp.zeros_like(power)
        for j in range(SUBS - 1, -1, -1):
            start = power * start + sub_ref[tile, pl.ds(j * modes, modes)]
            pair = pair + part_ref[tile, pl.ds(j * modes, modes)]
            lag_pair = lag_pair + part_ref[tile, pl.ds((SUBS + j) * modes, modes)]
        sums_ref[pl.ds(0, modes), lanes] = start
        sums_ref[pl.ds(modes, modes), lanes] = pair
        sums_ref[pl.ds(2 * modes, modes), lanes] = lag_pair


def backward_full(*refs, scale):
    (key_ref, value_ref, back_ref, sub_ref, log_ref, residue_ref, skip_ref, *sum_refs) = refs[:-9]
    (grad_key_ref, grad_value_ref, grad_residue_ref, grad_decay_ref, grad_skip_ref) = refs[-9:-4]
    (decay_ref, gain_ref, lead_ref, drive_grad_ref) = refs[-4:]
    length, channels = key_ref.shape
    modes = log_ref.shape[0]
    span = length // SUBS
    rate = jnp.exp(log_ref[...])
    norm = jnp.sqrt(2.0 * rate)
    gain = residue_ref[...] * norm
    decay_ref[...] = jnp.exp(-rate)
    gain_ref[...] = gain
    pair = tree_sum([ref[pl.ds(2 * modes, modes)] for ref in sum_refs])
    lag_pair = tree_sum([ref[pl.ds(3 * modes, modes)] for ref in sum_refs])
    grad_residue_ref[...] = norm * pair * scale
    grad_decay_ref[...] = gain * (0.5 * pair - rate * lag_pair) * scale
    grad_skip_ref[...] = tree_sum([ref[pl.ds(4 * modes, SUBS)] for ref in sum_refs]) * scale
    for tile, lanes in lane_tiles(channels):
        rate = jnp.exp(log_ref[:, lanes])
        stretch = jnp.exp(-length * rate)
        power = jnp.exp(-span * rate)
        start = jnp.zeros_like(rate)
        for distance in range(2 * RING - 1, 0, -1):
            start = stretch * start + nearby(sum_refs, distance, -1, 0, modes, lanes)
        for j in range(SUBS - 1, -1, -1):
            lead_ref[tile, pl.ds(j * modes, modes)] = start
            start = power * start + sub_ref[tile, pl.ds(j * modes, modes)]
        decay = [spread(decay_ref, m, lanes) for m in range(modes)]
        gain = [spread(gain_ref, m, lanes) for m in range(modes)]
        skip = spread(skip_ref, 0, lanes)

        def step(i, now):
            place = strided(span - 1 - i, span)
            g = back_ref[tile, place]
            now = [decay[m] * now[m] + g for m in range(modes)]
            drive_grad_ref[tile, place] = tree_sum([gain[m] * now[m] for m in range(modes)]) + skip * g
            return now

        first = [lead_ref[tile, strided(m, modes)] for m in range(modes)]
        lax.fori_loop(0, span, step, first, unroll=8)
        drive_grad = drive_grad_ref[tile]
        grad_key_ref[:, lanes] = (drive_grad * value_ref[:, lanes].astype(F32)).astype(BF16)
        grad_value_ref[:, lanes] = (drive_grad * key_ref[:, lanes].astype(F32)).astype(BF16)


def call(body, args, outs, scratch, micros, name):
    whole = pl.BlockSpec(memory_space=pltpu.VMEM)
    return pl.pallas_call(
        body,
        out_shape=[jax.ShapeDtypeStruct(o.shape, o.dtype) for o in outs],
        in_specs=[whole] * len(args),
        out_specs=[whole] * len(outs),
        scratch_shapes=[pltpu.VMEM(shape, F32) for shape in scratch],
        compiler_params=pltpu.CompilerParams(vmem_limit_bytes=32 * 2**20),
        cost_estimate=pl.CostEstimate(flops=int(micros * 1.15e9), bytes_accessed=0, transcendentals=0),
        name=name,
    )(*args)


def like(shape, dtype):
    return jax.ShapeDtypeStruct(shape, dtype)


def spread_over_x(value):
    return [value] + [hop(value, x=offset) for offset in range(1, RING)]


def together(*values):
    return lax.optimization_barrier(values)


def local(queries, key_proj, value_proj, skip_gain, residue, log_decay, out_weight, cotangent):
    length, channels = queries.shape
    modes = residue.shape[0]
    blocks = lax.axis_size("seq")
    scale = 1.0 / math.sqrt(length * blocks)
    skip_row = skip_gain.reshape(1, channels)
    tiles = channels // LANES
    wide = like((tiles, length, LANES), F32)
    narrow = like((length, channels), BF16)
    table = (modes, channels)

    block, log_first = together(gather_z(cotangent), log_decay)
    before_own, after_other = hop(block[0], y=1), hop(block[1], y=-1)
    ends, subs, driving = call(
        forward_ends,
        (key_proj, value_proj, log_first),
        (like((2 * modes, channels), F32), like((tiles, 2 * SUBS * modes, LANES), F32), wide),
        [table, (SUBS, LANES)],
        0.1,
        "forward_ends",
    )
    ends_pair = jnp.concatenate([ends, hop(ends, pair=1)])
    before_own, after_other, ends_pair = together(before_own, after_other, ends_pair)
    before_other, after_own = hop(block[1], y=1), hop(block[0], y=-1)
    earlier = spread_over_x(ends_pair)
    gated, turned, pre_gate, lead = call(
        forward_full,
        (queries, driving, subs, log_decay, residue, skip_row, *earlier),
        (narrow, narrow, wide, like((tiles, 2 * SUBS * modes, LANES), F32)),
        [table, table],
        0.1,
        "forward_full",
    )
    before_own, after_other, turned = together(before_own, after_other, turned)
    far_own, far_other = hop(before_own, y=1), hop(after_other, y=-1)
    before_other, after_own, turned = together(before_other, after_own, turned)
    near_first, near_rest, far_first, far_rest = project(turned, out_weight)
    got_first, got_rest = hop(far_first, core=1), hop(far_rest, core=1)
    gated_pair = jnp.concatenate([gated, hop(gated, pair=1)])
    opposite = add(near_first, got_first).astype(BF16)
    far_own, far_other, opposite = together(far_own, far_other, opposite)
    cot_rows = place_blocks(
        (block[0], before_own, after_own, far_own), (block[1], before_other, after_other, far_other)
    )
    cot_rows, got_rest = together(cot_rows.reshape(2 * length, -1), got_rest)

    half = out_weight.shape[1] // 2
    low_weight = lax.dynamic_slice(out_weight, (0, places()[3] * half), (channels, half))
    weights = {2: weigh(gated_pair, cot_rows, scale, 2)}
    cot_rows, weights[2] = together(cot_rows, weights[2])
    grad_parts = lax.dot_general(cot_rows, low_weight, (((1,), (1,)), ((), ())), preferred_element_type=F32)
    cot_rows, grad_parts, got_rest = together(cot_rows, grad_parts, got_rest)
    theirs = hop(grad_parts[length:].astype(BF16), pair=1)
    part = opposite.shape[0] // 2
    low_sum, high_sum = hop(opposite[:part], y=1), hop(opposite[part:], y=-1)
    above, below, own = (
        add(near_rest[i * 2 * part : (i + 1) * 2 * part], got_rest[i * 2 * part : (i + 1) * 2 * part]) for i in range(3)
    )
    above = jnp.concatenate([add(above[:part], low_sum), above[part:]]).astype(BF16)
    below = jnp.concatenate([below[:part], add(below[part:], high_sum)]).astype(BF16)
    for r in (1, 3, 0):
        weights[r] = weigh(gated_pair, cot_rows, scale, r)
    cut = channels // 2
    upper, lower = hop(weights[2][:cut], x=1), hop(weights[2][cut:], x=-1)
    up_sum = add(weights[1][:cut], upper).astype(BF16)
    down_sum = add(weights[3][cut:], lower).astype(BF16)
    up_rest, down_rest = weights[1][cut:], weights[3][:cut]
    theirs, up_sum, down_sum, up_rest, down_rest = together(theirs, up_sum, down_sum, up_rest, down_rest)
    up_rest, down_rest = hop(up_rest, x=1), hop(down_rest, x=-1)
    grad_gated = add(grad_parts[:length], theirs)
    own = add(own, hop(above, y=1), hop(below, y=-1))
    leaving = own[part:].astype(BF16)
    width = leaving.shape[1] // 2
    halfway = hop(leaving[:, width:], z=-1)
    crossed = hop(leaving[:, :width], z=2)

    grad_query, back, sums, back_subs = call(
        backward_ends,
        (grad_gated, queries, pre_gate, driving, lead, log_decay),
        (narrow, wide, like((3 * modes + SUBS, channels), F32), like((tiles, SUBS * modes, LANES), F32)),
        [table, (tiles, 2 * SUBS * modes, LANES), (SUBS, LANES)],
        2.0,
        "backward_ends",
    )
    sums, up_rest, down_rest = together(sums, up_rest, down_rest)
    up_sum, down_sum = hop(up_sum, x=1), hop(down_sum, x=-1)
    others = hop(sums, pair=1)
    sums_pair = jnp.concatenate([sums[:modes], others[:modes], sums[modes:] + others[modes:]])
    sums_pair, up_sum, down_sum = together(sums_pair, up_sum, down_sum)
    crossed = jnp.concatenate([crossed, hop(halfway, z=-1)], axis=1)
    mixed = add(own[:part], crossed).astype(BF16)
    all_sums = spread_over_x(sums_pair)
    grad_weight = jnp.concatenate(
        [add(weights[0][:cut], up_sum, down_rest), add(weights[0][cut:], up_rest, down_sum)]
    ).astype(BF16)
    grad_key, grad_value, grad_residue, grad_decay, grad_skip = call(
        functools.partial(backward_full, scale=scale),
        (key_proj, value_proj, back, back_subs, log_decay, residue, skip_row, *all_sums),
        (narrow, narrow, like(table, F32), like(table, F32), like((SUBS, channels), F32)),
        [table, table, (tiles, SUBS * modes, LANES), (tiles, length, LANES)],
        0.1,
        "backward_full",
    )
    return (
        mixed,
        grad_query,
        grad_key,
        grad_value,
        grad_weight,
        grad_residue,
        grad_decay,
        grad_skip[0],
    )


def solution(mesh):
    in_specs = (
        P("seq", "chan"),
        P("seq", "chan"),
        P("seq", "chan"),
        P("chan"),
        P(None, "chan"),
        P(None, "chan"),
        P("chan", None),
        P(("seq", "chan"), None),
    )
    out_specs = (
        P(("seq", "chan"), None),
        P("seq", "chan"),
        P("seq", "chan"),
        P("seq", "chan"),
        P("chan", "seq"),
        P(None, "chan"),
        P(None, "chan"),
        P("chan"),
    )
    return jax.shard_map(local, mesh=mesh, in_specs=in_specs, out_specs=out_specs, check_vma=False)
```

```python
import functools
import itertools
import math

import jax
import jax.numpy as jnp
from jax import lax
from jax.experimental import pallas as pl
from jax.experimental.pallas import tpu as pltpu
from jax.sharding import PartitionSpec as P

RING = 4
SUBS = 8
LANES = 128
F32 = jnp.float32
BF16 = jnp.bfloat16


def strided(first, step):
    return pl.ds(first, SUBS, stride=step)


def spread(ref, mode, lanes):
    return jnp.broadcast_to(ref[pl.ds(mode, 1), lanes], (SUBS, LANES))


def tree_sum(parts):
    while len(parts) > 1:
        parts = [a + b for a, b in zip(parts[::2], parts[1::2])] + parts[len(parts) & ~1 :]
    return parts[0]


def lane_tiles(channels):
    return [(tile, pl.ds(tile * LANES, LANES)) for tile in range(channels // LANES)]


def places():
    chan, seq = lax.axis_index("chan"), lax.axis_index("seq")
    return chan // 4, lax.rem(chan // 2, 2), lax.rem(chan, 2), seq // RING, lax.rem(seq, RING)


def hop(value, x=0, y=0, z=0, core=0, pair=0):
    moves = []
    for i, j, k, c in itertools.product(range(RING), range(RING), range(RING), range(2)):
        there = ((i + x) % RING, (j + y) % RING, ((k + z) % RING) ^ pair, c ^ core)
        moves.append(tuple(((b * 2 + d // 2) * 2 + e) * 2 * RING + d % 2 * RING + a for a, b, d, e in ((i, j, k, c), there)))
    return lax.ppermute(value, ("chan", "seq"), moves)


def gather_z(cotangent):
    _, high, _, low, _ = places()
    tokens, width = cotangent.shape
    half = width // 2
    mine = lax.dynamic_slice(cotangent, (0, low * half), (tokens, half))
    theirs = lax.dynamic_slice(cotangent, (0, (1 - low) * half), (tokens, half))
    above, below, across = hop(theirs, z=1), hop(theirs, z=-1), hop(mine, z=2)
    stack = jnp.where(high == 0, jnp.stack([mine, across]), jnp.stack([across, mine]))
    same, differ = jnp.where(low == 1, above, below), jnp.where(low == 1, below, above)
    other = jnp.where(high == 0, jnp.stack([same, differ]), jnp.stack([differ, same]))
    return jnp.stack([stack, other])


def place_blocks(*sides):
    y, _, core, _, _ = places()
    _, tokens, half = sides[0][0].shape
    whole = jnp.zeros((2, RING, 2, 2, tokens, half), BF16)
    for step, blocks in zip((0, RING - 1, 1, 2), zip(*sides)):
        row = lax.rem(y + step, RING)
        for side, block in enumerate(blocks):
            for part, at_core in ((block, core), (hop(block, core=1), 1 - core)):
                whole = lax.dynamic_update_slice(whole, part[None, None, :, None], (side, row, 0, at_core, 0, 0))
    return whole


def add(*parts):
    return functools.reduce(jnp.add, [part.astype(F32) for part in parts])


def project_tiles(rows_ref, weight_ref, *out_refs, tile):
    def one(i, carry):
        columns = pl.ds(pl.multiple_of(i * tile, tile), tile)
        product = jnp.dot(rows_ref[...], weight_ref[:, columns], preferred_element_type=F32).astype(BF16)
        first = 0
        for ref in out_refs:
            ref[:, columns] = product[first : first + ref.shape[0]]
            first += ref.shape[0]
        return carry

    lax.fori_loop(0, weight_ref.shape[1] // tile, one, 0)


def project(turned, out_weight):
    rows, depth = turned.shape
    width = out_weight.shape[1]
    sizes = [rows // 8, 3 * rows // 8] * 2
    whole = pl.BlockSpec(memory_space=pltpu.VMEM)
    return pl.pallas_call(
        functools.partial(project_tiles, tile=512),
        out_shape=[jax.ShapeDtypeStruct((size, width), BF16) for size in sizes],
        in_specs=[whole] * 2,
        out_specs=[whole] * len(sizes),
        compiler_params=pltpu.CompilerParams(vmem_limit_bytes=32 * 2**20),
        cost_estimate=pl.CostEstimate(
            flops=2 * rows * depth * width, bytes_accessed=2 * width * (rows + depth), transcendentals=0
        ),
        name="project",
    )(turned, out_weight)


def weigh(gated, cot_rows, scale, r):
    width = cot_rows.shape[1] // RING
    first = lax.rem(places()[4] + r, RING) * width
    columns = lax.dynamic_slice(cot_rows, (0, first), (cot_rows.shape[0], width))
    product = lax.dot_general(gated, columns, (((0,), (0,)), ((), ())), preferred_element_type=F32)
    return (product * scale).astype(BF16)


def nearby(refs, distance, way, first, modes, lanes):
    _, _, _, low, x = places()
    before = x if way == 1 else RING - 1 - x
    other_counts = low == (way + 1) // 2
    other = refs[0].shape[0] // 2 if way == 1 else modes
    step = distance % RING
    ref = refs[way * step % RING]
    mine = ref[pl.ds(first, modes), lanes]
    theirs = jnp.where(other_counts, ref[pl.ds(other + first, modes), lanes], 0.0)
    if distance < RING:
        return jnp.where(step <= before, mine, theirs)
    return jnp.where(step <= before, theirs, 0.0)


def forward_ends(key_ref, value_ref, log_ref, ends_ref, sub_ref, drive_ref, decay_ref, zero_ref):
    length, channels = key_ref.shape
    modes = log_ref.shape[0]
    span = length // SUBS
    decay_ref[...] = jnp.exp(-jnp.exp(log_ref[...]))
    zero_ref[...] = jnp.zeros_like(zero_ref)
    for tile, lanes in lane_tiles(channels):
        drive_ref[tile] = key_ref[:, lanes].astype(F32) * value_ref[:, lanes].astype(F32)
        decay = [spread(decay_ref, m, lanes) for m in range(modes)]

        def step(i, carry):
            now, lag = carry
            u = drive_ref[tile, strided(i, span)]
            lag = [decay[m] * (lag[m] + now[m]) for m in range(modes)]
            now = [decay[m] * now[m] + u for m in range(modes)]
            return now, lag

        zero = [zero_ref[...]] * modes
        now, lag = lax.fori_loop(0, span, step, (zero, zero), unroll=8)
        for m in range(modes):
            sub_ref[tile, strided(m, modes)] = now[m]
            sub_ref[tile, strided(SUBS * modes + m, modes)] = lag[m]
        power = jnp.exp(-span * jnp.exp(log_ref[:, lanes]))
        state = jnp.zeros_like(power)
        lagged = jnp.zeros_like(power)
        for j in range(SUBS):
            lagged = power * (lagged + span * state) + sub_ref[tile, pl.ds((SUBS + j) * modes, modes)]
            state = power * state + sub_ref[tile, pl.ds(j * modes, modes)]
        ends_ref[pl.ds(0, modes), lanes] = state
        ends_ref[pl.ds(modes, modes), lanes] = lagged


def forward_full(*refs):
    (query_ref, drive_ref, sub_ref, log_ref, residue_ref, skip_ref, *end_refs) = refs[:-6]
    (gated_ref, turned_ref, pre_ref, lead_ref, decay_ref, gain_ref) = refs[-6:]
    length, channels = query_ref.shape
    modes = log_ref.shape[0]
    span = length // SUBS
    rate = jnp.exp(log_ref[...])
    decay_ref[...] = jnp.exp(-rate)
    gain_ref[...] = residue_ref[...] * jnp.sqrt(2.0 * rate)
    for tile, lanes in lane_tiles(channels):
        rate = jnp.exp(log_ref[:, lanes])
        stretch = jnp.exp(-length * rate)
        power = jnp.exp(-span * rate)
        state = jnp.zeros_like(rate)
        lagged = jnp.zeros_like(rate)
        for distance in range(2 * RING - 1, 0, -1):
            lagged = stretch * (lagged + length * state) + nearby(end_refs, distance, 1, modes, modes, lanes)
            state = stretch * state + nearby(end_refs, distance, 1, 0, modes, lanes)
        for j in range(SUBS):
            now_rows, lag_rows = (pl.ds((j + k) * modes, modes) for k in (0, SUBS))
            lead_ref[tile, now_rows] = state
            lead_ref[tile, lag_rows] = lagged
            lagged = power * (lagged + span * state) + sub_ref[tile, lag_rows]
            state = power * state + sub_ref[tile, now_rows]
        decay = [spread(decay_ref, m, lanes) for m in range(modes)]
        gain = [spread(gain_ref, m, lanes) for m in range(modes)]
        skip = spread(skip_ref, 0, lanes)

        def step(i, now):
            place = strided(i, span)
            u = drive_ref[tile, place]
            now = [decay[m] * now[m] + u for m in range(modes)]
            pre_ref[tile, place] = tree_sum([gain[m] * now[m] for m in range(modes)]) + skip * u
            return now

        first = [lead_ref[tile, strided(m, modes)] for m in range(modes)]
        lax.fori_loop(0, span, step, first, unroll=8)
        gated_ref[:, lanes] = (query_ref[:, lanes].astype(F32) * pre_ref[tile]).astype(BF16)
    part = length // (RING * 4)
    y, high, core, _, _ = places()
    for i in range(RING * 4):
        on = lax.rem(i // 4 + RING - y, RING)
        there = lax.rem(i % 2 + core, 2) * RING + jnp.where(on == 0, 3, jnp.where(on == 2, 0, (on + 1) // 2))
        there = there * 2 + lax.rem(i // 2 % 2 + high, 2)
        turned_ref[pl.ds(pl.multiple_of(there * part, part), part)] = gated_ref[pl.ds(i * part, part)]


def backward_ends(
    grad_ref, query_ref, pre_ref, drive_ref, lead_ref, log_ref,
    grad_query_ref, back_ref, sums_ref, sub_ref, decay_ref, part_ref, zero_ref,
):
    length, channels = query_ref.shape
    modes = log_ref.shape[0]
    span = length // SUBS
    half = modes // 2
    decay_ref[...] = jnp.exp(-jnp.exp(log_ref[...]))
    zero_ref[...] = jnp.zeros_like(zero_ref)
    for tile, lanes in lane_tiles(channels):
        grad = grad_ref[:, lanes].astype(F32)
        grad_query_ref[:, lanes] = (grad * pre_ref[tile]).astype(BF16)
        back_ref[tile] = grad * query_ref[:, lanes].astype(F32)
        skip = zero_ref[...]
        for low in range(0, modes, half):
            group = range(low, low + half)
            decay = [spread(decay_ref, m, lanes) for m in group]

            def back_step(i, carry):
                start, lag, pair, lag_pair, skip = carry
                place = strided(span - 1 - i, span)
                u = drive_ref[tile, place]
                g = back_ref[tile, place]
                lag = [decay[m] * (lag[m] + start[m]) for m in range(half)]
                start = [decay[m] * start[m] + g for m in range(half)]
                pair = [pair[m] + u * start[m] for m in range(half)]
                lag_pair = [lag_pair[m] + u * lag[m] for m in range(half)]
                return start, lag, pair, lag_pair, (skip + g * u if low == 0 else skip)

            zero = [zero_ref[...]] * half
            start, lag, pair, lag_pair, skip = lax.fori_loop(
                0, span, back_step, (zero, zero, zero, zero, skip), unroll=8
            )
            for m in range(half):
                state = lead_ref[tile, strided(low + m, modes)]
                lagged = lead_ref[tile, strided(SUBS * modes + low + m, modes)]
                once = decay[m] * start[m]
                twice = decay[m] * (lag[m] + start[m])
                sub_ref[tile, strided(low + m, modes)] = start[m]
                part_ref[tile, strided(low + m, modes)] = pair[m] + state * once
                part_ref[tile, strided(SUBS * modes + low + m, modes)] = lag_pair[m] + state * twice + lagged * once
        total = jnp.sum(skip, axis=0, keepdims=True)
        sums_ref[pl.ds(3 * modes, SUBS), lanes] = jnp.broadcast_to(total, (SUBS, LANES))
        power = jnp.exp(-span * jnp.exp(log_ref[:, lanes]))
        start = jnp.zeros_like(power)
        pair = jnp.zeros_like(power)
        lag_pair = jnp.zeros_like(power)
        for j in range(SUBS - 1, -1, -1):
            start = power * start + sub_ref[tile, pl.ds(j * modes, modes)]
            pair = pair + part_ref[tile, pl.ds(j * modes, modes)]
            lag_pair = lag_pair + part_ref[tile, pl.ds((SUBS + j) * modes, modes)]
        sums_ref[pl.ds(0, modes), lanes] = start
        sums_ref[pl.ds(modes, modes), lanes] = pair
        sums_ref[pl.ds(2 * modes, modes), lanes] = lag_pair


def backward_full(*refs, scale):
    (key_ref, value_ref, back_ref, sub_ref, log_ref, residue_ref, skip_ref, *sum_refs) = refs[:-9]
    (grad_key_ref, grad_value_ref, grad_residue_ref, grad_decay_ref, grad_skip_ref) = refs[-9:-4]
    (decay_ref, gain_ref, lead_ref, drive_grad_ref) = refs[-4:]
    length, channels = key_ref.shape
    modes = log_ref.shape[0]
    span = length // SUBS
    rate = jnp.exp(log_ref[...])
    norm = jnp.sqrt(2.0 * rate)
    gain = residue_ref[...] * norm
    decay_ref[...] = jnp.exp(-rate)
    gain_ref[...] = gain
    pair = tree_sum([ref[pl.ds(2 * modes, modes)] for ref in sum_refs])
    lag_pair = tree_sum([ref[pl.ds(3 * modes, modes)] for ref in sum_refs])
    grad_residue_ref[...] = norm * pair * scale
    grad_decay_ref[...] = gain * (0.5 * pair - rate * lag_pair) * scale
    grad_skip_ref[...] = tree_sum([ref[pl.ds(4 * modes, SUBS)] for ref in sum_refs]) * scale
    for tile, lanes in lane_tiles(channels):
        rate = jnp.exp(log_ref[:, lanes])
        stretch = jnp.exp(-length * rate)
        power = jnp.exp(-span * rate)
        start = jnp.zeros_like(rate)
        for distance in range(2 * RING - 1, 0, -1):
            start = stretch * start + nearby(sum_refs, distance, -1, 0, modes, lanes)
        for j in range(SUBS - 1, -1, -1):
            lead_ref[tile, pl.ds(j * modes, modes)] = start
            start = power * start + sub_ref[tile, pl.ds(j * modes, modes)]
        decay = [spread(decay_ref, m, lanes) for m in range(modes)]
        gain = [spread(gain_ref, m, lanes) for m in range(modes)]
        skip = spread(skip_ref, 0, lanes)

        def step(i, now):
            place = strided(span - 1 - i, span)
            g = back_ref[tile, place]
            now = [decay[m] * now[m] + g for m in range(modes)]
            drive_grad_ref[tile, place] = tree_sum([gain[m] * now[m] for m in range(modes)]) + skip * g
            return now

        first = [lead_ref[tile, strided(m, modes)] for m in range(modes)]
        lax.fori_loop(0, span, step, first, unroll=8)
        drive_grad = drive_grad_ref[tile]
        grad_key_ref[:, lanes] = (drive_grad * value_ref[:, lanes].astype(F32)).astype(BF16)
        grad_value_ref[:, lanes] = (drive_grad * key_ref[:, lanes].astype(F32)).astype(BF16)


def call(body, args, outs, scratch, micros, name):
    whole = pl.BlockSpec(memory_space=pltpu.VMEM)
    return pl.pallas_call(
        body,
        out_shape=[jax.ShapeDtypeStruct(o.shape, o.dtype) for o in outs],
        in_specs=[whole] * len(args),
        out_specs=[whole] * len(outs),
        scratch_shapes=[pltpu.VMEM(shape, F32) for shape in scratch],
        compiler_params=pltpu.CompilerParams(vmem_limit_bytes=32 * 2**20),
        cost_estimate=pl.CostEstimate(flops=int(micros * 1.15e9), bytes_accessed=0, transcendentals=0),
        name=name,
    )(*args)


def like(shape, dtype):
    return jax.ShapeDtypeStruct(shape, dtype)


def spread_over_x(value):
    return [value] + [hop(value, x=offset) for offset in range(1, RING)]


def together(*values):
    return lax.optimization_barrier(values)


def local(queries, key_proj, value_proj, skip_gain, residue, log_decay, out_weight, cotangent):
    length, channels = queries.shape
    modes = residue.shape[0]
    blocks = lax.axis_size("seq")
    scale = 1.0 / math.sqrt(length * blocks)
    skip_row = skip_gain.reshape(1, channels)
    tiles = channels // LANES
    wide = like((tiles, length, LANES), F32)
    narrow = like((length, channels), BF16)
    table = (modes, channels)

    block, log_first = together(gather_z(cotangent), log_decay)
    before_own, after_other = hop(block[0], y=1), hop(block[1], y=-1)
    ends, subs, driving = call(
        forward_ends,
        (key_proj, value_proj, log_first),
        (like((2 * modes, channels), F32), like((tiles, 2 * SUBS * modes, LANES), F32), wide),
        [table, (SUBS, LANES)],
        0.1,
        "forward_ends",
    )
    ends_pair = jnp.concatenate([ends, hop(ends, pair=1)])
    before_own, after_other, ends_pair = together(before_own, after_other, ends_pair)
    before_other, after_own = hop(block[1], y=1), hop(block[0], y=-1)
    earlier = spread_over_x(ends_pair)
    gated, turned, pre_gate, lead = call(
        forward_full,
        (queries, driving, subs, log_decay, residue, skip_row, *earlier),
        (narrow, narrow, wide, like((tiles, 2 * SUBS * modes, LANES), F32)),
        [table, table],
        0.1,
        "forward_full",
    )
    before_own, after_other, turned = together(before_own, after_other, turned)
    far_own, far_other = hop(before_own, y=1), hop(after_other, y=-1)
    before_other, after_own, turned = together(before_other, after_own, turned)
    near_first, near_rest, far_first, far_rest = project(turned, out_weight)
    got_first, got_rest = hop(far_first, core=1), hop(far_rest, core=1)
    gated_pair = jnp.concatenate([gated, hop(gated, pair=1)])
    opposite = add(near_first, got_first).astype(BF16)
    far_own, far_other, opposite = together(far_own, far_other, opposite)
    cot_rows = place_blocks(
        (block[0], before_own, after_own, far_own), (block[1], before_other, after_other, far_other)
    )
    cot_rows, got_rest = together(cot_rows.reshape(2 * length, -1), got_rest)

    half = out_weight.shape[1] // 2
    low_weight = lax.dynamic_slice(out_weight, (0, places()[3] * half), (channels, half))
    weights = {2: weigh(gated_pair, cot_rows, scale, 2)}
    cot_rows, weights[2] = together(cot_rows, weights[2])
    grad_parts = lax.dot_general(cot_rows, low_weight, (((1,), (1,)), ((), ())), preferred_element_type=F32)
    cot_rows, grad_parts, got_rest = together(cot_rows, grad_parts, got_rest)
    theirs = hop(grad_parts[length:].astype(BF16), pair=1)
    part = opposite.shape[0] // 2
    low_sum, high_sum = hop(opposite[:part], y=1), hop(opposite[part:], y=-1)
    above, below, own = (
        add(near_rest[i * 2 * part : (i + 1) * 2 * part], got_rest[i * 2 * part : (i + 1) * 2 * part]) for i in range(3)
    )
    above = jnp.concatenate([add(above[:part], low_sum), above[part:]]).astype(BF16)
    below = jnp.concatenate([below[:part], add(below[part:], high_sum)]).astype(BF16)
    for r in (1, 3, 0):
        weights[r] = weigh(gated_pair, cot_rows, scale, r)
    cut = channels // 2
    upper, lower = hop(weights[2][:cut], x=1), hop(weights[2][cut:], x=-1)
    up_sum = add(weights[1][:cut], upper).astype(BF16)
    down_sum = add(weights[3][cut:], lower).astype(BF16)
    up_rest, down_rest = weights[1][cut:], weights[3][:cut]
    theirs, up_sum, down_sum, up_rest, down_rest = together(theirs, up_sum, down_sum, up_rest, down_rest)
    up_rest, down_rest = hop(up_rest, x=1), hop(down_rest, x=-1)
    grad_gated = add(grad_parts[:length], theirs)
    own = add(own, hop(above, y=1), hop(below, y=-1))
    leaving = own[part:].astype(BF16)
    width = leaving.shape[1] // 2
    halfway = hop(leaving[:, width:], z=-1)
    crossed = hop(leaving[:, :width], z=2)

    grad_query, back, sums, back_subs = call(
        backward_ends,
        (grad_gated, queries, pre_gate, driving, lead, log_decay),
        (narrow, wide, like((3 * modes + SUBS, channels), F32), like((tiles, SUBS * modes, LANES), F32)),
        [table, (tiles, 2 * SUBS * modes, LANES), (SUBS, LANES)],
        2.0,
        "backward_ends",
    )
    sums, up_rest, down_rest = together(sums, up_rest, down_rest)
    up_sum, down_sum = hop(up_sum, x=1), hop(down_sum, x=-1)
    others = hop(sums, pair=1)
    sums_pair = jnp.concatenate([sums[:modes], others[:modes], sums[modes:] + others[modes:]])
    sums_pair, up_sum, down_sum = together(sums_pair, up_sum, down_sum)
    crossed = jnp.concatenate([crossed, hop(halfway, z=-1)], axis=1)
    mixed = add(own[:part], crossed).astype(BF16)
    all_sums = spread_over_x(sums_pair)
    grad_weight = jnp.concatenate(
        [add(weights[0][:cut], up_sum, down_rest), add(weights[0][cut:], up_rest, down_sum)]
    ).astype(BF16)
    grad_key, grad_value, grad_residue, grad_decay, grad_skip = call(
        functools.partial(backward_full, scale=scale),
        (key_proj, value_proj, back, back_subs, log_decay, residue, skip_row, *all_sums),
        (narrow, narrow, like(table, F32), like(table, F32), like((SUBS, channels), F32)),
        [table, table, (tiles, SUBS * modes, LANES), (tiles, length, LANES)],
        0.1,
        "backward_full",
    )
    return (
        mixed,
        grad_query,
        grad_key,
        grad_value,
        grad_weight,
        grad_residue,
        grad_decay,
        grad_skip[0],
    )


def solution(mesh):
    in_specs = (
        P("seq", "chan"),
        P("seq", "chan"),
        P("seq", "chan"),
        P("chan"),
        P(None, "chan"),
        P(None, "chan"),
        P("chan", None),
        P(("seq", "chan"), None),
    )
    out_specs = (
        P(("seq", "chan"), None),
        P("seq", "chan"),
        P("seq", "chan"),
        P("seq", "chan"),
        P("chan", "seq"),
        P(None, "chan"),
        P(None, "chan"),
        P("chan"),
    )
    return jax.shard_map(local, mesh=mesh, in_specs=in_specs, out_specs=out_specs, check_vma=False)
```

```python
import functools
import itertools
import math

import jax
import jax.numpy as jnp
from jax import lax
from jax.experimental import pallas as pl
from jax.experimental.pallas import tpu as pltpu
from jax.sharding import PartitionSpec as P

RING = 4
SUBS = 8
LANES = 128
F32 = jnp.float32
BF16 = jnp.bfloat16


def strided(first, step):
    return pl.ds(first, SUBS, stride=step)


def spread(ref, mode, lanes):
    return jnp.broadcast_to(ref[pl.ds(mode, 1), lanes], (SUBS, LANES))


def tree_sum(parts):
    while len(parts) > 1:
        parts = [a + b for a, b in zip(parts[::2], parts[1::2])] + parts[len(parts) & ~1 :]
    return parts[0]


def lane_tiles(channels):
    return [(tile, pl.ds(tile * LANES, LANES)) for tile in range(channels // LANES)]


def places():
    chan, seq = lax.axis_index("chan"), lax.axis_index("seq")
    return chan // 4, lax.rem(chan // 2, 2), lax.rem(chan, 2), seq // RING, lax.rem(seq, RING)


def hop(value, x=0, y=0, z=0, core=0, pair=0):
    moves = []
    for i, j, k, c in itertools.product(range(RING), range(RING), range(RING), range(2)):
        there = ((i + x) % RING, (j + y) % RING, ((k + z) % RING) ^ pair, c ^ core)
        moves.append(tuple(((b * 2 + d // 2) * 2 + e) * 2 * RING + d % 2 * RING + a for a, b, d, e in ((i, j, k, c), there)))
    return lax.ppermute(value, ("chan", "seq"), moves)


def gather_z(cotangent):
    _, high, _, low, _ = places()
    tokens, width = cotangent.shape
    half = width // 2
    mine = lax.dynamic_slice(cotangent, (0, low * half), (tokens, half))
    theirs = lax.dynamic_slice(cotangent, (0, (1 - low) * half), (tokens, half))
    above, below, across = hop(theirs, z=1), hop(theirs, z=-1), hop(mine, z=2)
    stack = jnp.where(high == 0, jnp.stack([mine, across]), jnp.stack([across, mine]))
    same, differ = jnp.where(low == 1, above, below), jnp.where(low == 1, below, above)
    other = jnp.where(high == 0, jnp.stack([same, differ]), jnp.stack([differ, same]))
    return jnp.stack([stack, other])


def place_blocks(*sides):
    y, _, core, _, _ = places()
    _, tokens, half = sides[0][0].shape
    whole = jnp.zeros((2, RING, 2, 2, tokens, half), BF16)
    for step, blocks in zip((0, RING - 1, 1, 2), zip(*sides)):
        row = lax.rem(y + step, RING)
        for side, block in enumerate(blocks):
            for part, at_core in ((block, core), (hop(block, core=1), 1 - core)):
                whole = lax.dynamic_update_slice(whole, part[None, None, :, None], (side, row, 0, at_core, 0, 0))
    return whole


def add(*parts):
    return functools.reduce(jnp.add, [part.astype(F32) for part in parts])


def project_tile(rows_ref, weight_ref, *out_refs):
    product = jnp.dot(rows_ref[...], weight_ref[...], preferred_element_type=F32).astype(BF16)
    first = 0
    for ref in out_refs:
        ref[...] = product[first : first + ref.shape[0]]
        first += ref.shape[0]


def project(turned, out_weight):
    rows, depth = turned.shape
    width = out_weight.shape[1]
    tile = 1024
    sizes = [rows // 8, 3 * rows // 8] * 2
    return pl.pallas_call(
        project_tile,
        grid=(width // tile,),
        out_shape=[jax.ShapeDtypeStruct((size, width), BF16) for size in sizes],
        in_specs=[pl.BlockSpec((rows, depth), lambda i: (0, 0)), pl.BlockSpec((depth, tile), lambda i: (0, i))],
        out_specs=[pl.BlockSpec((size, tile), lambda i: (0, i)) for size in sizes],
        compiler_params=pltpu.CompilerParams(vmem_limit_bytes=32 * 2**20),
        cost_estimate=pl.CostEstimate(
            flops=2 * rows * depth * width, bytes_accessed=2 * width * (rows + depth), transcendentals=0
        ),
        name="project",
    )(turned, out_weight)


def weigh(gated, cot_rows, scale, r):
    width = cot_rows.shape[1] // RING
    first = lax.rem(places()[4] + r, RING) * width
    columns = lax.dynamic_slice(cot_rows, (0, first), (cot_rows.shape[0], width))
    product = lax.dot_general(gated, columns, (((0,), (0,)), ((), ())), preferred_element_type=F32)
    return (product * scale).astype(BF16)


def nearby(refs, distance, way, first, modes, lanes):
    _, _, _, low, x = places()
    before = x if way == 1 else RING - 1 - x
    other_counts = low == (way + 1) // 2
    other = refs[0].shape[0] // 2 if way == 1 else modes
    step = distance % RING
    ref = refs[way * step % RING]
    mine = ref[pl.ds(first, modes), lanes]
    theirs = jnp.where(other_counts, ref[pl.ds(other + first, modes), lanes], 0.0)
    if distance < RING:
        return jnp.where(step <= before, mine, theirs)
    return jnp.where(step <= before, theirs, 0.0)


def forward_ends(key_ref, value_ref, log_ref, ends_ref, sub_ref, drive_ref, decay_ref, zero_ref):
    length, channels = key_ref.shape
    modes = log_ref.shape[0]
    span = length // SUBS
    decay_ref[...] = jnp.exp(-jnp.exp(log_ref[...]))
    zero_ref[...] = jnp.zeros_like(zero_ref)
    for tile, lanes in lane_tiles(channels):
        drive_ref[tile] = key_ref[:, lanes].astype(F32) * value_ref[:, lanes].astype(F32)
        decay = [spread(decay_ref, m, lanes) for m in range(modes)]

        def step(i, carry):
            now, lag = carry
            u = drive_ref[tile, strided(i, span)]
            lag = [decay[m] * (lag[m] + now[m]) for m in range(modes)]
            now = [decay[m] * now[m] + u for m in range(modes)]
            return now, lag

        zero = [zero_ref[...]] * modes
        now, lag = lax.fori_loop(0, span, step, (zero, zero), unroll=8)
        for m in range(modes):
            sub_ref[tile, strided(m, modes)] = now[m]
            sub_ref[tile, strided(SUBS * modes + m, modes)] = lag[m]
        power = jnp.exp(-span * jnp.exp(log_ref[:, lanes]))
        state = jnp.zeros_like(power)
        lagged = jnp.zeros_like(power)
        for j in range(SUBS):
            lagged = power * (lagged + span * state) + sub_ref[tile, pl.ds((SUBS + j) * modes, modes)]
            state = power * state + sub_ref[tile, pl.ds(j * modes, modes)]
        ends_ref[pl.ds(0, modes), lanes] = state
        ends_ref[pl.ds(modes, modes), lanes] = lagged


def forward_full(*refs):
    (query_ref, drive_ref, sub_ref, log_ref, residue_ref, skip_ref, *end_refs) = refs[:-6]
    (gated_ref, turned_ref, pre_ref, lead_ref, decay_ref, gain_ref) = refs[-6:]
    length, channels = query_ref.shape
    modes = log_ref.shape[0]
    span = length // SUBS
    rate = jnp.exp(log_ref[...])
    decay_ref[...] = jnp.exp(-rate)
    gain_ref[...] = residue_ref[...] * jnp.sqrt(2.0 * rate)
    for tile, lanes in lane_tiles(channels):
        rate = jnp.exp(log_ref[:, lanes])
        stretch = jnp.exp(-length * rate)
        power = jnp.exp(-span * rate)
        state = jnp.zeros_like(rate)
        lagged = jnp.zeros_like(rate)
        for distance in range(2 * RING - 1, 0, -1):
            lagged = stretch * (lagged + length * state) + nearby(end_refs, distance, 1, modes, modes, lanes)
            state = stretch * state + nearby(end_refs, distance, 1, 0, modes, lanes)
        for j in range(SUBS):
            now_rows, lag_rows = (pl.ds((j + k) * modes, modes) for k in (0, SUBS))
            lead_ref[tile, now_rows] = state
            lead_ref[tile, lag_rows] = lagged
            lagged = power * (lagged + span * state) + sub_ref[tile, lag_rows]
            state = power * state + sub_ref[tile, now_rows]
        decay = [spread(decay_ref, m, lanes) for m in range(modes)]
        gain = [spread(gain_ref, m, lanes) for m in range(modes)]
        skip = spread(skip_ref, 0, lanes)

        def step(i, now):
            place = strided(i, span)
            u = drive_ref[tile, place]
            now = [decay[m] * now[m] + u for m in range(modes)]
            pre_ref[tile, place] = tree_sum([gain[m] * now[m] for m in range(modes)]) + skip * u
            return now

        first = [lead_ref[tile, strided(m, modes)] for m in range(modes)]
        lax.fori_loop(0, span, step, first, unroll=8)
        gated_ref[:, lanes] = (query_ref[:, lanes].astype(F32) * pre_ref[tile]).astype(BF16)
    part = length // (RING * 4)
    y, high, core, _, _ = places()
    for i in range(RING * 4):
        on = lax.rem(i // 4 + RING - y, RING)
        there = lax.rem(i % 2 + core, 2) * RING + jnp.where(on == 0, 3, jnp.where(on == 2, 0, (on + 1) // 2))
        there = there * 2 + lax.rem(i // 2 % 2 + high, 2)
        turned_ref[pl.ds(pl.multiple_of(there * part, part), part)] = gated_ref[pl.ds(i * part, part)]


def backward_ends(
    grad_ref, query_ref, pre_ref, drive_ref, lead_ref, log_ref,
    grad_query_ref, back_ref, sums_ref, sub_ref, decay_ref, part_ref, zero_ref,
):
    length, channels = query_ref.shape
    modes = log_ref.shape[0]
    span = length // SUBS
    half = modes // 2
    decay_ref[...] = jnp.exp(-jnp.exp(log_ref[...]))
    zero_ref[...] = jnp.zeros_like(zero_ref)
    for tile, lanes in lane_tiles(channels):
        grad = grad_ref[:, lanes].astype(F32)
        grad_query_ref[:, lanes] = (grad * pre_ref[tile]).astype(BF16)
        back_ref[tile] = grad * query_ref[:, lanes].astype(F32)
        skip = zero_ref[...]
        for low in range(0, modes, half):
            group = range(low, low + half)
            decay = [spread(decay_ref, m, lanes) for m in group]

            def back_step(i, carry):
                start, lag, pair, lag_pair, skip = carry
                place = strided(span - 1 - i, span)
                u = drive_ref[tile, place]
                g = back_ref[tile, place]
                lag = [decay[m] * (lag[m] + start[m]) for m in range(half)]
                start = [decay[m] * start[m] + g for m in range(half)]
                pair = [pair[m] + u * start[m] for m in range(half)]
                lag_pair = [lag_pair[m] + u * lag[m] for m in range(half)]
                return start, lag, pair, lag_pair, (skip + g * u if low == 0 else skip)

            zero = [zero_ref[...]] * half
            start, lag, pair, lag_pair, skip = lax.fori_loop(
                0, span, back_step, (zero, zero, zero, zero, skip), unroll=8
            )
            for m in range(half):
                state = lead_ref[tile, strided(low + m, modes)]
                lagged = lead_ref[tile, strided(SUBS * modes + low + m, modes)]
                once = decay[m] * start[m]
                twice = decay[m] * (lag[m] + start[m])
                sub_ref[tile, strided(low + m, modes)] = start[m]
                part_ref[tile, strided(low + m, modes)] = pair[m] + state * once
                part_ref[tile, strided(SUBS * modes + low + m, modes)] = lag_pair[m] + state * twice + lagged * once
        total = jnp.sum(skip, axis=0, keepdims=True)
        sums_ref[pl.ds(3 * modes, SUBS), lanes] = jnp.broadcast_to(total, (SUBS, LANES))
        power = jnp.exp(-span * jnp.exp(log_ref[:, lanes]))
        start = jnp.zeros_like(power)
        pair = jnp.zeros_like(power)
        lag_pair = jnp.zeros_like(power)
        for j in range(SUBS - 1, -1, -1):
            start = power * start + sub_ref[tile, pl.ds(j * modes, modes)]
            pair = pair + part_ref[tile, pl.ds(j * modes, modes)]
            lag_pair = lag_pair + part_ref[tile, pl.ds((SUBS + j) * modes, modes)]
        sums_ref[pl.ds(0, modes), lanes] = start
        sums_ref[pl.ds(modes, modes), lanes] = pair
        sums_ref[pl.ds(2 * modes, modes), lanes] = lag_pair


def backward_full(*refs, scale):
    (key_ref, value_ref, back_ref, sub_ref, log_ref, residue_ref, skip_ref, *sum_refs) = refs[:-9]
    (grad_key_ref, grad_value_ref, grad_residue_ref, grad_decay_ref, grad_skip_ref) = refs[-9:-4]
    (decay_ref, gain_ref, lead_ref, drive_grad_ref) = refs[-4:]
    length, channels = key_ref.shape
    modes = log_ref.shape[0]
    span = length // SUBS
    rate = jnp.exp(log_ref[...])
    norm = jnp.sqrt(2.0 * rate)
    gain = residue_ref[...] * norm
    decay_ref[...] = jnp.exp(-rate)
    gain_ref[...] = gain
    pair = tree_sum([ref[pl.ds(2 * modes, modes)] for ref in sum_refs])
    lag_pair = tree_sum([ref[pl.ds(3 * modes, modes)] for ref in sum_refs])
    grad_residue_ref[...] = norm * pair * scale
    grad_decay_ref[...] = gain * (0.5 * pair - rate * lag_pair) * scale
    grad_skip_ref[...] = tree_sum([ref[pl.ds(4 * modes, SUBS)] for ref in sum_refs]) * scale
    for tile, lanes in lane_tiles(channels):
        rate = jnp.exp(log_ref[:, lanes])
        stretch = jnp.exp(-length * rate)
        power = jnp.exp(-span * rate)
        start = jnp.zeros_like(rate)
        for distance in range(2 * RING - 1, 0, -1):
            start = stretch * start + nearby(sum_refs, distance, -1, 0, modes, lanes)
        for j in range(SUBS - 1, -1, -1):
            lead_ref[tile, pl.ds(j * modes, modes)] = start
            start = power * start + sub_ref[tile, pl.ds(j * modes, modes)]
        decay = [spread(decay_ref, m, lanes) for m in range(modes)]
        gain = [spread(gain_ref, m, lanes) for m in range(modes)]
        skip = spread(skip_ref, 0, lanes)

        def step(i, now):
            place = strided(span - 1 - i, span)
            g = back_ref[tile, place]
            now = [decay[m] * now[m] + g for m in range(modes)]
            drive_grad_ref[tile, place] = tree_sum([gain[m] * now[m] for m in range(modes)]) + skip * g
            return now

        first = [lead_ref[tile, strided(m, modes)] for m in range(modes)]
        lax.fori_loop(0, span, step, first, unroll=8)
        drive_grad = drive_grad_ref[tile]
        grad_key_ref[:, lanes] = (drive_grad * value_ref[:, lanes].astype(F32)).astype(BF16)
        grad_value_ref[:, lanes] = (drive_grad * key_ref[:, lanes].astype(F32)).astype(BF16)


def call(body, args, outs, scratch, micros, name):
    whole = pl.BlockSpec(memory_space=pltpu.VMEM)
    return pl.pallas_call(
        body,
        out_shape=[jax.ShapeDtypeStruct(o.shape, o.dtype) for o in outs],
        in_specs=[whole] * len(args),
        out_specs=[whole] * len(outs),
        scratch_shapes=[pltpu.VMEM(shape, F32) for shape in scratch],
        compiler_params=pltpu.CompilerParams(vmem_limit_bytes=32 * 2**20),
        cost_estimate=pl.CostEstimate(flops=int(micros * 1.15e9), bytes_accessed=0, transcendentals=0),
        name=name,
    )(*args)


def like(shape, dtype):
    return jax.ShapeDtypeStruct(shape, dtype)


def spread_over_x(value):
    return [value] + [hop(value, x=offset) for offset in range(1, RING)]


def together(*values):
    return lax.optimization_barrier(values)


def local(queries, key_proj, value_proj, skip_gain, residue, log_decay, out_weight, cotangent):
    length, channels = queries.shape
    modes = residue.shape[0]
    blocks = lax.axis_size("seq")
    scale = 1.0 / math.sqrt(length * blocks)
    skip_row = skip_gain.reshape(1, channels)
    tiles = channels // LANES
    wide = like((tiles, length, LANES), F32)
    narrow = like((length, channels), BF16)
    table = (modes, channels)

    block, log_first = together(gather_z(cotangent), log_decay)
    before_own, after_other = hop(block[0], y=1), hop(block[1], y=-1)
    ends, subs, driving = call(
        forward_ends,
        (key_proj, value_proj, log_first),
        (like((2 * modes, channels), F32), like((tiles, 2 * SUBS * modes, LANES), F32), wide),
        [table, (SUBS, LANES)],
        0.1,
        "forward_ends",
    )
    ends_pair = jnp.concatenate([ends, hop(ends, pair=1)])
    before_own, after_other, ends_pair = together(before_own, after_other, ends_pair)
    before_other, after_own = hop(block[1], y=1), hop(block[0], y=-1)
    earlier = spread_over_x(ends_pair)
    gated, turned, pre_gate, lead = call(
        forward_full,
        (queries, driving, subs, log_decay, residue, skip_row, *earlier),
        (narrow, narrow, wide, like((tiles, 2 * SUBS * modes, LANES), F32)),
        [table, table],
        0.1,
        "forward_full",
    )
    before_own, after_other, turned = together(before_own, after_other, turned)
    far_own, far_other = hop(before_own, y=1), hop(after_other, y=-1)
    before_other, after_own, turned = together(before_other, after_own, turned)
    near_first, near_rest, far_first, far_rest = project(turned, out_weight)
    got_first, got_rest = hop(far_first, core=1), hop(far_rest, core=1)
    gated_pair = jnp.concatenate([gated, hop(gated, pair=1)])
    opposite = add(near_first, got_first).astype(BF16)
    far_own, far_other, opposite = together(far_own, far_other, opposite)
    cot_rows = place_blocks(
        (block[0], before_own, after_own, far_own), (block[1], before_other, after_other, far_other)
    )
    cot_rows, got_rest = together(cot_rows.reshape(2 * length, -1), got_rest)

    half = out_weight.shape[1] // 2
    low_weight = lax.dynamic_slice(out_weight, (0, places()[3] * half), (channels, half))
    weights = {2: weigh(gated_pair, cot_rows, scale, 2)}
    cot_rows, weights[2] = together(cot_rows, weights[2])
    grad_parts = lax.dot_general(cot_rows, low_weight, (((1,), (1,)), ((), ())), preferred_element_type=F32)
    cot_rows, grad_parts, got_rest = together(cot_rows, grad_parts, got_rest)
    theirs = hop(grad_parts[length:].astype(BF16), pair=1)
    part = opposite.shape[0] // 2
    low_sum, high_sum = hop(opposite[:part], y=1), hop(opposite[part:], y=-1)
    above, below, own = (
        add(near_rest[i * 2 * part : (i + 1) * 2 * part], got_rest[i * 2 * part : (i + 1) * 2 * part]) for i in range(3)
    )
    above = jnp.concatenate([add(above[:part], low_sum), above[part:]]).astype(BF16)
    below = jnp.concatenate([below[:part], add(below[part:], high_sum)]).astype(BF16)
    for r in (1, 3, 0):
        weights[r] = weigh(gated_pair, cot_rows, scale, r)
    cut = channels // 2
    upper, lower = hop(weights[2][:cut], x=1), hop(weights[2][cut:], x=-1)
    up_sum = add(weights[1][:cut], upper).astype(BF16)
    down_sum = add(weights[3][cut:], lower).astype(BF16)
    up_rest, down_rest = weights[1][cut:], weights[3][:cut]
    theirs, up_sum, down_sum, up_rest, down_rest = together(theirs, up_sum, down_sum, up_rest, down_rest)
    up_rest, down_rest = hop(up_rest, x=1), hop(down_rest, x=-1)
    grad_gated = add(grad_parts[:length], theirs)
    own = add(own, hop(above, y=1), hop(below, y=-1))
    leaving = own[part:].astype(BF16)
    width = leaving.shape[1] // 2
    halfway = hop(leaving[:, width:], z=-1)
    crossed = hop(leaving[:, :width], z=2)

    grad_query, back, sums, back_subs = call(
        backward_ends,
        (grad_gated, queries, pre_gate, driving, lead, log_decay),
        (narrow, wide, like((3 * modes + SUBS, channels), F32), like((tiles, SUBS * modes, LANES), F32)),
        [table, (tiles, 2 * SUBS * modes, LANES), (SUBS, LANES)],
        2.0,
        "backward_ends",
    )
    sums, up_rest, down_rest = together(sums, up_rest, down_rest)
    up_sum, down_sum = hop(up_sum, x=1), hop(down_sum, x=-1)
    others = hop(sums, pair=1)
    sums_pair = jnp.concatenate([sums[:modes], others[:modes], sums[modes:] + others[modes:]])
    crossed = jnp.concatenate([crossed, hop(halfway, z=-1)], axis=1)
    mixed = add(own[:part], crossed).astype(BF16)
    all_sums = spread_over_x(sums_pair)
    all_sums[0], up_sum, down_sum = together(all_sums[0], up_sum, down_sum)
    grad_weight = jnp.concatenate(
        [add(weights[0][:cut], up_sum, down_rest), add(weights[0][cut:], up_rest, down_sum)]
    ).astype(BF16)
    grad_key, grad_value, grad_residue, grad_decay, grad_skip = call(
        functools.partial(backward_full, scale=scale),
        (key_proj, value_proj, back, back_subs, log_decay, residue, skip_row, *all_sums),
        (narrow, narrow, like(table, F32), like(table, F32), like((SUBS, channels), F32)),
        [table, table, (tiles, SUBS * modes, LANES), (tiles, length, LANES)],
        0.1,
        "backward_full",
    )
    return (
        mixed,
        grad_query,
        grad_key,
        grad_value,
        grad_weight,
        grad_residue,
        grad_decay,
        grad_skip[0],
    )


def solution(mesh):
    in_specs = (
        P("seq", "chan"),
        P("seq", "chan"),
        P("seq", "chan"),
        P("chan"),
        P(None, "chan"),
        P(None, "chan"),
        P("chan", None),
        P(("seq", "chan"), None),
    )
    out_specs = (
        P(("seq", "chan"), None),
        P("seq", "chan"),
        P("seq", "chan"),
        P("seq", "chan"),
        P("chan", "seq"),
        P(None, "chan"),
        P(None, "chan"),
        P("chan"),
    )
    return jax.shard_map(local, mesh=mesh, in_specs=in_specs, out_specs=out_specs, check_vma=False)
```

```python
import functools
import itertools
import math

import jax
import jax.numpy as jnp
from jax import lax
from jax.experimental import pallas as pl
from jax.experimental.pallas import tpu as pltpu
from jax.sharding import PartitionSpec as P

RING = 4
SUBS = 8
LANES = 128
F32 = jnp.float32
BF16 = jnp.bfloat16


def strided(first, step):
    return pl.ds(first, SUBS, stride=step)


def spread(ref, mode, lanes):
    return jnp.broadcast_to(ref[pl.ds(mode, 1), lanes], (SUBS, LANES))


def tree_sum(parts):
    while len(parts) > 1:
        parts = [a + b for a, b in zip(parts[::2], parts[1::2])] + parts[len(parts) & ~1 :]
    return parts[0]


def lane_tiles(channels):
    return [(tile, pl.ds(tile * LANES, LANES)) for tile in range(channels // LANES)]


def places():
    chan, seq = lax.axis_index("chan"), lax.axis_index("seq")
    return chan // 4, lax.rem(chan // 2, 2), lax.rem(chan, 2), seq // RING, lax.rem(seq, RING)


def hop(value, x=0, y=0, z=0, core=0, pair=0):
    moves = []
    for i, j, k, c in itertools.product(range(RING), range(RING), range(RING), range(2)):
        there = ((i + x) % RING, (j + y) % RING, ((k + z) % RING) ^ pair, c ^ core)
        moves.append(tuple(((b * 2 + d // 2) * 2 + e) * 2 * RING + d % 2 * RING + a for a, b, d, e in ((i, j, k, c), there)))
    return lax.ppermute(value, ("chan", "seq"), moves)


def gather_z(cotangent):
    _, high, _, low, _ = places()
    tokens, width = cotangent.shape
    half = width // 2
    mine = lax.dynamic_slice(cotangent, (0, low * half), (tokens, half))
    theirs = lax.dynamic_slice(cotangent, (0, (1 - low) * half), (tokens, half))
    above, below, across = hop(theirs, z=1), hop(theirs, z=-1), hop(mine, z=2)
    stack = jnp.where(high == 0, jnp.stack([mine, across]), jnp.stack([across, mine]))
    same, differ = jnp.where(low == 1, above, below), jnp.where(low == 1, below, above)
    other = jnp.where(high == 0, jnp.stack([same, differ]), jnp.stack([differ, same]))
    return jnp.stack([stack, other])


def place_blocks(*sides):
    y, _, core, _, _ = places()
    _, tokens, half = sides[0][0].shape
    whole = jnp.zeros((2, RING, 2, 2, tokens, half), BF16)
    for step, blocks in zip((0, RING - 1, 1, 2), zip(*sides)):
        row = lax.rem(y + step, RING)
        for side, block in enumerate(blocks):
            for part, at_core in ((block, core), (hop(block, core=1), 1 - core)):
                whole = lax.dynamic_update_slice(whole, part[None, None, :, None], (side, row, 0, at_core, 0, 0))
    return whole


def add(*parts):
    return functools.reduce(jnp.add, [part.astype(F32) for part in parts])


def project_tile(rows_ref, weight_ref, *out_refs):
    product = jnp.dot(rows_ref[...], weight_ref[...], preferred_element_type=F32).astype(BF16)
    first = 0
    for ref in out_refs:
        ref[...] = product[first : first + ref.shape[0]]
        first += ref.shape[0]


def project(turned, out_weight):
    rows, depth = turned.shape
    width = out_weight.shape[1]
    tile = 1024
    sizes = [rows // 8, 3 * rows // 8] * 2
    return pl.pallas_call(
        project_tile,
        grid=(width // tile,),
        out_shape=[jax.ShapeDtypeStruct((size, width), BF16) for size in sizes],
        in_specs=[pl.BlockSpec((rows, depth), lambda i: (0, 0)), pl.BlockSpec((depth, tile), lambda i: (0, i))],
        out_specs=[pl.BlockSpec((size, tile), lambda i: (0, i)) for size in sizes],
        compiler_params=pltpu.CompilerParams(vmem_limit_bytes=32 * 2**20),
        cost_estimate=pl.CostEstimate(
            flops=2 * rows * depth * width, bytes_accessed=2 * width * (rows + depth), transcendentals=0
        ),
        name="project",
    )(turned, out_weight)


def weigh(gated, cot_rows, scale, r):
    width = cot_rows.shape[1] // RING
    first = lax.rem(places()[4] + r, RING) * width
    columns = lax.dynamic_slice(cot_rows, (0, first), (cot_rows.shape[0], width))
    product = lax.dot_general(gated, columns, (((0,), (0,)), ((), ())), preferred_element_type=F32)
    return (product * scale).astype(BF16)


def nearby(refs, distance, way, first, modes, lanes):
    _, _, _, low, x = places()
    before = x if way == 1 else RING - 1 - x
    other_counts = low == (way + 1) // 2
    other = refs[0].shape[0] // 2 if way == 1 else modes
    step = distance % RING
    ref = refs[way * step % RING]
    mine = ref[pl.ds(first, modes), lanes]
    theirs = jnp.where(other_counts, ref[pl.ds(other + first, modes), lanes], 0.0)
    if distance < RING:
        return jnp.where(step <= before, mine, theirs)
    return jnp.where(step <= before, theirs, 0.0)


def forward_ends(key_ref, value_ref, log_ref, ends_ref, sub_ref, drive_ref, decay_ref, zero_ref):
    length, channels = key_ref.shape
    modes = log_ref.shape[0]
    span = length // SUBS
    decay_ref[...] = jnp.exp(-jnp.exp(log_ref[...]))
    zero_ref[...] = jnp.zeros_like(zero_ref)
    for tile, lanes in lane_tiles(channels):
        drive_ref[tile] = key_ref[:, lanes].astype(F32) * value_ref[:, lanes].astype(F32)
        decay = [spread(decay_ref, m, lanes) for m in range(modes)]

        def step(i, carry):
            now, lag = carry
            u = drive_ref[tile, strided(i, span)]
            lag = [decay[m] * (lag[m] + now[m]) for m in range(modes)]
            now = [decay[m] * now[m] + u for m in range(modes)]
            return now, lag

        zero = [zero_ref[...]] * modes
        now, lag = lax.fori_loop(0, span, step, (zero, zero), unroll=16)
        for m in range(modes):
            sub_ref[tile, strided(m, modes)] = now[m]
            sub_ref[tile, strided(SUBS * modes + m, modes)] = lag[m]
        power = jnp.exp(-span * jnp.exp(log_ref[:, lanes]))
        state = jnp.zeros_like(power)
        lagged = jnp.zeros_like(power)
        for j in range(SUBS):
            lagged = power * (lagged + span * state) + sub_ref[tile, pl.ds((SUBS + j) * modes, modes)]
            state = power * state + sub_ref[tile, pl.ds(j * modes, modes)]
        ends_ref[pl.ds(0, modes), lanes] = state
        ends_ref[pl.ds(modes, modes), lanes] = lagged


def forward_full(*refs):
    (query_ref, drive_ref, sub_ref, log_ref, residue_ref, skip_ref, *end_refs) = refs[:-6]
    (gated_ref, turned_ref, pre_ref, lead_ref, decay_ref, gain_ref) = refs[-6:]
    length, channels = query_ref.shape
    modes = log_ref.shape[0]
    span = length // SUBS
    rate = jnp.exp(log_ref[...])
    decay_ref[...] = jnp.exp(-rate)
    gain_ref[...] = residue_ref[...] * jnp.sqrt(2.0 * rate)
    for tile, lanes in lane_tiles(channels):
        rate = jnp.exp(log_ref[:, lanes])
        stretch = jnp.exp(-length * rate)
        power = jnp.exp(-span * rate)
        state = jnp.zeros_like(rate)
        lagged = jnp.zeros_like(rate)
        for distance in range(2 * RING - 1, 0, -1):
            lagged = stretch * (lagged + length * state) + nearby(end_refs, distance, 1, modes, modes, lanes)
            state = stretch * state + nearby(end_refs, distance, 1, 0, modes, lanes)
        for j in range(SUBS):
            now_rows, lag_rows = (pl.ds((j + k) * modes, modes) for k in (0, SUBS))
            lead_ref[tile, now_rows] = state
            lead_ref[tile, lag_rows] = lagged
            lagged = power * (lagged + span * state) + sub_ref[tile, lag_rows]
            state = power * state + sub_ref[tile, now_rows]
        decay = [spread(decay_ref, m, lanes) for m in range(modes)]
        gain = [spread(gain_ref, m, lanes) for m in range(modes)]
        skip = spread(skip_ref, 0, lanes)

        def step(i, now):
            place = strided(i, span)
            u = drive_ref[tile, place]
            now = [decay[m] * now[m] + u for m in range(modes)]
            pre_ref[tile, place] = tree_sum([gain[m] * now[m] for m in range(modes)]) + skip * u
            return now

        first = [lead_ref[tile, strided(m, modes)] for m in range(modes)]
        lax.fori_loop(0, span, step, first, unroll=16)
        gated_ref[:, lanes] = (query_ref[:, lanes].astype(F32) * pre_ref[tile]).astype(BF16)
    part = length // (RING * 4)
    y, high, core, _, _ = places()
    for i in range(RING * 4):
        on = lax.rem(i // 4 + RING - y, RING)
        there = lax.rem(i % 2 + core, 2) * RING + jnp.where(on == 0, 3, jnp.where(on == 2, 0, (on + 1) // 2))
        there = there * 2 + lax.rem(i // 2 % 2 + high, 2)
        turned_ref[pl.ds(pl.multiple_of(there * part, part), part)] = gated_ref[pl.ds(i * part, part)]


def backward_ends(
    grad_ref, query_ref, pre_ref, drive_ref, lead_ref, log_ref,
    grad_query_ref, back_ref, sums_ref, sub_ref, decay_ref, part_ref, zero_ref,
):
    length, channels = query_ref.shape
    modes = log_ref.shape[0]
    span = length // SUBS
    half = modes // 2
    decay_ref[...] = jnp.exp(-jnp.exp(log_ref[...]))
    zero_ref[...] = jnp.zeros_like(zero_ref)
    for tile, lanes in lane_tiles(channels):
        grad = grad_ref[:, lanes].astype(F32)
        grad_query_ref[:, lanes] = (grad * pre_ref[tile]).astype(BF16)
        back_ref[tile] = grad * query_ref[:, lanes].astype(F32)
        skip = zero_ref[...]
        for low in range(0, modes, half):
            group = range(low, low + half)
            decay = [spread(decay_ref, m, lanes) for m in group]

            def back_step(i, carry):
                start, lag, pair, lag_pair, skip = carry
                place = strided(span - 1 - i, span)
                u = drive_ref[tile, place]
                g = back_ref[tile, place]
                lag = [decay[m] * (lag[m] + start[m]) for m in range(half)]
                start = [decay[m] * start[m] + g for m in range(half)]
                pair = [pair[m] + u * start[m] for m in range(half)]
                lag_pair = [lag_pair[m] + u * lag[m] for m in range(half)]
                return start, lag, pair, lag_pair, (skip + g * u if low == 0 else skip)

            zero = [zero_ref[...]] * half
            start, lag, pair, lag_pair, skip = lax.fori_loop(
                0, span, back_step, (zero, zero, zero, zero, skip), unroll=16
            )
            for m in range(half):
                state = lead_ref[tile, strided(low + m, modes)]
                lagged = lead_ref[tile, strided(SUBS * modes + low + m, modes)]
                once = decay[m] * start[m]
                twice = decay[m] * (lag[m] + start[m])
                sub_ref[tile, strided(low + m, modes)] = start[m]
                part_ref[tile, strided(low + m, modes)] = pair[m] + state * once
                part_ref[tile, strided(SUBS * modes + low + m, modes)] = lag_pair[m] + state * twice + lagged * once
        total = jnp.sum(skip, axis=0, keepdims=True)
        sums_ref[pl.ds(3 * modes, SUBS), lanes] = jnp.broadcast_to(total, (SUBS, LANES))
        power = jnp.exp(-span * jnp.exp(log_ref[:, lanes]))
        start = jnp.zeros_like(power)
        pair = jnp.zeros_like(power)
        lag_pair = jnp.zeros_like(power)
        for j in range(SUBS - 1, -1, -1):
            start = power * start + sub_ref[tile, pl.ds(j * modes, modes)]
            pair = pair + part_ref[tile, pl.ds(j * modes, modes)]
            lag_pair = lag_pair + part_ref[tile, pl.ds((SUBS + j) * modes, modes)]
        sums_ref[pl.ds(0, modes), lanes] = start
        sums_ref[pl.ds(modes, modes), lanes] = pair
        sums_ref[pl.ds(2 * modes, modes), lanes] = lag_pair


def backward_full(*refs, scale):
    (key_ref, value_ref, back_ref, sub_ref, log_ref, residue_ref, skip_ref, *sum_refs) = refs[:-9]
    (grad_key_ref, grad_value_ref, grad_residue_ref, grad_decay_ref, grad_skip_ref) = refs[-9:-4]
    (decay_ref, gain_ref, lead_ref, drive_grad_ref) = refs[-4:]
    length, channels = key_ref.shape
    modes = log_ref.shape[0]
    span = length // SUBS
    rate = jnp.exp(log_ref[...])
    norm = jnp.sqrt(2.0 * rate)
    gain = residue_ref[...] * norm
    decay_ref[...] = jnp.exp(-rate)
    gain_ref[...] = gain
    pair = tree_sum([ref[pl.ds(2 * modes, modes)] for ref in sum_refs])
    lag_pair = tree_sum([ref[pl.ds(3 * modes, modes)] for ref in sum_refs])
    grad_residue_ref[...] = norm * pair * scale
    grad_decay_ref[...] = gain * (0.5 * pair - rate * lag_pair) * scale
    grad_skip_ref[...] = tree_sum([ref[pl.ds(4 * modes, SUBS)] for ref in sum_refs]) * scale
    for tile, lanes in lane_tiles(channels):
        rate = jnp.exp(log_ref[:, lanes])
        stretch = jnp.exp(-length * rate)
        power = jnp.exp(-span * rate)
        start = jnp.zeros_like(rate)
        for distance in range(2 * RING - 1, 0, -1):
            start = stretch * start + nearby(sum_refs, distance, -1, 0, modes, lanes)
        for j in range(SUBS - 1, -1, -1):
            lead_ref[tile, pl.ds(j * modes, modes)] = start
            start = power * start + sub_ref[tile, pl.ds(j * modes, modes)]
        decay = [spread(decay_ref, m, lanes) for m in range(modes)]
        gain = [spread(gain_ref, m, lanes) for m in range(modes)]
        skip = spread(skip_ref, 0, lanes)

        def step(i, now):
            place = strided(span - 1 - i, span)
            g = back_ref[tile, place]
            now = [decay[m] * now[m] + g for m in range(modes)]
            drive_grad_ref[tile, place] = tree_sum([gain[m] * now[m] for m in range(modes)]) + skip * g
            return now

        first = [lead_ref[tile, strided(m, modes)] for m in range(modes)]
        lax.fori_loop(0, span, step, first, unroll=16)
        drive_grad = drive_grad_ref[tile]
        grad_key_ref[:, lanes] = (drive_grad * value_ref[:, lanes].astype(F32)).astype(BF16)
        grad_value_ref[:, lanes] = (drive_grad * key_ref[:, lanes].astype(F32)).astype(BF16)


def call(body, args, outs, scratch, micros, name):
    whole = pl.BlockSpec(memory_space=pltpu.VMEM)
    return pl.pallas_call(
        body,
        out_shape=[jax.ShapeDtypeStruct(o.shape, o.dtype) for o in outs],
        in_specs=[whole] * len(args),
        out_specs=[whole] * len(outs),
        scratch_shapes=[pltpu.VMEM(shape, F32) for shape in scratch],
        compiler_params=pltpu.CompilerParams(vmem_limit_bytes=32 * 2**20),
        cost_estimate=pl.CostEstimate(flops=int(micros * 1.15e9), bytes_accessed=0, transcendentals=0),
        name=name,
    )(*args)


def like(shape, dtype):
    return jax.ShapeDtypeStruct(shape, dtype)


def spread_over_x(value):
    return [value] + [hop(value, x=offset) for offset in range(1, RING)]


def together(*values):
    return lax.optimization_barrier(values)


def local(queries, key_proj, value_proj, skip_gain, residue, log_decay, out_weight, cotangent):
    length, channels = queries.shape
    modes = residue.shape[0]
    blocks = lax.axis_size("seq")
    scale = 1.0 / math.sqrt(length * blocks)
    skip_row = skip_gain.reshape(1, channels)
    tiles = channels // LANES
    wide = like((tiles, length, LANES), F32)
    narrow = like((length, channels), BF16)
    table = (modes, channels)

    block, log_first = together(gather_z(cotangent), log_decay)
    before_own, after_other = hop(block[0], y=1), hop(block[1], y=-1)
    ends, subs, driving = call(
        forward_ends,
        (key_proj, value_proj, log_first),
        (like((2 * modes, channels), F32), like((tiles, 2 * SUBS * modes, LANES), F32), wide),
        [table, (SUBS, LANES)],
        0.1,
        "forward_ends",
    )
    ends_pair = jnp.concatenate([ends, hop(ends, pair=1)])
    before_own, after_other, ends_pair = together(before_own, after_other, ends_pair)
    before_other, after_own = hop(block[1], y=1), hop(block[0], y=-1)
    earlier = spread_over_x(ends_pair)
    gated, turned, pre_gate, lead = call(
        forward_full,
        (queries, driving, subs, log_decay, residue, skip_row, *earlier),
        (narrow, narrow, wide, like((tiles, 2 * SUBS * modes, LANES), F32)),
        [table, table],
        0.1,
        "forward_full",
    )
    before_own, after_other, turned = together(before_own, after_other, turned)
    far_own, far_other = hop(before_own, y=1), hop(after_other, y=-1)
    before_other, after_own, turned = together(before_other, after_own, turned)
    near_first, near_rest, far_first, far_rest = project(turned, out_weight)
    got_first, got_rest = hop(far_first, core=1), hop(far_rest, core=1)
    gated_pair = jnp.concatenate([gated, hop(gated, pair=1)])
    opposite = add(near_first, got_first).astype(BF16)
    far_own, far_other, opposite = together(far_own, far_other, opposite)
    cot_rows = place_blocks(
        (block[0], before_own, after_own, far_own), (block[1], before_other, after_other, far_other)
    )
    cot_rows = cot_rows.reshape(2 * length, -1)

    half = out_weight.shape[1] // 2
    low_weight = lax.dynamic_slice(out_weight, (0, places()[3] * half), (channels, half))
    weights = {2: weigh(gated_pair, cot_rows, scale, 2)}
    cot_rows, weights[2] = together(cot_rows, weights[2])
    grad_parts = lax.dot_general(cot_rows, low_weight, (((1,), (1,)), ((), ())), preferred_element_type=F32)
    cot_rows, grad_parts, got_rest = together(cot_rows, grad_parts, got_rest)
    theirs = hop(grad_parts[length:].astype(BF16), pair=1)
    part = opposite.shape[0] // 2
    low_sum, high_sum = hop(opposite[:part], y=1), hop(opposite[part:], y=-1)
    above, below, own = (
        add(near_rest[i * 2 * part : (i + 1) * 2 * part], got_rest[i * 2 * part : (i + 1) * 2 * part]) for i in range(3)
    )
    above = jnp.concatenate([add(above[:part], low_sum), above[part:]]).astype(BF16)
    below = jnp.concatenate([below[:part], add(below[part:], high_sum)]).astype(BF16)
    for r in (1, 3, 0):
        weights[r] = weigh(gated_pair, cot_rows, scale, r)
    cut = channels // 2
    upper, lower = hop(weights[2][:cut], x=1), hop(weights[2][cut:], x=-1)
    up_sum = add(weights[1][:cut], upper).astype(BF16)
    down_sum = add(weights[3][cut:], lower).astype(BF16)
    up_rest, down_rest = weights[1][cut:], weights[3][:cut]
    theirs, up_sum, down_sum, up_rest, down_rest = together(theirs, up_sum, down_sum, up_rest, down_rest)
    up_rest, down_rest = hop(up_rest, x=1), hop(down_rest, x=-1)
    grad_gated = add(grad_parts[:length], theirs)
    own = add(own, hop(above, y=1), hop(below, y=-1))
    leaving = own[part:].astype(BF16)
    width = leaving.shape[1] // 2
    halfway = hop(leaving[:, width:], z=-1)
    crossed = hop(leaving[:, :width], z=2)

    grad_query, back, sums, back_subs = call(
        backward_ends,
        (grad_gated, queries, pre_gate, driving, lead, log_decay),
        (narrow, wide, like((3 * modes + SUBS, channels), F32), like((tiles, SUBS * modes, LANES), F32)),
        [table, (tiles, 2 * SUBS * modes, LANES), (SUBS, LANES)],
        2.0,
        "backward_ends",
    )
    sums, up_rest, down_rest = together(sums, up_rest, down_rest)
    up_sum, down_sum = hop(up_sum, x=1), hop(down_sum, x=-1)
    others = hop(sums, pair=1)
    sums_pair = jnp.concatenate([sums[:modes], others[:modes], sums[modes:] + others[modes:]])
    crossed = jnp.concatenate([crossed, hop(halfway, z=-1)], axis=1)
    mixed = add(own[:part], crossed).astype(BF16)
    all_sums = spread_over_x(sums_pair)
    all_sums[0], up_sum, down_sum = together(all_sums[0], up_sum, down_sum)
    grad_weight = jnp.concatenate(
        [add(weights[0][:cut], up_sum, down_rest), add(weights[0][cut:], up_rest, down_sum)]
    ).astype(BF16)
    grad_key, grad_value, grad_residue, grad_decay, grad_skip = call(
        functools.partial(backward_full, scale=scale),
        (key_proj, value_proj, back, back_subs, log_decay, residue, skip_row, *all_sums),
        (narrow, narrow, like(table, F32), like(table, F32), like((SUBS, channels), F32)),
        [table, table, (tiles, SUBS * modes, LANES), (tiles, length, LANES)],
        0.1,
        "backward_full",
    )
    return (
        mixed,
        grad_query,
        grad_key,
        grad_value,
        grad_weight,
        grad_residue,
        grad_decay,
        grad_skip[0],
    )


def solution(mesh):
    in_specs = (
        P("seq", "chan"),
        P("seq", "chan"),
        P("seq", "chan"),
        P("chan"),
        P(None, "chan"),
        P(None, "chan"),
        P("chan", None),
        P(("seq", "chan"), None),
    )
    out_specs = (
        P(("seq", "chan"), None),
        P("seq", "chan"),
        P("seq", "chan"),
        P("seq", "chan"),
        P("chan", "seq"),
        P(None, "chan"),
        P(None, "chan"),
        P("chan"),
    )
    return jax.shard_map(local, mesh=mesh, in_specs=in_specs, out_specs=out_specs, check_vma=False)
```
